256 devices in a mesh: member: 2 (over y_lo), lat: 8 (over z), lon: 16 (over y_hi, x, core).
Axes of the slice: x: 4, y: 4 (y_hi: 2, y_lo: 2; y = y_hi * 2 + y_lo), z: 8, core: 2. Of those that a mesh axis runs over, the one named last changes fastest.
Arguments:
- fields: bfloat16 [2, 2, 48, 192, 768], P('member', None, 'lat', 'lon'), may hold values from -6 to 6
- cotangent: bfloat16 [2, 2, 48, 192, 768], P('member', None, 'lat', 'lon'), may hold values from -6 to 6
- qkv_weight: bfloat16 [2, 768, 2304], replicated, may hold values from -0.21875 to 0.21875
- out_weight: bfloat16 [2, 768, 768], replicated, may hold values from -0.21875 to 0.21875
- norm_gain: float32 [2, 768], replicated, may hold values from 0.25 to 1.75
- bias_table: float32 [2, 8, 759, 24], P(None, 'lat'), may hold values from -4 to 253
- bias_index: int32 [144, 144], replicated, may hold values from 0 to 758
- region: int32 [2, 48, 192], P(None, 'lat', 'lon'), may hold values from 0 to 1
Outputs:
- output: bfloat16 [2, 2, 48, 192, 768], P('member', None, 'lat', 'lon')
- grad_fields: bfloat16 [2, 2, 48, 192, 768], P('member', None, 'lat', 'lon')
- grad_out: float32 [2, 768, 768], P(None, 'lat', 'lon')
The draws below stay inside these ranges and needn't reach their ends.
All inputs are finite; a program needn't handle non-finite values.
Results may differ from the reference program's by a relative error of at most 0.03.
Values may be sent and summed in bfloat16 or wider, within the bound.
No kernel may reach another device: no remote copies, remote signals or barrier semaphores. Data moves between devices by JAX's collectives and lax.ppermute only.
A program may use at most 128 MiB of HBM per device.

```python
import jax
import jax.numpy as jnp
from jax import lax

D = 768
HEADS = 24
LEVELS = 2
WIN_LAT = 6
WIN_LON = 12
WIN = 144
NREL = 759
LAT_TILES = 8
NLAT = 48
NLON = 192
MEMBERS = 2
TOKENS = 36864


def draw_bias_table(key, part):
    key = jax.random.fold_in(key, 5)
    key_base = jax.random.fold_in(key, 0)
    table_shape = (2, LAT_TILES, NREL, HEADS)
    values_out = jnp.clip(jax.random.normal(key_base, table_shape, jnp.float32), -4.0, 4.0)
    return values_out


def touch_ends(values, key, least, top_value):
    longest = values.shape.index(max(values.shape))
    spots = []
    for shift in (0, 1):
        where = [jax.random.randint(jax.random.fold_in(key, axis), (), 0, length) for axis, length in enumerate(values.shape)]
        where[longest] = (where[longest] + shift) % values.shape[longest]
        spots.append(tuple(where))
    return values.at[spots[0]].set(least).at[spots[1]].set(top_value)


def spiked(values, key, source, target, shards_of, factor):
    def block_of(dim):
        return (jnp.arange(values.shape[dim]) // (values.shape[dim] // shards_of)).reshape((-1,) + (1,) * (values.ndim - 1 - dim))

    first = jax.random.permutation(key, shards_of)[block_of(target)]
    far = (block_of(target) + shards_of // 2) % shards_of
    return jnp.where((block_of(source) == first) | (block_of(source) == far), factor * values, values)


def shard_levels(key, dims, cuts, least, high):
    def one(dim, shards_of):
        steps = jax.random.uniform(jax.random.fold_in(jax.random.fold_in(key, 6), dim), (shards_of,), jnp.float32, least / len(cuts), high / len(cuts))
        return jnp.repeat(jnp.exp(steps), dims[dim] // shards_of).reshape((-1,) + (1,) * (len(dims) - dim - 1))

    factor_of = one(*cuts[0])
    for cut in cuts[1:]:
        factor_of = factor_of * one(*cut)
    return factor_of


def bell_draw(stream_key, extent, deviation, reach, cuts=(), kind=jnp.bfloat16):
    entries = jax.random.normal(stream_key, extent, jnp.float32) * deviation
    if len(cuts) > 0:
        entries = shard_levels(stream_key, extent, cuts, -0.22, 0.18) * entries
    return jnp.clip(entries, min=-reach, max=reach).astype(kind)


def gaussian_with(stream_key, shape, width, most, cuts, heavy, held_as=jnp.bfloat16):
    values = width * jax.random.normal(stream_key, shape, jnp.float32)
    if cuts:
        values = values * shard_levels(stream_key, shape, cuts, -0.22, 0.18)
    return jnp.clip(spiked(values, jax.random.fold_in(stream_key, 3), *heavy), -most, most).astype(held_as)


def setup_inputs(seed: int = 0) -> dict:
    streams_of = jax.random.split(jax.random.key(seed), 9)
    fields = bell_draw(streams_of[0], (MEMBERS, LEVELS, NLAT, NLON, D), 1.0, 6.0, ((0, 2), (2, 8), (3, 16)))
    cotangent = gaussian_with(streams_of[1], (MEMBERS, LEVELS, NLAT, NLON, D), 1.0, 6.0, ((0, 2), (2, 8), (3, 16)), (3, 4, 16, 2.0))
    qkv_weight = bell_draw(streams_of[2], (2, D, 3 * D), D ** -0.5, 0.21875)
    out_weight = bell_draw(streams_of[3], (2, D, D), D ** -0.5, 0.21875)
    norm_gain = jnp.clip(1.0 + 0.15 * jax.random.normal(streams_of[4], (2, D), jnp.float32), 0.25, 1.75)
    bias_table = draw_bias_table(jax.random.fold_in(streams_of[8], 71), 0)
    bias_index = touch_ends(jax.random.randint(streams_of[6], (WIN, WIN), 0, NREL), jax.random.fold_in(streams_of[6], 1), 0, NREL - 1).astype(jnp.int32)
    region = touch_ends(jax.random.randint(streams_of[7], (LEVELS, NLAT, NLON), 0, 2), jax.random.fold_in(streams_of[7], 1), 0, 1).astype(jnp.int32)
    return dict(fields=fields, cotangent=cotangent, qkv_weight=qkv_weight, out_weight=out_weight, norm_gain=norm_gain, bias_table=bias_table, bias_index=bias_index, region=region)


EPS = 1e-05

def normalize(values_f, gain):
    centre = lax.optimization_barrier(jnp.mean(values_f, axis=-1, keepdims=True))
    centred = values_f - centre
    variance = lax.optimization_barrier(jnp.mean(centred * centred, axis=-1, keepdims=True))
    inv_std = lax.rsqrt(variance + EPS)
    normed = centred * inv_std
    return (normed, inv_std, (normed * gain).astype(jnp.bfloat16))

def batched(form, left, right):
    return jnp.einsum(form, left.astype(jnp.float32), right.astype(jnp.float32))

def window_forward(windows, gain, w_qkv, w_out, bias, allowed):
    n_windows, win_tokens, features = windows.shape
    n_heads = bias.shape[0]
    head_dim = features // n_heads
    values_f = windows.astype(jnp.float32)
    normed, inv_std, hidden = normalize(values_f, gain)
    flat_hidden = hidden.reshape(n_windows * win_tokens, features)
    qkv = jnp.dot(flat_hidden, w_qkv, preferred_element_type=jnp.float32).astype(jnp.bfloat16)
    qkv = qkv.reshape(n_windows, win_tokens, 3, n_heads, head_dim)
    query, key_part, value_part = (qkv[:, :, 0], qkv[:, :, 1], qkv[:, :, 2])
    scores = batched('bihd,bjhd->bhij', query, key_part) * head_dim ** (-0.5) + bias[None]
    if allowed is not None:
        scores = jnp.where(allowed[:, None], scores, -jnp.inf)
    row_max = lax.optimization_barrier(jnp.max(scores, axis=-1, keepdims=True))
    exponent = jnp.exp(scores - row_max)
    probability = exponent / lax.optimization_barrier(jnp.sum(exponent, axis=-1, keepdims=True))
    weights = probability.astype(jnp.bfloat16)
    mixed = batched('bhij,bjhd->bihd', weights, value_part).astype(jnp.bfloat16)
    mixed = mixed.reshape(n_windows * win_tokens, features)
    projected = jnp.dot(mixed, w_out, preferred_element_type=jnp.float32)
    result = (values_f.reshape(n_windows * win_tokens, features) + projected).astype(jnp.bfloat16)
    stored = (normed, inv_std, query, key_part, value_part, probability, weights, mixed)
    return (result.reshape(n_windows, win_tokens, features), stored)

def window_backward(grad_result, stored, gain, w_qkv, w_out):
    normed, inv_std, query, key_part, value_part, probability, weights, mixed = stored
    n_windows, win_tokens, features = grad_result.shape
    n_heads, head_dim = (query.shape[2], query.shape[3])
    grad_flat = grad_result.reshape(n_windows * win_tokens, features)
    grad_wout = lax.dot_general(mixed, grad_flat, (((0,), (0,)), ((), ())), preferred_element_type=jnp.float32)
    grad_mixed = lax.dot_general(grad_flat, w_out, (((1,), (1,)), ((), ())), preferred_element_type=jnp.float32)
    grad_mixed = grad_mixed.astype(jnp.bfloat16).reshape(n_windows, win_tokens, n_heads, head_dim)
    grad_weights = batched('bihd,bjhd->bhij', grad_mixed, value_part)
    grad_value = batched('bhij,bihd->bjhd', weights, grad_mixed).astype(jnp.bfloat16)
    row_inner = lax.optimization_barrier(jnp.sum(grad_weights * probability, axis=-1, keepdims=True))
    grad_scores = (probability * (grad_weights - row_inner) * head_dim ** (-0.5)).astype(jnp.bfloat16)
    grad_query = batched('bhij,bjhd->bihd', grad_scores, key_part).astype(jnp.bfloat16)
    grad_key = batched('bhij,bihd->bjhd', grad_scores, query).astype(jnp.bfloat16)
    grad_rows = jnp.stack([grad_query, grad_key, grad_value], axis=2).reshape(n_windows * win_tokens, 3 * features)
    grad_hidden = lax.dot_general(grad_rows, w_qkv, (((1,), (1,)), ((), ())), preferred_element_type=jnp.float32)
    grad_normed = grad_hidden.reshape(n_windows, win_tokens, features) * gain
    mean_one = lax.optimization_barrier(jnp.mean(grad_normed, axis=-1, keepdims=True))
    mean_two = lax.optimization_barrier(jnp.mean(grad_normed * normed, axis=-1, keepdims=True))
    grad_x = inv_std * (grad_normed - mean_one - normed * mean_two)
    grad_input = (grad_result.astype(jnp.float32) + grad_x).astype(jnp.bfloat16)
    return (grad_input, grad_wout)

def window_rows(grid_cells, lat_index):
    band_cells = lax.dynamic_slice_in_dim(grid_cells, lat_index * WIN_LAT, WIN_LAT, axis=2)
    members, levels, n_rows, n_cols, features = band_cells.shape
    band_cells = band_cells.reshape(members, levels, n_rows, n_cols // WIN_LON, WIN_LON, features)
    band_cells = band_cells.transpose(0, 3, 1, 2, 4, 5)
    return band_cells.reshape(members * (n_cols // WIN_LON), levels * n_rows * WIN_LON, features)

def band_back(windows, members, n_cols):
    features = windows.shape[2]
    cells = windows.reshape(members, n_cols // WIN_LON, LEVELS, WIN_LAT, WIN_LON, features)
    return cells.transpose(0, 2, 3, 1, 4, 5).reshape(members, LEVELS, WIN_LAT, n_cols, features)

def band_mask(region, lat_index):
    band_cells = lax.dynamic_slice_in_dim(region, lat_index * WIN_LAT, WIN_LAT, axis=1)
    levels, n_rows, n_cols = band_cells.shape
    labels = band_cells.reshape(levels, n_rows, n_cols // WIN_LON, WIN_LON).transpose(2, 0, 1, 3)
    labels = labels.reshape(n_cols // WIN_LON, levels * n_rows * WIN_LON)
    same_label = labels[:, :, None] == labels[:, None, :]
    position = jnp.arange(levels * n_rows * WIN_LON, dtype=jnp.int32)
    upper_half = position // WIN_LON % n_rows >= n_rows // 2
    across = upper_half[:, None] != upper_half[None, :]
    on_edge = jnp.logical_and(across, lat_index == LAT_TILES - 1)
    allowed = jnp.logical_and(same_label, jnp.logical_not(on_edge)[None])
    return jnp.tile(allowed, (MEMBERS, 1, 1))

def band_pass(grid_cells, grad_cells, bias_rows, gain, w_qkv, w_out, bias_index, region, masked):
    members, n_cols = (grid_cells.shape[0], grid_cells.shape[3])

    def band_step(lat_index):
        windows = window_rows(grid_cells, lat_index)
        bias = jnp.take(bias_rows[lat_index], bias_index, axis=0).transpose(2, 0, 1)
        allowed = band_mask(region, lat_index) if masked else None
        result, stored = window_forward(windows, gain, w_qkv, w_out, bias, allowed)
        if grad_cells is None:
            return band_back(result, members, n_cols)
        grad_input, grad_wout = window_backward(window_rows(grad_cells, lat_index), stored, gain, w_qkv, w_out)
        return (band_back(grad_input, members, n_cols), grad_wout)
    return lax.map(band_step, jnp.arange(LAT_TILES, dtype=jnp.int32))

def reference(fields, cotangent, qkv_weight, out_weight, norm_gain, bias_table, bias_index, region):
    half_lat, half_lon = (WIN_LAT // 2, WIN_LON // 2)

    def assemble(band_list):
        return band_list.transpose(1, 2, 0, 3, 4, 5).reshape(fields.shape)
    block_one = assemble(band_pass(fields, None, bias_table[0], norm_gain[0], qkv_weight[0], out_weight[0], bias_index, region, False))
    shifted = jnp.roll(block_one, (-half_lat, -half_lon), axis=(2, 3))
    block_two = assemble(band_pass(shifted, None, bias_table[1], norm_gain[1], qkv_weight[1], out_weight[1], bias_index, region, True))
    output = jnp.roll(block_two, (half_lat, half_lon), axis=(2, 3))
    grad_two = jnp.roll(cotangent, (-half_lat, -half_lon), axis=(2, 3))
    band_list, out_two = band_pass(shifted, grad_two, bias_table[1], norm_gain[1], qkv_weight[1], out_weight[1], bias_index, region, True)
    grad_mid = jnp.roll(assemble(band_list), (half_lat, half_lon), axis=(2, 3))
    band_list, out_one = band_pass(fields, grad_mid, bias_table[0], norm_gain[0], qkv_weight[0], out_weight[0], bias_index, region, False)
    grad_fields = assemble(band_list)
    grad_scale = float(TOKENS) ** (-0.5)
    grad_out = jnp.stack([lax.optimization_barrier(jnp.sum(out_one, axis=0)), lax.optimization_barrier(jnp.sum(out_two, axis=0))]) * grad_scale
    return (output, grad_fields, grad_out)
```

```python
import functools

import jax
import jax.numpy as jnp
import numpy as np
from jax import lax
from jax.experimental import pallas as pl
from jax.experimental.pallas import tpu as pltpu
from jax.sharding import PartitionSpec as P

LEVELS = 2
WIN_LAT = 6
WIN_LON = 12
HALF_LAT = WIN_LAT // 2
HALF_LON = WIN_LON // 2
WIN = LEVELS * WIN_LAT * WIN_LON
QUAD = WIN // 4
D = 768
HEADS = 24
HEAD_DIM = D // HEADS
GROUP = 128 // HEAD_DIM
GROUPS = HEADS // GROUP
NREL = 759
CHUNKS = 6
SCALE = HEAD_DIM ** (-0.5)
EPS = 1e-05

bf16 = jnp.bfloat16
f32 = jnp.float32


def quad_order():
    token = np.arange(WIN)
    quad, inside = token // QUAD, token % QUAD
    level = inside // (HALF_LAT * HALF_LON)
    row = inside // HALF_LON % HALF_LAT + HALF_LAT * (quad // 2)
    col = inside % HALF_LON + HALF_LON * (quad % 2)
    line = level * WIN_LAT + row
    return line, col, line * WIN_LON + col


def constants():
    line, col, natural = quad_order()
    order = np.eye(WIN, dtype=np.float32)[natural]
    at_line = np.eye(LEVELS * WIN_LAT, dtype=np.float32)[line]
    at_col = np.eye(WIN_LON, dtype=np.float32)[col]
    return order, at_line, at_col


def contract(left, right, dims):
    return lax.dot_general(left, right, ((dims[:1], dims[1:]), ((), ())), preferred_element_type=f32)


def mm(left, right):
    return contract(left, right, (1, 0))


def mm_t(left, right):
    return contract(left, right, (1, 1))


def eye(size):
    rows = lax.broadcasted_iota(jnp.int32, (size, size), 0)
    cols = lax.broadcasted_iota(jnp.int32, (size, size), 1)
    return (rows == cols).astype(f32).astype(bf16)


def head_masks():
    lane = lax.broadcasted_iota(jnp.int32, (1, 128), 1)
    masks = []
    for head in range(GROUP):
        inside = jnp.logical_and(lane >= head * HEAD_DIM, lane < (head + 1) * HEAD_DIM)
        masks.append(inside.astype(f32).astype(bf16))
    return masks


def layer_norm(values_f):
    centred = values_f - jnp.mean(values_f, axis=-1, keepdims=True)
    variance = jnp.mean(centred * centred, axis=-1, keepdims=True)
    inv_std = lax.rsqrt(variance + EPS)
    return centred * inv_std, inv_std


def gather_bias(index_ref, order, table_ref, bias_ref, wide_ref, rows_ref, allowed):
    index_f = index_ref[...].astype(f32)
    high = jnp.floor(index_f * 0.125)
    low = index_f - high * 8.0
    parts = []
    for part in (high, low):
        half = mm(order, part.astype(bf16)).astype(bf16)
        parts.append(mm_t(half, order))
    moved = parts[0] * 8.0 + parts[1]
    wide_ref[:, :WIN] = (moved + 0.5).astype(jnp.int32)
    wide_ref[:, WIN:] = jnp.zeros((WIN, 256 - WIN), jnp.int32)
    rows_ref[...] = jnp.zeros_like(rows_ref)
    turned = table_ref[...].T
    for head in range(HEADS):
        rows_ref[head, :, :NREL] = turned[head : head + 1, :]
    depth = 24
    strips = WIN // depth
    tail = WIN - 128
    lane = lax.broadcasted_iota(jnp.int32, (depth, 128), 1)
    packed = jnp.zeros((depth, 128), jnp.int32)
    for strip in range(strips):
        piece = wide_ref[strip * depth : (strip + 1) * depth, 128:256]
        if strip:
            piece = pltpu.roll(piece, strip * tail, axis=1)
        inside = jnp.logical_and(lane >= strip * tail, lane < (strip + 1) * tail)
        packed = jnp.where(inside, piece, packed)
    wide_ref[:depth, 128:256] = packed

    def look_up(index, head):
        low_part = jnp.bitwise_and(index, 127)
        high_part = jnp.right_shift(index, 7)
        found = jnp.zeros(index.shape, f32)
        for chunk in range(CHUNKS):
            row = rows_ref[head, :, chunk * 128 : (chunk + 1) * 128]
            row = jnp.broadcast_to(row, index.shape)
            taken = jnp.take_along_axis(row, low_part, axis=1, mode="promise_in_bounds")
            found = jnp.where(high_part == chunk, taken, found)
        return found

    def one_head(head, carry):
        for strip in range(3):
            rows = slice(strip * 48, (strip + 1) * 48)
            bias_ref[head, rows, :128] = look_up(wide_ref[rows, :128], head)
        rest = look_up(wide_ref[:depth, 128:256], head)
        for strip in range(strips):
            piece = rest if strip == 0 else pltpu.roll(rest, 128 - strip * tail, axis=1)
            bias_ref[head, strip * depth : (strip + 1) * depth, 128:WIN] = piece[:, :tail]
        if allowed is not None:
            bias_ref[head] = jnp.where(allowed, bias_ref[head], -jnp.inf)
        return carry

    lax.fori_loop(0, HEADS, one_head, 0)


def project_qkv(hidden, w_qkv_ref, qkv_ref):
    for part in range(3):
        cols = slice(part * D, (part + 1) * D)
        qkv_ref[:, cols] = mm(hidden, w_qkv_ref[:, cols]).astype(bf16)


def attend(qkv_ref, bias_ref, probs_ref, mixed_ref):
    masks = head_masks()
    for group in range(GROUPS):
        query = qkv_ref[:, group * 128 : (group + 1) * 128]
        key = qkv_ref[:, D + group * 128 : D + (group + 1) * 128]
        value = qkv_ref[:, 2 * D + group * 128 : 2 * D + (group + 1) * 128]
        total = jnp.zeros((WIN, 128), f32)
        for inner in range(GROUP):
            head = group * GROUP + inner
            scores = mm_t(query * masks[inner], key) * SCALE + bias_ref[head]
            exponent = jnp.exp(scores - jnp.max(scores, axis=-1, keepdims=True))
            share = 1.0 / jnp.sum(exponent, axis=-1, keepdims=True)
            weights = (exponent * share).astype(bf16)
            probs_ref[head] = weights
            total += mm(weights, value * masks[inner])
        mixed_ref[:, group * 128 : (group + 1) * 128] = total.astype(bf16)


def back_attend(grad, qkv_ref, probs_ref, w_out_ref, grad_mixed_ref, turned_ref, rows_ref):
    masks = head_masks()
    unit = eye(256)
    small = eye(WIN)
    grad_mixed_ref[...] = mm_t(grad, w_out_ref[...]).astype(bf16)
    for part in range(3):
        cols = slice(part * 256, (part + 1) * 256)
        turned_ref[0, cols, :] = mm_t(unit, grad_mixed_ref[:, cols]).astype(bf16)
        turned_ref[1, cols, :] = mm_t(unit, qkv_ref[:, cols]).astype(bf16)
    for group in range(GROUPS):
        cols = slice(group * 128, (group + 1) * 128)
        grad_mixed = grad_mixed_ref[:, cols]
        key = qkv_ref[:, D + group * 128 : D + (group + 1) * 128]
        value = qkv_ref[:, 2 * D + group * 128 : 2 * D + (group + 1) * 128]
        grad_query = jnp.zeros((WIN, 128), f32)
        for inner in range(GROUP):
            head = group * GROUP + inner
            lines = slice(head * HEAD_DIM, (head + 1) * HEAD_DIM)
            grad_weights = mm_t(grad_mixed * masks[inner], value)
            weights = probs_ref[head]
            probs = weights.astype(f32)
            row_inner = jnp.sum(grad_weights * probs, axis=-1, keepdims=True)
            grad_scores = (probs * (grad_weights - row_inner) * SCALE).astype(bf16)
            grad_query += mm(grad_scores, key * masks[inner])
            turned_ref[2, lines, :] = mm(turned_ref[1, lines, :], grad_scores).astype(bf16)
            turned_ref[3, lines, :] = mm(turned_ref[0, lines, :], weights).astype(bf16)
        rows_ref[:, cols] = grad_query.astype(bf16)
    for part in range(3):
        cols = slice(part * 256, (part + 1) * 256)
        for which in (1, 2):
            out = slice(which * D + part * 256, which * D + (part + 1) * 256)
            rows_ref[:, out] = mm_t(small, turned_ref[1 + which, cols, :]).astype(bf16)


def back_norm(grad_f, normed, inv_std, gain, rows_ref, w_qkv_ref):
    grad_normed = mm_t(rows_ref[...], w_qkv_ref[...]) * gain
    mean_one = jnp.mean(grad_normed, axis=-1, keepdims=True)
    mean_two = jnp.mean(grad_normed * normed, axis=-1, keepdims=True)
    return grad_f + inv_std * (grad_normed - mean_one - normed * mean_two)


def split_quads(values_f, hold_ref, quad_refs):
    hold_ref[...] = values_f
    for quad in range(4):
        quad_refs[quad][...] = hold_ref[quad * QUAD : (quad + 1) * QUAD, :].astype(bf16)


def join_quads(quad_refs, hold_ref):
    for quad in range(4):
        hold_ref[quad * QUAD : (quad + 1) * QUAD, :] = quad_refs[quad][...].astype(f32)
    return hold_ref[...]


def read_tile(tile_ref, order, hold_ref):
    for line in range(LEVELS * WIN_LAT):
        piece = tile_ref[0, line // WIN_LAT, line % WIN_LAT].astype(f32)
        hold_ref[line * WIN_LON : (line + 1) * WIN_LON, :] = piece
    return mm(order, hold_ref[...].astype(bf16))


def write_tile(values, back_order, hold_ref, tile_ref):
    hold_ref[...] = mm(back_order, values)
    for line in range(LEVELS * WIN_LAT):
        piece = hold_ref[line * WIN_LON : (line + 1) * WIN_LON, :]
        tile_ref[0, line // WIN_LAT, line % WIN_LAT] = piece.astype(bf16)


def start_weights(w_qkv_hbm, w_out_hbm, block, w_qkv_ref, w_out_ref, sems):
    copies = (
        pltpu.make_async_copy(w_qkv_hbm.at[block], w_qkv_ref, sems.at[0]),
        pltpu.make_async_copy(w_out_hbm.at[block], w_out_ref, sems.at[1]),
    )
    for copy in copies:
        copy.start()
    return copies


def first_forward(
    fields_ref, cotangent_ref, gain_ref, table_ref, index_ref, order_ref, w_qkv_hbm, w_out_hbm,
    b0, b1, b2, b3, g0, g1, g2, g3, m0, m1, m2, m3, input_ref, qkv_ref, probs_ref,
    w_qkv_ref, w_out_ref, sems, bias_ref, wide_ref, rows_ref, hold_ref, mixed_ref,
):
    copy_qkv, copy_out = start_weights(w_qkv_hbm, w_out_hbm, 0, w_qkv_ref, w_out_ref, sems)
    order = order_ref[...]
    split_quads(read_tile(cotangent_ref, order, hold_ref), hold_ref, (g0, g1, g2, g3))
    gather_bias(index_ref, order, table_ref.at[0, 0], bias_ref, wide_ref, rows_ref, None)
    values_f = read_tile(fields_ref, order, hold_ref)
    input_ref[...] = values_f.astype(bf16)
    normed, _ = layer_norm(values_f)
    hidden = (normed * gain_ref[0:1, :]).astype(bf16)
    copy_qkv.wait()
    project_qkv(hidden, w_qkv_ref, qkv_ref)
    attend(qkv_ref, bias_ref, probs_ref, mixed_ref)
    copy_out.wait()
    mixed = mixed_ref[...]
    result = input_ref[...].astype(f32) + mm(mixed, w_out_ref[...])
    split_quads(result, hold_ref, (b0, b1, b2, b3))
    split_quads(mixed.astype(f32), hold_ref, (m0, m1, m2, m3))


def second_bias(
    table_ref, index_ref, order_ref, region_ref, line_ref, col_ref, edge_ref,
    bias_ref, wide_ref, rows_ref,
):
    labels = jnp.concatenate([region_ref[0], region_ref[1]], axis=0).astype(f32) * 2.0 - 1.0
    at_line, at_col = line_ref[...], col_ref[...]
    column = jnp.sum(mm(at_line, labels.astype(bf16)) * at_col.astype(f32), axis=1, keepdims=True)
    signs = jnp.broadcast_to(column, (WIN, 128)).astype(bf16)
    same = mm_t(signs, signs) > 0.0
    half = WIN // 2
    rows = lax.broadcasted_iota(jnp.int32, (WIN, WIN), 0) >= half
    cols = lax.broadcasted_iota(jnp.int32, (WIN, WIN), 1) >= half
    across = jnp.logical_and(jnp.logical_xor(rows, cols), edge_ref[0] != 0)
    allowed = jnp.logical_and(same, jnp.logical_not(across))
    gather_bias(
        index_ref, order_ref[...], table_ref.at[1, 0], bias_ref, wide_ref, rows_ref, allowed
    )


def weight_terms(grad, mixed_ref, block, terms_ref):
    rows = terms_ref.shape[1] // 2
    unit = eye(256)
    mixed = mixed_ref[...]
    per_step = 256 // rows
    for start in range(0, D, per_step * rows):
        size = min(per_step * rows, D - start)
        turned = mm_t(unit[:size, :size], grad[:, start : start + size]).astype(bf16)
        product = mm(turned, mixed).astype(bf16)
        for part in range(size // rows):
            place = start // rows + part
            piece = product[part * rows : (part + 1) * rows, :]
            terms_ref[place, block * rows : (block + 1) * rows, :] = piece


def sum_lon(parts_ref, out_ref):
    total = parts_ref[0].astype(f32)
    for part in range(1, parts_ref.shape[0]):
        total += parts_ref[part].astype(f32)
    copies, width = 2, D * 2 // out_ref.shape[0]
    for place in range(out_ref.shape[0] // copies):
        piece = total[:, place * width : (place + 1) * width].astype(bf16)
        for copy in range(copies):
            out_ref[copy * (out_ref.shape[0] // copies) + place, :, :width] = piece


def sum_lat(scale, parts_ref, out_ref):
    total = parts_ref[0].astype(f32)
    for part in range(1, parts_ref.shape[0]):
        total += parts_ref[part].astype(f32)
    _, rows, cols = out_ref.shape
    total = total * scale
    turned = total.T
    for block in range(2):
        out_ref[block] = turned[:rows, block * cols : (block + 1) * cols]


def second_block(
    b0, b1, b2, b3, g0, g1, g2, g3, m0, m1, m2, m3, gain_ref, bias_ref, w_qkv_hbm, w_out_hbm,
    r0, r1, r2, r3, e0, e1, e2, e3, terms_ref,
    w_qkv_ref, w_out_ref, sems, hold_ref, mixed_ref, qkv_ref, probs_ref,
    grad_mixed_ref, turned_ref, grad_rows_ref,
):
    copy_qkv, copy_out = start_weights(w_qkv_hbm, w_out_hbm, 1, w_qkv_ref, w_out_ref, sems)
    gain = gain_ref[1:2, :]
    values_f = join_quads((b0, b1, b2, b3), hold_ref)
    normed, inv_std = layer_norm(values_f)
    hidden = (normed * gain).astype(bf16)
    copy_qkv.wait()
    project_qkv(hidden, w_qkv_ref, qkv_ref)
    attend(qkv_ref, bias_ref, probs_ref, mixed_ref)
    copy_out.wait()
    result = values_f + mm(mixed_ref[...], w_out_ref[...])
    split_quads(result, hold_ref, (r0, r1, r2, r3))
    grad_f = join_quads((g0, g1, g2, g3), hold_ref)
    grad = grad_f.astype(bf16)
    weight_terms(grad, mixed_ref, 1, terms_ref)
    back_attend(grad, qkv_ref, probs_ref, w_out_ref, grad_mixed_ref, turned_ref, grad_rows_ref)
    grad_input = back_norm(grad_f, normed, inv_std, gain, grad_rows_ref, w_qkv_ref)
    split_quads(grad_input, hold_ref, (e0, e1, e2, e3))
    first_grad = grad_input.astype(bf16)
    mixed_ref[...] = join_quads((m0, m1, m2, m3), hold_ref).astype(bf16)
    weight_terms(first_grad, mixed_ref, 0, terms_ref)


def first_backward(
    e0, e1, e2, e3, r0, r1, r2, r3, input_ref, qkv_ref, probs_ref, gain_ref, back_order_ref,
    w_qkv_hbm, w_out_hbm,
    output_ref, grad_fields_ref,
    w_qkv_ref, w_out_ref, sems, hold_ref, grad_mixed_ref, turned_ref, grad_rows_ref,
):
    copy_qkv, copy_out = start_weights(w_qkv_hbm, w_out_hbm, 0, w_qkv_ref, w_out_ref, sems)
    back_order = back_order_ref[...]
    normed, inv_std = layer_norm(input_ref[...].astype(f32))
    grad_f = join_quads((e0, e1, e2, e3), hold_ref)
    copy_out.wait()
    back_attend(
        grad_f.astype(bf16), qkv_ref, probs_ref, w_out_ref, grad_mixed_ref, turned_ref,
        grad_rows_ref,
    )
    copy_qkv.wait()
    grad_input = back_norm(grad_f, normed, inv_std, gain_ref[0:1, :], grad_rows_ref, w_qkv_ref)
    write_tile(grad_input.astype(bf16), back_order, hold_ref, grad_fields_ref)
    result = join_quads((r0, r1, r2, r3), hold_ref).astype(bf16)
    write_tile(result, back_order, hold_ref, output_ref)


def call(kernel, outs, scratch, in_spaces, args, flops, name):
    return pl.pallas_call(
        kernel,
        out_shape=[jax.ShapeDtypeStruct(shape, kind) for shape, kind in outs],
        in_specs=[pl.BlockSpec(memory_space=space) for space in in_spaces],
        out_specs=[pl.BlockSpec(memory_space=pltpu.VMEM) for _ in outs],
        scratch_shapes=scratch,
        compiler_params=pltpu.CompilerParams(vmem_limit_bytes=48 * 1024 * 1024),
        cost_estimate=pl.CostEstimate(flops=flops, bytes_accessed=8_000_000, transcendentals=0),
        name=name,
    )(*args)


def exchange(quads, forward):
    n_lat, n_lon = lax.axis_size("lat"), lax.axis_size("lon")
    by = -1 if forward else 1

    def moved(shard, over_lat, over_lon):
        pairs = []
        for row in range(n_lat):
            for col in range(n_lon):
                to = (row + by * over_lat) % n_lat * n_lon + (col + by * over_lon) % n_lon
                pairs.append((row * n_lon + col, to))
        return lax.ppermute(shard, ("lat", "lon"), pairs)

    if forward:
        return (
            quads[3],
            moved(quads[2], 0, 1),
            moved(quads[1], 1, 0),
            moved(quads[0], 1, 1),
        )
    return (
        moved(quads[3], 1, 1),
        moved(quads[2], 1, 0),
        moved(quads[1], 0, 1),
        quads[0],
    )


def reduce_terms(terms, scale):
    n_lon, rows, _ = terms.shape
    n_lat, n_member = lax.axis_size("lat"), lax.axis_size("member")
    parts = lax.all_to_all(terms, "lon", 0, 0, tiled=True)
    (lon_sum,) = call(
        sum_lon,
        [((n_member * n_lat, rows, -(-D // n_lat // 128) * 128), bf16)],
        [],
        [pltpu.VMEM],
        (parts,),
        5_000_000,
        "sum_lon",
    )
    parts = lax.all_to_all(lon_sum, ("member", "lat"), 0, 0, tiled=True)
    (total,) = call(
        functools.partial(sum_lat, scale),
        [((2, D // n_lat, D // n_lon), f32)],
        [],
        [pltpu.VMEM],
        (parts,),
        1_000_000,
        "sum_lat",
    )
    return total


def body(fields, cotangent, qkv_weight, out_weight, norm_gain, bias_table, bias_index, region):
    order, at_line, at_col = constants()
    back_order = jnp.asarray(order.T, bf16)
    order = jnp.asarray(order, bf16)
    at_line, at_col = jnp.asarray(at_line, bf16), jnp.asarray(at_col, bf16)
    edge = (lax.axis_index("lat") == lax.axis_size("lat") - 1).astype(jnp.int32).reshape(1)
    vmem, hbm = pltpu.VMEM, pl.ANY
    n_lon = lax.axis_size("lon")
    quads = [((QUAD, D), bf16)] * 4
    weights_scratch = [
        pltpu.VMEM((D, 3 * D), bf16),
        pltpu.VMEM((D, D), bf16),
        pltpu.SemaphoreType.DMA((2,)),
    ]
    gather_scratch = [pltpu.VMEM((WIN, 256), jnp.int32), pltpu.VMEM((HEADS, 1, CHUNKS * 128), f32)]
    hold = pltpu.VMEM((WIN, D), f32)
    mixed_scratch = pltpu.VMEM((WIN, D), bf16)
    back_scratch = [
        pltpu.VMEM((WIN, D), bf16),
        pltpu.VMEM((4, D, WIN), bf16),
        pltpu.VMEM((WIN, 3 * D), bf16),
    ]
    first = call(
        first_forward,
        quads * 3 + [((WIN, D), bf16), ((WIN, 3 * D), bf16), ((HEADS, WIN, WIN), bf16)],
        weights_scratch
        + [pltpu.VMEM((HEADS, WIN, WIN), f32)]
        + gather_scratch
        + [hold, mixed_scratch],
        [vmem] * 6 + [hbm] * 2,
        (fields, cotangent, norm_gain, bias_table, bias_index, order, qkv_weight, out_weight),
        1_000_000_000,
        "first_forward",
    )
    block_one, grad_two, mixed_one = first[0:4], first[4:8], first[8:12]
    inputs, qkv_one, probs_one = first[12:]
    shifted = exchange(block_one, True)
    grad_shifted = exchange(grad_two, True)
    mixed_shifted = exchange(mixed_one, True)
    (bias_two,) = call(
        second_bias,
        [((HEADS, WIN, WIN), f32)],
        gather_scratch,
        [vmem] * 6 + [pltpu.SMEM],
        (bias_table, bias_index, order, region, at_line, at_col, edge),
        3_000_000_000,
        "second_bias",
    )
    second = call(
        second_block,
        quads * 2 + [((n_lon, 2 * D // n_lon, D), bf16)],
        weights_scratch
        + [hold, mixed_scratch, pltpu.VMEM((WIN, 3 * D), bf16), pltpu.VMEM((HEADS, WIN, WIN), bf16)]
        + back_scratch,
        [vmem] * 14 + [hbm] * 2,
        (*shifted, *grad_shifted, *mixed_shifted, norm_gain, bias_two, qkv_weight, out_weight),
        4_000_000_000,
        "second_block",
    )
    block_two, grad_mid, terms = second[0:4], second[4:8], second[8]
    grad_first = exchange(grad_mid, False)
    result = exchange(block_two, False)
    output, grad_fields = call(
        first_backward,
        [(fields.shape, bf16)] * 2,
        weights_scratch + [hold] + back_scratch,
        [vmem] * 13 + [hbm] * 2,
        (
            *grad_first, *result, inputs, qkv_one, probs_one, norm_gain, back_order,
            qkv_weight, out_weight,
        ),
        3_000_000_000,
        "first_backward",
    )
    token_total = lax.axis_size("member") * lax.axis_size("lat") * n_lon * WIN
    grad_out = reduce_terms(terms, float(token_total) ** (-0.5))
    return output, grad_fields, grad_out


def solution(mesh):
    grid = P("member", None, "lat", "lon", None)
    placed = (grid, grid, P(), P(), P(), P(None, "lat", None, None), P(), P(None, "lat", "lon"))
    return jax.shard_map(
        body,
        mesh=mesh,
        in_specs=placed,
        out_specs=(grid, grid, P(None, "lat", "lon")),
        check_vma=False,
    )
```

```python
import functools
import math

import jax
import jax.numpy as jnp
import numpy as np
from jax import lax
from jax.experimental import pallas as pl
from jax.experimental.pallas import tpu as pltpu
from jax.sharding import PartitionSpec as P

LEVELS = 2
WIN_LAT = 6
WIN_LON = 12
HALF_LAT = WIN_LAT // 2
HALF_LON = WIN_LON // 2
WIN = LEVELS * WIN_LAT * WIN_LON
QUAD = WIN // 4
D = 768
HEADS = 24
HEAD_DIM = D // HEADS
GROUP = 128 // HEAD_DIM
GROUPS = HEADS // GROUP
NREL = 759
CHUNKS = 6
DEPTH = 24
TAIL = WIN - 128
SCALE = HEAD_DIM ** (-0.5)
EPS = 1e-05

bf16 = jnp.bfloat16
f32 = jnp.float32


def quad_order():
    token = np.arange(WIN)
    quad, inside = token // QUAD, token % QUAD
    level = inside // (HALF_LAT * HALF_LON)
    row = inside // HALF_LON % HALF_LAT + HALF_LAT * (quad // 2)
    col = inside % HALF_LON + HALF_LON * (quad % 2)
    stored = (row * WIN_LON + col) * LEVELS + level
    window = (level * WIN_LAT + row) * WIN_LON + col
    return row * LEVELS + level, col, stored, window


def constants():
    line, col, stored, window = quad_order()
    order = np.eye(WIN, dtype=np.float32)[stored]
    window_order = np.eye(WIN, dtype=np.float32)[window]
    at_line = np.eye(LEVELS * WIN_LAT, dtype=np.float32)[line]
    at_col = np.eye(WIN_LON, dtype=np.float32)[col]
    return order, window_order, at_line, at_col


def contract(left, right, dims):
    return lax.dot_general(left, right, ((dims[:1], dims[1:]), ((), ())), preferred_element_type=f32)


def mm(left, right):
    return contract(left, right, (1, 0))


def mm_t(left, right):
    return contract(left, right, (1, 1))


def eye(size):
    rows = lax.broadcasted_iota(jnp.int32, (size, size), 0)
    cols = lax.broadcasted_iota(jnp.int32, (size, size), 1)
    return (rows == cols).astype(f32).astype(bf16)


def head_masks():
    lane = lax.broadcasted_iota(jnp.int32, (1, 128), 1)
    masks = []
    for head in range(GROUP):
        inside = jnp.logical_and(lane >= head * HEAD_DIM, lane < (head + 1) * HEAD_DIM)
        masks.append(inside.astype(f32).astype(bf16))
    return masks


def layer_norm(values_f):
    centred = values_f - jnp.mean(values_f, axis=-1, keepdims=True)
    variance = jnp.mean(centred * centred, axis=-1, keepdims=True)
    inv_std = lax.rsqrt(variance + EPS)
    return centred * inv_std, inv_std


def place_index(index_ref, order, wide_ref):
    index_f = index_ref[...].astype(f32)
    high = jnp.floor(index_f * 0.125)
    low = index_f - high * 8.0
    parts = []
    for part in (high, low):
        half = mm(order, part.astype(bf16)).astype(bf16)
        parts.append(mm_t(half, order))
    moved = parts[0] * 8.0 + parts[1]
    wide_ref[:, :WIN] = (moved + 0.5).astype(jnp.int32)
    wide_ref[:, WIN:] = jnp.zeros((WIN, 256 - WIN), jnp.int32)
    lane = lax.broadcasted_iota(jnp.int32, (DEPTH, 128), 1)
    packed = jnp.zeros((DEPTH, 128), jnp.int32)
    for strip in range(WIN // DEPTH):
        piece = wide_ref[strip * DEPTH : (strip + 1) * DEPTH, 128:256]
        if strip:
            piece = pltpu.roll(piece, strip * TAIL, axis=1)
        inside = jnp.logical_and(lane >= strip * TAIL, lane < (strip + 1) * TAIL)
        packed = jnp.where(inside, piece, packed)
    wide_ref[:DEPTH, 128:256] = packed


def lane_gather(row, index):
    numbers = lax.GatherDimensionNumbers(
        offset_dims=(),
        collapsed_slice_dims=(1,),
        start_index_map=(1,),
        operand_batching_dims=(0,),
        start_indices_batching_dims=(0,),
    )
    mode = lax.GatherScatterMode.PROMISE_IN_BOUNDS
    return lax.gather(row, index[..., None], numbers, slice_sizes=(1, 1), mode=mode)


def gather_bias(wide_ref, table_ref, bias_ref, rows_ref, tail_ref, mask_ref, done=None):
    for head in range(HEADS):
        rows_ref[head, :, :NREL] = jnp.broadcast_to(table_ref[head : head + 1, :], (8, NREL))

    def look_up(index, store):
        low_part = jnp.bitwise_and(index, 127)
        high_part = jnp.right_shift(index, 7)
        for head in range(HEADS):
            found = jnp.zeros((8, 128), f32)
            for chunk in range(CHUNKS):
                row = rows_ref[head, :, chunk * 128 : (chunk + 1) * 128]
                found = jnp.where(high_part == chunk, lane_gather(row, low_part), found)
            store(head, found)

    def main_strip(strip, carry):
        lines = pl.ds(pl.multiple_of(strip * 8, 8), 8)
        mask = None if mask_ref is None else mask_ref[lines, :128]

        def store(head, found):
            bias_ref[head, lines, :128] = found if mask is None else found + mask

        look_up(wide_ref[lines, :128], store)
        return carry

    def tail_strip(strip, carry):
        lines = pl.ds(pl.multiple_of(strip * 8, 8), 8)

        def store(head, found):
            tail_ref[head, lines, :] = found

        look_up(wide_ref[lines, 128:256], store)
        return carry

    def unpack(head, carry):
        rest = tail_ref[head]
        for strip in range(WIN // DEPTH):
            lines = slice(strip * DEPTH, (strip + 1) * DEPTH)
            piece = rest if strip == 0 else pltpu.roll(rest, 128 - strip * TAIL, axis=1)
            piece = piece[:, :TAIL]
            if mask_ref is not None:
                piece = piece + mask_ref[lines, 128:WIN]
            bias_ref[head, lines, 128:WIN] = piece
        return carry

    lax.fori_loop(0, DEPTH // 8, tail_strip, 0, unroll=3)
    lax.fori_loop(0, HEADS, unpack, 0, unroll=4)
    for third in range(3):
        lax.fori_loop(third * 6, third * 6 + 6, main_strip, 0, unroll=6)
        if done is not None:
            done(third)


def project_qkv(hidden, w_parts, qkv_ref):
    for part in range(3):
        qkv_ref[:, part * D : (part + 1) * D] = mm(hidden, w_parts(part)[...]).astype(bf16)


def attend(qkv_ref, bias_ref, probs_ref, mixed_ref):
    masks = head_masks()
    for group in range(GROUPS):
        query = qkv_ref[:, group * 128 : (group + 1) * 128]
        key = qkv_ref[:, D + group * 128 : D + (group + 1) * 128]
        value = qkv_ref[:, 2 * D + group * 128 : 2 * D + (group + 1) * 128]
        total = jnp.zeros((WIN, 128), f32)
        for inner in range(GROUP):
            head = group * GROUP + inner
            scores = mm_t(query * masks[inner], key) * SCALE + bias_ref[head]
            exponent = jnp.exp(scores - jnp.max(scores, axis=-1, keepdims=True))
            share = 1.0 / jnp.sum(exponent, axis=-1, keepdims=True)
            weights = (exponent * share).astype(bf16)
            probs_ref[head] = weights
            total += mm(weights, value * masks[inner])
        mixed_ref[:, group * 128 : (group + 1) * 128] = total.astype(bf16)


def back_attend(grad, qkv_ref, probs_ref, w_out_ref, grad_mixed_ref, turned_ref, rows_ref):
    masks = head_masks()
    unit = eye(256)
    small = eye(WIN)
    grad_mixed_ref[...] = mm_t(grad, w_out_ref[...]).astype(bf16)
    for part in range(3):
        cols = slice(part * 256, (part + 1) * 256)
        turned_ref[0, cols, :] = mm_t(unit, grad_mixed_ref[:, cols]).astype(bf16)
        turned_ref[1, cols, :] = mm_t(unit, qkv_ref[:, cols]).astype(bf16)
    for group in range(GROUPS):
        cols = slice(group * 128, (group + 1) * 128)
        grad_mixed = grad_mixed_ref[:, cols]
        key = qkv_ref[:, D + group * 128 : D + (group + 1) * 128]
        value = qkv_ref[:, 2 * D + group * 128 : 2 * D + (group + 1) * 128]
        grad_query = jnp.zeros((WIN, 128), f32)
        for inner in range(GROUP):
            head = group * GROUP + inner
            lines = slice(head * HEAD_DIM, (head + 1) * HEAD_DIM)
            grad_weights = mm_t(grad_mixed * masks[inner], value)
            weights = probs_ref[head]
            probs = weights.astype(f32)
            row_inner = jnp.sum(grad_weights * probs, axis=-1, keepdims=True)
            grad_scores = (probs * (grad_weights - row_inner) * SCALE).astype(bf16)
            grad_query += mm(grad_scores, key * masks[inner])
            turned_ref[2, lines, :] = mm(turned_ref[1, lines, :], grad_scores).astype(bf16)
            turned_ref[3, lines, :] = mm(turned_ref[0, lines, :], weights).astype(bf16)
        rows_ref[:, cols] = grad_query.astype(bf16)
    for part in range(3):
        cols = slice(part * 256, (part + 1) * 256)
        for which in (1, 2):
            out = slice(which * D + part * 256, which * D + (part + 1) * 256)
            rows_ref[:, out] = mm_t(small, turned_ref[1 + which, cols, :]).astype(bf16)


def back_norm(grad_f, normed, inv_std, gain, rows_ref, w_parts):
    grad_hidden = jnp.zeros((WIN, D), f32)
    for part in range(3):
        grad_hidden += mm_t(rows_ref[:, part * D : (part + 1) * D], w_parts(part)[...])
    grad_normed = grad_hidden * gain
    mean_one = jnp.mean(grad_normed, axis=-1, keepdims=True)
    mean_two = jnp.mean(grad_normed * normed, axis=-1, keepdims=True)
    return grad_f + inv_std * (grad_normed - mean_one - normed * mean_two)


def put_quads(values_f, hold_ref, quad_refs, section):
    hold_ref[...] = values_f
    cols = slice(section * D, (section + 1) * D)
    for quad in range(4):
        quad_refs[quad][:, cols] = hold_ref[quad * QUAD : (quad + 1) * QUAD, :].astype(bf16)


def take_quads(quad_refs, hold_ref, section):
    cols = slice(section * D, (section + 1) * D)
    for quad in range(4):
        hold_ref[quad * QUAD : (quad + 1) * QUAD, :] = quad_refs[quad][:, cols].astype(f32)
    return hold_ref[...]


def first_forward(
    blocks, bias_ref, rows_ref, tail_ref, hold_ref, mixed_ref,
):
    quads = blocks.outs[:4]
    wide_ref, input_ref, qkv_ref, probs_ref = blocks.outs[4:]
    place_index(blocks.get(1), blocks.get(0)[...], wide_ref)
    blocks.put(4)
    gather_bias(wide_ref, blocks.get(2), bias_ref, rows_ref, tail_ref, None)
    order = blocks.get(10)[...]
    values_f = mm(order, blocks.get(3)[...].reshape(WIN, D))
    input_ref[...] = values_f.astype(bf16)
    blocks.put(5)
    normed, _ = layer_norm(values_f)
    hidden = (normed * blocks.get(4)[0:1, :]).astype(bf16)
    project_qkv(hidden, lambda part: blocks.get(7 + part), qkv_ref)
    blocks.put(6)
    attend(qkv_ref, bias_ref, probs_ref, mixed_ref)
    blocks.put(7)
    put_quads(mm(order, blocks.get(6)[...].reshape(WIN, D)), hold_ref, quads, 1)
    mixed = mixed_ref[...]
    put_quads(mixed.astype(f32), hold_ref, quads, 2)
    result = input_ref[...].astype(f32) + mm(mixed, blocks.get(5)[...])
    put_quads(result, hold_ref, quads, 0)
    for quad in range(4):
        blocks.put(quad)


def second_bias(blocks, rows_ref, tail_ref, mask_ref, sems):
    region_ref, edge_ref, bias_ref = blocks.get(0), blocks.get(1), blocks.outs[0]
    labels = jnp.concatenate([region_ref[row] for row in range(WIN_LAT)], axis=0)
    labels = labels.astype(f32) * 2.0 - 1.0
    at_line, at_col = blocks.get(2)[...], blocks.get(3)[...]
    column = jnp.sum(mm(at_line, labels.astype(bf16)) * at_col.astype(f32), axis=1, keepdims=True)
    signs = jnp.broadcast_to(column, (WIN, 128)).astype(bf16)
    same = mm_t(signs, signs) > 0.0
    half = WIN // 2
    rows = lax.broadcasted_iota(jnp.int32, (WIN, WIN), 0) >= half
    cols = lax.broadcasted_iota(jnp.int32, (WIN, WIN), 1) >= half
    across = jnp.logical_and(jnp.logical_xor(rows, cols), edge_ref[0] != 0)
    allowed = jnp.logical_and(same, jnp.logical_not(across))
    mask_ref[...] = jnp.where(allowed, 0.0, -jnp.inf)

    def done(third):
        blocks.put(0, pl.ds(third * (WIN // 3), WIN // 3), sems.at[third])

    gather_bias(blocks.get(5), blocks.get(4), bias_ref, rows_ref, tail_ref, mask_ref, done)


def pick_columns(core, width):
    rows = lax.broadcasted_iota(jnp.int32, (D // 2, D), 0)
    cols = lax.broadcasted_iota(jnp.int32, (D // 2, D), 1)
    part = jnp.floor((rows.astype(f32) + 0.5) * (1.0 / width)).astype(jnp.int32)
    return (cols == rows + width * (part + core)).astype(f32).astype(bf16)


def second_block(
    width, blocks, hold_ref, mixed_ref, qkv_ref, probs_ref, grad_mixed_ref, turned_ref, grad_rows_ref
):
    leaving = blocks.outs[:4]
    own_ref, other_ref = blocks.outs[4:]
    arrived = [blocks.get(quad) for quad in range(4)]
    values_f = take_quads(arrived, hold_ref, 0)
    normed, inv_std = layer_norm(values_f)
    gain = blocks.get(4)[1:2, :]
    hidden = (normed * gain).astype(bf16)

    def w_parts(part):
        return blocks.get(5 + part)

    project_qkv(hidden, w_parts, qkv_ref)
    attend(qkv_ref, blocks.get(8), probs_ref, mixed_ref)
    w_out_ref = blocks.get(9)
    result = values_f + mm(mixed_ref[...], w_out_ref[...])
    put_quads(result, hold_ref, leaving, 1)
    grad_f = take_quads(arrived, hold_ref, 1)
    grad = grad_f.astype(bf16)
    first_mixed = take_quads(arrived, hold_ref, 2).astype(bf16)
    half = D // 2
    core = blocks.get(10)[0]
    own, other = pick_columns(core, width), pick_columns(1 - core, width)
    for ref, pick in ((own_ref, own), (other_ref, other)):
        ref[:, :D] = first_mixed
        ref[:, D : 2 * D] = mixed_ref[...]
        ref[:, 2 * D + half :] = mm_t(grad, pick).astype(bf16)
    back_attend(grad, qkv_ref, probs_ref, w_out_ref, grad_mixed_ref, turned_ref, grad_rows_ref)
    grad_input = back_norm(grad_f, normed, inv_std, gain, grad_rows_ref, w_parts)
    first_grad = grad_input.astype(bf16)
    other_ref[:, 2 * D : 2 * D + half] = mm_t(first_grad, other).astype(bf16)
    blocks.put(5)
    put_quads(grad_input, hold_ref, leaving, 0)
    for quad in range(4):
        blocks.put(quad)
    own_ref[:, 2 * D : 2 * D + half] = mm_t(first_grad, own).astype(bf16)
    blocks.put(4)


def weight_terms(blocks):
    terms_ref = blocks.outs[0]
    n_parts, rows, _ = terms_ref.shape
    rows //= 2
    half = n_parts * rows
    unit = eye(half)
    packs = (blocks.get(0), blocks.get(1))
    for block in range(2):
        cols = slice(2 * D + block * half, 2 * D + (block + 1) * half)
        total = jnp.zeros((half, D), f32)
        for pack in packs:
            turned = mm_t(unit, pack[:, cols]).astype(bf16)
            total += mm(turned, pack[:, block * D : (block + 1) * D])
        for part in range(n_parts):
            piece = total[part * rows : (part + 1) * rows, :].astype(bf16)
            terms_ref[part, block * rows : (block + 1) * rows, :] = piece
    blocks.put(0)


def fold(width):
    return 128 // math.gcd(width, 128)


def sum_lon(blocks):
    parts_ref, out_ref = blocks.get(0), blocks.outs[0]
    total = parts_ref[0].astype(f32)
    for part in range(1, parts_ref.shape[0]):
        total += parts_ref[part].astype(f32)
    copies = 2
    places = out_ref.shape[0] // copies
    width = D // places
    folds = fold(width)
    rows = total.shape[0] // folds
    for place in range(places):
        piece = total[:, place * width : (place + 1) * width]
        lines = [piece[line * rows : (line + 1) * rows] for line in range(folds)]
        flat = jnp.concatenate(lines, axis=1)
        tiles = [flat[:, start : start + 128] for start in range(0, folds * width, 128)]
        piece = jnp.concatenate(tiles, axis=0).astype(bf16)
        for copy in range(copies):
            out_ref[copy * places + place] = piece
    blocks.put(0)


def sum_lat(scale, blocks):
    parts_ref, out_ref = blocks.get(0), blocks.outs[0]
    total = parts_ref[0].astype(f32)
    for part in range(1, parts_ref.shape[0]):
        total += parts_ref[part].astype(f32)
    _, rows, width = out_ref.shape
    folds = fold(width)
    lines = 2 * rows // folds
    tiles = [total[start : start + lines] for start in range(0, total.shape[0], lines)]
    flat = jnp.concatenate(tiles, axis=1) * scale
    pieces = [flat[:, line * width : (line + 1) * width] for line in range(folds)]
    total = jnp.concatenate(pieces, axis=0)
    for block in range(2):
        out_ref[block] = total[block * rows : (block + 1) * rows]
    blocks.put(0)


def first_backward(blocks, hold_ref, grad_mixed_ref, turned_ref, grad_rows_ref):
    grad_fields_ref, output_ref = blocks.outs
    normed, inv_std = layer_norm(blocks.get(4)[...].astype(f32))
    arrived = [blocks.get(quad) for quad in range(4)]
    grad_f = take_quads(arrived, hold_ref, 0)
    qkv_ref, probs_ref, w_out_ref = blocks.get(5), blocks.get(6), blocks.get(7)
    back_attend(
        grad_f.astype(bf16), qkv_ref, probs_ref, w_out_ref, grad_mixed_ref, turned_ref,
        grad_rows_ref,
    )
    gain = blocks.get(8)[0:1, :]
    grad_input = back_norm(
        grad_f, normed, inv_std, gain, grad_rows_ref, lambda part: blocks.get(10 + part)
    )
    back_order = blocks.get(9)[...]
    shape = grad_fields_ref.shape
    grad_input = mm(back_order, grad_input.astype(bf16))
    grad_fields_ref[...] = grad_input.astype(bf16).reshape(shape)
    blocks.put(0)
    result = mm(back_order, take_quads(arrived, hold_ref, 1).astype(bf16))
    output_ref[...] = result.astype(bf16).reshape(shape)
    blocks.put(1)


class Blocks:
    def __init__(self, in_refs, in_holds, out_refs, out_holds, in_sems, out_sems):
        self.ins, self.outs, self.waiting, self.leaving = [], [], {}, []
        self.out_refs, self.out_sems = out_refs, out_sems
        for place, (ref, hold) in enumerate(zip(in_refs, in_holds)):
            if hold is not None:
                copy = pltpu.make_async_copy(ref, hold, in_sems.at[place])
                copy.start()
                self.waiting[place] = copy
            self.ins.append(ref if hold is None else hold)
        for ref, hold in zip(out_refs, out_holds):
            self.outs.append(ref if hold is None else hold)

    def get(self, place):
        if place in self.waiting:
            self.waiting.pop(place).wait()
        return self.ins[place]

    def put(self, place, rows=None, sem=None):
        source, target = self.outs[place], self.out_refs[place]
        if rows is not None:
            source, target = source.at[:, rows, :], target.at[:, rows, :]
        sem = self.out_sems.at[place] if sem is None else sem
        copy = pltpu.make_async_copy(source, target, sem)
        copy.start()
        self.leaving.append(copy)


HBM, SMEM = pltpu.HBM, pltpu.SMEM


def call(kernel, ins, outs, scratch, flops, name, mib=63):
    holds = []
    for array, space, index in ins:
        if space is HBM:
            shape = array.shape
            if index is not None:
                shape = array.shape[1:] if isinstance(index, int) else index[0]
            holds.append(pltpu.VMEM(shape, array.dtype))
    for shape, kind, space in outs:
        if space is HBM:
            holds.append(pltpu.VMEM(shape, kind))
    n_in, n_out = len(ins), len(outs)

    def run(*refs):
        in_refs = []
        for ref, (_, _, index) in zip(refs, ins):
            if index is not None:
                ref = ref.at[index] if isinstance(index, int) else index[1](ref)
            in_refs.append(ref)
        out_refs = refs[n_in : n_in + n_out]
        spare = list(refs[n_in + n_out : n_in + n_out + len(holds)])
        in_sems, out_sems, *rest = refs[n_in + n_out + len(holds) :]
        in_holds = [spare.pop(0) if space is HBM else None for _, space, _ in ins]
        out_holds = [spare.pop(0) if space is HBM else None for _, _, space in outs]
        blocks = Blocks(in_refs, in_holds, out_refs, out_holds, in_sems, out_sems)
        kernel(blocks, *rest)
        for copy in blocks.leaving:
            copy.wait()

    return pl.pallas_call(
        run,
        out_shape=[jax.ShapeDtypeStruct(shape, kind) for shape, kind, _ in outs],
        in_specs=[pl.BlockSpec(memory_space=space) for _, space, _ in ins],
        out_specs=[pl.BlockSpec(memory_space=space) for _, _, space in outs],
        scratch_shapes=holds
        + [pltpu.SemaphoreType.DMA((n_in,)), pltpu.SemaphoreType.DMA((n_out,))]
        + scratch,
        compiler_params=pltpu.CompilerParams(vmem_limit_bytes=mib * 1024 * 1024),
        cost_estimate=pl.CostEstimate(flops=flops, bytes_accessed=4_000_000, transcendentals=0),
        name=name,
    )(*[array for array, _, _ in ins])


def exchange(quads, forward):
    n_lat, n_pair, n_core = (lax.axis_size(axis) for axis in ("lat", "pair", "core"))
    n_lon = n_pair * n_core
    by = -1 if forward else 1

    def moved(shard, over_lat, over_lon):
        pairs = []
        for row in range(n_lat):
            for col in range(n_lon):
                to = (row + by * over_lat) % n_lat * n_lon + (col + by * over_lon) % n_lon
                pairs.append((row * n_lon + col, to))
        return lax.ppermute(shard, ("lat", "pair", "core"), pairs)

    if forward:
        return (
            quads[3],
            moved(quads[2], 0, 1),
            moved(quads[1], 1, 0),
            moved(quads[0], 1, 1),
        )
    return (
        moved(quads[3], 1, 1),
        moved(quads[2], 1, 0),
        moved(quads[1], 0, 1),
        quads[0],
    )


def reduce_terms(own, other, returned, after, scale):
    n_lat, n_member = lax.axis_size("lat"), lax.axis_size("member")
    n_pair, n_core = lax.axis_size("pair"), lax.axis_size("core")
    rows = 2 * D // (n_pair * n_core)
    partner = lax.ppermute(other, "core", [(i, (i + 1) % n_core) for i in range(n_core)])
    (terms,) = call(
        weight_terms,
        [(own, HBM, None), (partner, HBM, None)],
        [((n_pair, rows, D), bf16, HBM)],
        [],
        30_000_000_000,
        "weight_terms",
        16,
    )
    terms, *_ = lax.optimization_barrier((terms, *returned))
    parts = lax.all_to_all(terms, "pair", 0, 0, tiled=True)
    (lon_sum,) = call(
        sum_lon,
        [(parts, HBM, None)] + [(array, pl.ANY, None) for array in after],
        [((n_member * n_lat, rows * D // n_lat // 128, 128), bf16, HBM)],
        [],
        5_000_000,
        "sum_lon",
        16,
    )
    parts = lax.all_to_all(lon_sum, ("member", "lat"), 0, 0, tiled=True)
    (total,) = call(
        functools.partial(sum_lat, scale),
        [(parts, HBM, None)],
        [((2, rows // 2, D // n_lat), f32, HBM)],
        [],
        1_000_000,
        "sum_lat",
        8,
    )
    return total.transpose(0, 2, 1)


def body(fields, cotangent, qkv_weight, out_weight, norm_gain, bias_table, bias_index, region):
    order, window_order, at_line, at_col = constants()
    window_order = jnp.asarray(window_order, bf16)
    back_order = jnp.asarray(order.T, bf16)
    order = jnp.asarray(order, bf16)
    at_line, at_col = jnp.asarray(at_line, bf16), jnp.asarray(at_col, bf16)
    edge = (lax.axis_index("lat") == lax.axis_size("lat") - 1).astype(jnp.int32).reshape(1)
    n_pair, n_core = lax.axis_size("pair"), lax.axis_size("core")
    core = lax.axis_index("core")

    def qkv_parts(block):
        def part_of(part):
            return (D, D), lambda ref: ref.at[block, :, pl.ds(part * D, D)]

        return [(qkv_weight, HBM, part_of(part)) for part in range(3)]

    gather_scratch = [pltpu.VMEM((HEADS, 8, CHUNKS * 128), f32), pltpu.VMEM((HEADS, DEPTH, 128), f32)]
    hold = pltpu.VMEM((WIN, D), f32)
    mixed_scratch = pltpu.VMEM((WIN, D), bf16)
    back_scratch = [
        pltpu.VMEM((WIN, D), bf16),
        pltpu.VMEM((4, D, WIN), bf16),
        pltpu.VMEM((WIN, 3 * D), bf16),
    ]
    cells = (WIN_LAT * WIN_LON, LEVELS, D)
    table = bias_table.transpose(0, 1, 3, 2).reshape(2, HEADS, NREL)
    first = call(
        first_forward,
        [
            (window_order, HBM, None),
            (bias_index, HBM, None),
            (table, HBM, 0),
            (fields.transpose(0, 2, 3, 1, 4).reshape(cells), HBM, None),
            (norm_gain, HBM, None),
            (out_weight, HBM, 0),
            (cotangent.transpose(0, 2, 3, 1, 4).reshape(cells), HBM, None),
        ]
        + qkv_parts(0)
        + [(order, HBM, None)],
        [((QUAD, 3 * D), bf16, HBM)] * 4
        + [
            ((WIN, 256), jnp.int32, HBM),
            ((WIN, D), bf16, HBM),
            ((WIN, 3 * D), bf16, HBM),
            ((HEADS, WIN, WIN), bf16, HBM),
        ],
        [pltpu.VMEM((HEADS, WIN, WIN), f32)] + gather_scratch + [hold, mixed_scratch],
        1_000_000_000,
        "first_forward",
    )
    wide, inputs, qkv_one, probs_one = first[4:]
    shifted = exchange(first[:4], True)
    (bias_two,) = call(
        second_bias,
        [
            (region.transpose(1, 0, 2), HBM, None),
            (edge, SMEM, None),
            (at_line, HBM, None),
            (at_col, HBM, None),
            (table, HBM, 1),
            (wide, HBM, None),
        ],
        [((HEADS, WIN, WIN), f32, HBM)],
        gather_scratch + [pltpu.VMEM((WIN, WIN), f32), pltpu.SemaphoreType.DMA((3,))],
        5_000_000_000,
        "second_bias",
    )
    second = call(
        functools.partial(second_block, D // (n_pair * n_core)),
        [(quad, HBM, None) for quad in shifted]
        + [
            (norm_gain, HBM, None),
            *qkv_parts(1),
            (bias_two, HBM, None),
            (out_weight, HBM, 1),
            (core.astype(jnp.int32).reshape(1), SMEM, None),
        ],
        [((QUAD, 2 * D), bf16, HBM)] * 4 + [((WIN, 3 * D), bf16, HBM)] * 2,
        [hold, mixed_scratch, pltpu.VMEM((WIN, 3 * D), bf16), pltpu.VMEM((HEADS, WIN, WIN), bf16)]
        + back_scratch,
        15_000_000_000,
        "second_block",
    )
    returned = exchange(second[:4], False)
    grad_fields, output = call(
        first_backward,
        [(quad, HBM, None) for quad in returned]
        + [
            (inputs, HBM, None),
            (qkv_one, HBM, None),
            (probs_one, HBM, None),
            (out_weight, HBM, 0),
            (norm_gain, HBM, None),
            (back_order, HBM, None),
        ]
        + qkv_parts(0),
        [(cells, bf16, HBM)] * 2,
        [hold] + back_scratch,
        9_000_000_000,
        "first_backward",
        61,
    )

    token_total = lax.axis_size("member") * lax.axis_size("lat") * n_pair * n_core * WIN
    scale = float(token_total) ** (-0.5)
    grad_out = reduce_terms(second[4], second[5], returned, (grad_fields,), scale)

    def whole(values):
        grid = values.reshape(1, WIN_LAT, WIN_LON, LEVELS, D)
        return grid.transpose(0, 3, 1, 2, 4)

    return whole(output), whole(grad_fields), grad_out


def solution(mesh):
    n_member, n_lat, n_lon = mesh.devices.shape
    split = mesh.devices.reshape(n_member, n_lat, n_lon // 2, 2)
    mesh = jax.sharding.Mesh(split, ("member", "lat", "pair", "core"))
    lon = ("pair", "core")
    grid = P("member", None, "lat", lon, None)
    placed = (grid, grid, P(), P(), P(), P(None, "lat", None, None), P(), P(None, "lat", lon))
    return jax.shard_map(
        body,
        mesh=mesh,
        in_specs=placed,
        out_specs=(grid, grid, P(None, "lat", lon)),
        check_vma=False,
    )
```

```python
import functools

import jax
import jax.numpy as jnp
import numpy as np
from jax import lax
from jax.experimental import pallas as pl
from jax.experimental.pallas import tpu as pltpu
from jax.sharding import PartitionSpec as P

LEVELS = 2
WIN_LAT = 6
WIN_LON = 12
HALF_LAT = WIN_LAT // 2
HALF_LON = WIN_LON // 2
WIN = LEVELS * WIN_LAT * WIN_LON
QUAD = WIN // 4
D = 768
HEADS = 24
HEAD_DIM = D // HEADS
GROUP = 128 // HEAD_DIM
GROUPS = HEADS // GROUP
NREL = 759
CHUNKS = 6
DEPTH = 24
TAIL = WIN - 128
SCALE = HEAD_DIM ** (-0.5)
EPS = 1e-05

bf16 = jnp.bfloat16
f32 = jnp.float32


def quad_order():
    token = np.arange(WIN)
    quad, inside = token // QUAD, token % QUAD
    level = inside // (HALF_LAT * HALF_LON)
    row = inside // HALF_LON % HALF_LAT + HALF_LAT * (quad // 2)
    col = inside % HALF_LON + HALF_LON * (quad % 2)
    stored = (row * WIN_LON + col) * LEVELS + level
    window = (level * WIN_LAT + row) * WIN_LON + col
    return row * LEVELS + level, col, stored, window


def constants():
    line, col, stored, window = quad_order()
    order = np.eye(WIN, dtype=np.float32)[stored]
    window_order = np.eye(WIN, dtype=np.float32)[window]
    at_line = np.eye(LEVELS * WIN_LAT, dtype=np.float32)[line]
    at_col = np.eye(WIN_LON, dtype=np.float32)[col]
    return order, window_order, at_line, at_col


def contract(left, right, dims):
    return lax.dot_general(left, right, ((dims[:1], dims[1:]), ((), ())), preferred_element_type=f32)


def mm(left, right):
    return contract(left, right, (1, 0))


def mm_t(left, right):
    return contract(left, right, (1, 1))


def eye(size):
    rows = lax.broadcasted_iota(jnp.int32, (size, size), 0)
    cols = lax.broadcasted_iota(jnp.int32, (size, size), 1)
    return (rows == cols).astype(f32).astype(bf16)


def head_masks():
    lane = lax.broadcasted_iota(jnp.int32, (1, 128), 1)
    masks = []
    for head in range(GROUP):
        inside = jnp.logical_and(lane >= head * HEAD_DIM, lane < (head + 1) * HEAD_DIM)
        masks.append(inside.astype(f32).astype(bf16))
    return masks


def layer_norm(values_f):
    centred = values_f - jnp.mean(values_f, axis=-1, keepdims=True)
    variance = jnp.mean(centred * centred, axis=-1, keepdims=True)
    inv_std = lax.rsqrt(variance + EPS)
    return centred * inv_std, inv_std


def place_index(index_ref, order, wide_ref):
    index_f = index_ref[...].astype(f32)
    high = jnp.floor(index_f * 0.125)
    low = index_f - high * 8.0
    parts = []
    for part in (high, low):
        half = mm(order, part.astype(bf16)).astype(bf16)
        parts.append(mm_t(half, order))
    moved = parts[0] * 8.0 + parts[1]
    wide_ref[:, :WIN] = (moved + 0.5).astype(jnp.int32)
    wide_ref[:, WIN:] = jnp.zeros((WIN, 256 - WIN), jnp.int32)
    lane = lax.broadcasted_iota(jnp.int32, (DEPTH, 128), 1)
    packed = jnp.zeros((DEPTH, 128), jnp.int32)
    for strip in range(WIN // DEPTH):
        piece = wide_ref[strip * DEPTH : (strip + 1) * DEPTH, 128:256]
        if strip:
            piece = pltpu.roll(piece, strip * TAIL, axis=1)
        inside = jnp.logical_and(lane >= strip * TAIL, lane < (strip + 1) * TAIL)
        packed = jnp.where(inside, piece, packed)
    wide_ref[:DEPTH, 128:256] = packed


def lane_gather(row, index):
    numbers = lax.GatherDimensionNumbers(
        offset_dims=(),
        collapsed_slice_dims=(1,),
        start_index_map=(1,),
        operand_batching_dims=(0,),
        start_indices_batching_dims=(0,),
    )
    mode = lax.GatherScatterMode.PROMISE_IN_BOUNDS
    return lax.gather(row, index[..., None], numbers, slice_sizes=(1, 1), mode=mode)


def gather_bias(wide_ref, table_ref, bias_ref, rows_ref, tail_ref, mask_ref, done=None):
    for head in range(HEADS):
        rows_ref[head, :, :NREL] = jnp.broadcast_to(table_ref[head : head + 1, :], (8, NREL))

    def look_up(index, store):
        low_part = jnp.bitwise_and(index, 127)
        high_part = jnp.right_shift(index, 7)
        for head in range(HEADS):
            found = jnp.zeros((8, 128), f32)
            for chunk in range(CHUNKS):
                row = rows_ref[head, :, chunk * 128 : (chunk + 1) * 128]
                found = jnp.where(high_part == chunk, lane_gather(row, low_part), found)
            store(head, found)

    def main_strip(strip, carry):
        lines = pl.ds(pl.multiple_of(strip * 8, 8), 8)
        mask = None if mask_ref is None else mask_ref[lines, :128]

        def store(head, found):
            bias_ref[head, lines, :128] = found if mask is None else found + mask

        look_up(wide_ref[lines, :128], store)
        return carry

    def tail_strip(strip, carry):
        lines = pl.ds(pl.multiple_of(strip * 8, 8), 8)

        def store(head, found):
            tail_ref[head, lines, :] = found

        look_up(wide_ref[lines, 128:256], store)
        return carry

    def unpack(head, carry):
        rest = tail_ref[head]
        for strip in range(WIN // DEPTH):
            lines = slice(strip * DEPTH, (strip + 1) * DEPTH)
            piece = rest if strip == 0 else pltpu.roll(rest, 128 - strip * TAIL, axis=1)
            piece = piece[:, :TAIL]
            if mask_ref is not None:
                piece = piece + mask_ref[lines, 128:WIN]
            bias_ref[head, lines, 128:WIN] = piece
        return carry

    lax.fori_loop(0, DEPTH // 8, tail_strip, 0, unroll=3)
    lax.fori_loop(0, HEADS, unpack, 0, unroll=4)
    for third in range(3):
        lax.fori_loop(third * 6, third * 6 + 6, main_strip, 0, unroll=6)
        if done is not None:
            done(third)


def project_qkv(hidden, w_parts, qkv_ref):
    for part in range(3):
        qkv_ref[:, part * D : (part + 1) * D] = mm(hidden, w_parts(part)[...]).astype(bf16)


def stack_heads(values, masks):
    return jnp.concatenate([values * mask for mask in masks], axis=0)


def merge_heads(stacked):
    lane = lax.broadcasted_iota(jnp.int32, (1, 128), 1)
    merged = stacked[:WIN]
    for head in range(1, GROUP):
        later = lane >= head * HEAD_DIM
        merged = jnp.where(later, stacked[head * WIN : (head + 1) * WIN], merged)
    return merged


def group_cols(group, part):
    return slice(part * D + group * 128, part * D + (group + 1) * 128)


def attend(qkv_ref, bias_ref, probs_ref, mixed_ref):
    masks = head_masks()
    ones = jnp.ones((WIN, 128), bf16)
    for group in range(GROUPS):
        heads = slice(group * GROUP, (group + 1) * GROUP)
        query = qkv_ref[:, group_cols(group, 0)]
        key = qkv_ref[:, group_cols(group, 1)]
        value = qkv_ref[:, group_cols(group, 2)]
        scores = mm_t(stack_heads(query, masks), key) * SCALE
        scores = scores + bias_ref[heads].reshape(GROUP * WIN, WIN)
        exponent = jnp.exp(scores - jnp.max(scores, axis=-1, keepdims=True)).astype(bf16)
        product = mm(exponent, jnp.concatenate([value, ones], axis=1))
        share = 1.0 / product[:, 128:]
        weights = exponent.astype(f32) * jnp.concatenate([share, share[:, : WIN - 128]], axis=1)
        probs_ref[heads] = weights.astype(bf16).reshape(GROUP, WIN, WIN)
        mixed = merge_heads(product[:, :128] * share)
        mixed_ref[:, group_cols(group, 0)] = mixed.astype(bf16)


def back_attend(grad, qkv_ref, probs_ref, mixed_ref, w_out_ref, grad_mixed_ref, turned_ref, rows_ref):
    masks = head_masks()
    unit = eye(256)
    small = eye(WIN)
    minus = -jnp.ones((WIN, 128), bf16)
    grad_mixed_ref[...] = mm_t(grad, w_out_ref[...]).astype(bf16)
    for part in range(3):
        cols = slice(part * 256, (part + 1) * 256)
        turned_ref[0, cols, :] = mm_t(unit, grad_mixed_ref[:, cols]).astype(bf16)
        turned_ref[1, cols, :] = mm_t(unit, qkv_ref[:, cols]).astype(bf16)
    for group in range(GROUPS):
        heads = slice(group * GROUP, (group + 1) * GROUP)
        cols = group_cols(group, 0)
        grad_mixed = grad_mixed_ref[:, cols]
        key = qkv_ref[:, group_cols(group, 1)]
        value = qkv_ref[:, group_cols(group, 2)]
        weights = probs_ref[heads].reshape(GROUP * WIN, WIN)
        probs = weights.astype(f32)
        left = stack_heads(grad_mixed, masks)
        if mixed_ref is None:
            grad_weights = mm_t(left, value)
            moved = grad_weights - jnp.sum(grad_weights * probs, axis=-1, keepdims=True)
        else:
            inner = grad_mixed.astype(f32) * mixed_ref[:, cols].astype(f32)
            left = jnp.concatenate([left, stack_heads(inner.astype(bf16), masks)], axis=1)
            moved = mm_t(left, jnp.concatenate([value, minus], axis=1))
        grad_scores = (probs * moved * SCALE).astype(bf16)
        rows_ref[:, cols] = merge_heads(mm(grad_scores, key)).astype(bf16)
        for inner in range(GROUP):
            head = group * GROUP + inner
            lines = slice(head * HEAD_DIM, (head + 1) * HEAD_DIM)
            tokens = slice(inner * WIN, (inner + 1) * WIN)
            turned_ref[2, lines, :] = mm(turned_ref[1, lines, :], grad_scores[tokens]).astype(bf16)
            turned_ref[3, lines, :] = mm(turned_ref[0, lines, :], weights[tokens]).astype(bf16)
    for part in range(3):
        cols = slice(part * 256, (part + 1) * 256)
        for which in (1, 2):
            out = slice(which * D + part * 256, which * D + (part + 1) * 256)
            rows_ref[:, out] = mm_t(small, turned_ref[1 + which, cols, :]).astype(bf16)


def back_norm(grad_f, normed, inv_std, gain, rows_ref, w_parts):
    grad_hidden = jnp.zeros((WIN, D), f32)
    for part in range(3):
        grad_hidden += mm_t(rows_ref[:, part * D : (part + 1) * D], w_parts(part)[...])
    grad_normed = grad_hidden * gain
    mean_one = jnp.mean(grad_normed, axis=-1, keepdims=True)
    mean_two = jnp.mean(grad_normed * normed, axis=-1, keepdims=True)
    return grad_f + inv_std * (grad_normed - mean_one - normed * mean_two)


def put_quads(values_f, hold_ref, quad_refs, section):
    hold_ref[...] = values_f
    cols = slice(section * D, (section + 1) * D)
    for quad in range(4):
        quad_refs[quad][:, cols] = hold_ref[quad * QUAD : (quad + 1) * QUAD, :].astype(bf16)


def take_quads(quad_refs, hold_ref, section):
    cols = slice(section * D, (section + 1) * D)
    for quad in range(4):
        hold_ref[quad * QUAD : (quad + 1) * QUAD, :] = quad_refs[quad][:, cols].astype(f32)
    return hold_ref[...]


def first_forward(
    blocks, bias_ref, rows_ref, tail_ref, hold_ref, mixed_ref,
):
    quads = blocks.outs[:4]
    wide_ref, input_ref, qkv_ref, probs_ref = blocks.outs[4:]
    place_index(blocks.get(1), blocks.get(0)[...], wide_ref)
    blocks.put(4)
    order = blocks.get(4)[...]
    values_f = mm(order, blocks.get(3)[...].reshape(WIN, D))
    input_ref[...] = values_f.astype(bf16)
    blocks.put(5)
    normed, _ = layer_norm(values_f)
    hidden = (normed * blocks.get(5)[0:1, :]).astype(bf16)

    def project(third):
        cols = slice(third * D, (third + 1) * D)
        qkv_ref[:, cols] = mm(hidden, blocks.get(6 + third)[...]).astype(bf16)

    gather_bias(wide_ref, blocks.get(2), bias_ref, rows_ref, tail_ref, None, project)
    blocks.put(6)
    attend(qkv_ref, bias_ref, probs_ref, mixed_ref)
    blocks.put(7)
    put_quads(mm(order, blocks.get(10)[...].reshape(WIN, D)), hold_ref, quads, 1)
    mixed = mixed_ref[...]
    put_quads(mixed.astype(f32), hold_ref, quads, 2)
    result = input_ref[...].astype(f32) + mm(mixed, blocks.get(9)[...])
    put_quads(result, hold_ref, quads, 0)
    for quad in range(4):
        blocks.put(quad)


def second_bias(blocks, rows_ref, tail_ref, mask_ref, sems):
    region_ref, edge_ref, bias_ref = blocks.get(0), blocks.get(1), blocks.outs[0]
    labels = jnp.concatenate([region_ref[row] for row in range(WIN_LAT)], axis=0)
    labels = labels.astype(f32) * 2.0 - 1.0
    at_line, at_col = blocks.get(2)[...], blocks.get(3)[...]
    column = jnp.sum(mm(at_line, labels.astype(bf16)) * at_col.astype(f32), axis=1, keepdims=True)
    signs = jnp.broadcast_to(column, (WIN, 128)).astype(bf16)
    same = mm_t(signs, signs) > 0.0
    half = WIN // 2
    rows = lax.broadcasted_iota(jnp.int32, (WIN, WIN), 0) >= half
    cols = lax.broadcasted_iota(jnp.int32, (WIN, WIN), 1) >= half
    across = jnp.logical_and(jnp.logical_xor(rows, cols), edge_ref[0] != 0)
    allowed = jnp.logical_and(same, jnp.logical_not(across))
    mask_ref[...] = jnp.where(allowed, 0.0, -jnp.inf)

    def done(third):
        rows = pl.ds(third * (WIN // 3), WIN // 3)
        blocks.put(0, (slice(None), rows), sems.at[third])

    gather_bias(blocks.get(5), blocks.get(4), bias_ref, rows_ref, tail_ref, mask_ref, done)


def pick_columns(core, width):
    rows = lax.broadcasted_iota(jnp.int32, (D // 2, D), 0)
    cols = lax.broadcasted_iota(jnp.int32, (D // 2, D), 1)
    part = jnp.floor((rows.astype(f32) + 0.5) * (1.0 / width)).astype(jnp.int32)
    return (cols == rows + width * (part + core)).astype(f32).astype(bf16)


def second_block(
    width, blocks, hold_ref, mixed_ref, qkv_ref, probs_ref, grad_mixed_ref, turned_ref, grad_rows_ref
):
    leaving = blocks.outs[:4]
    own_ref, other_ref = blocks.outs[4:]
    arrived = [blocks.get(quad) for quad in range(4)]
    values_f = take_quads(arrived, hold_ref, 0)
    normed, inv_std = layer_norm(values_f)
    gain = blocks.get(4)[1:2, :]
    hidden = (normed * gain).astype(bf16)

    def w_parts(part):
        return blocks.get(5 + part)

    project_qkv(hidden, w_parts, qkv_ref)
    attend(qkv_ref, blocks.get(8), probs_ref, mixed_ref)
    w_out_ref = blocks.get(9)
    result = values_f + mm(mixed_ref[...], w_out_ref[...])
    put_quads(result, hold_ref, leaving, 1)
    grad_f = take_quads(arrived, hold_ref, 1)
    grad = grad_f.astype(bf16)
    first_mixed = take_quads(arrived, hold_ref, 2).astype(bf16)
    half = D // 2
    core = blocks.get(10)[0]
    own, other = pick_columns(core, width), pick_columns(1 - core, width)
    for ref, pick in ((own_ref, own), (other_ref, other)):
        ref[:, :D] = first_mixed
        ref[:, D : 2 * D] = mixed_ref[...]
        ref[:, 2 * D + half :] = mm_t(grad, pick).astype(bf16)
    back_attend(
        grad, qkv_ref, probs_ref, mixed_ref, w_out_ref, grad_mixed_ref, turned_ref, grad_rows_ref
    )
    grad_input = back_norm(grad_f, normed, inv_std, gain, grad_rows_ref, w_parts)
    first_grad = grad_input.astype(bf16)
    other_ref[:, 2 * D : 2 * D + half] = mm_t(first_grad, other).astype(bf16)
    blocks.put(5)
    put_quads(grad_input, hold_ref, leaving, 0)
    for quad in range(4):
        blocks.put(quad)
    own_ref[:, 2 * D : 2 * D + half] = mm_t(first_grad, own).astype(bf16)
    blocks.put(4)


def weight_terms(blocks, sems):
    terms_ref = blocks.outs[0]
    n_parts, rows, _ = terms_ref.shape
    n_parts //= 2
    half = n_parts * rows
    unit = eye(half)
    packs = (blocks.get(0), blocks.get(1))
    for block in range(2):
        cols = slice(2 * D + block * half, 2 * D + (block + 1) * half)
        total = jnp.zeros((half, D), f32)
        for pack in packs:
            turned = mm_t(unit, pack[:, cols]).astype(bf16)
            total += mm(turned, pack[:, block * D : (block + 1) * D])
        for part in range(n_parts):
            piece = total[part * rows : (part + 1) * rows, :].astype(bf16)
            terms_ref[block * n_parts + part] = piece
        blocks.put(0, pl.ds(block * n_parts, n_parts), sems.at[block])


def sum_plane(blocks):
    parts_ref, out_ref = blocks.get(0), blocks.outs[0]
    total = parts_ref[0].astype(f32)
    for part in range(1, parts_ref.shape[0]):
        total += parts_ref[part].astype(f32)
    copies = 2
    places = out_ref.shape[0] // copies
    width = D // places
    for place in range(places):
        piece = total[:, place * width : (place + 1) * width].astype(bf16)
        for copy in range(copies):
            out_ref[copy * places + place, :, :width] = piece
    blocks.put(0)


def sum_lat(scale, blocks):
    parts_ref, out_ref = blocks.get(0), blocks.outs[0]
    width = out_ref.shape[2]
    count = parts_ref.shape[0] // 2
    for block in range(2):
        total = parts_ref[block * count].astype(f32)
        for part in range(1, count):
            total += parts_ref[block * count + part].astype(f32)
        out_ref[block] = total[:, :width] * scale
    blocks.put(0)


def first_backward(blocks, hold_ref, grad_mixed_ref, turned_ref, grad_rows_ref):
    grad_fields_ref, output_ref = blocks.outs
    normed, inv_std = layer_norm(blocks.get(4)[...].astype(f32))
    arrived = [blocks.get(quad) for quad in range(4)]
    grad_f = take_quads(arrived, hold_ref, 0)
    qkv_ref, probs_ref, w_out_ref = blocks.get(5), blocks.get(6), blocks.get(7)
    back_attend(
        grad_f.astype(bf16), qkv_ref, probs_ref, None, w_out_ref, grad_mixed_ref, turned_ref,
        grad_rows_ref,
    )
    gain = blocks.get(8)[0:1, :]
    grad_input = back_norm(
        grad_f, normed, inv_std, gain, grad_rows_ref, lambda part: blocks.get(10 + part)
    )
    back_order = blocks.get(9)[...]
    shape = grad_fields_ref.shape
    grad_input = mm(back_order, grad_input.astype(bf16))
    grad_fields_ref[...] = grad_input.astype(bf16).reshape(shape)
    blocks.put(0)
    result = mm(back_order, take_quads(arrived, hold_ref, 1).astype(bf16))
    output_ref[...] = result.astype(bf16).reshape(shape)
    blocks.put(1)


class Blocks:
    def __init__(self, in_refs, in_holds, out_refs, out_holds, in_sems, out_sems):
        self.ins, self.outs, self.waiting, self.leaving = [], [], {}, []
        self.out_refs, self.out_sems = out_refs, out_sems
        for place, (ref, hold) in enumerate(zip(in_refs, in_holds)):
            if hold is not None:
                copy = pltpu.make_async_copy(ref, hold, in_sems.at[place])
                copy.start()
                self.waiting[place] = copy
            self.ins.append(ref if hold is None else hold)
        for ref, hold in zip(out_refs, out_holds):
            self.outs.append(ref if hold is None else hold)

    def get(self, place):
        if place in self.waiting:
            self.waiting.pop(place).wait()
        return self.ins[place]

    def put(self, place, part=None, sem=None):
        source, target = self.outs[place], self.out_refs[place]
        if part is not None:
            source, target = source.at[part], target.at[part]
        sem = self.out_sems.at[place] if sem is None else sem
        copy = pltpu.make_async_copy(source, target, sem)
        copy.start()
        self.leaving.append(copy)


HBM, SMEM = pltpu.HBM, pltpu.SMEM


def call(kernel, ins, outs, scratch, flops, name, mib=63):
    holds = []
    for array, space, index in ins:
        if space is HBM:
            shape = array.shape
            if index is not None:
                shape = array.shape[1:] if isinstance(index, int) else index[0]
            holds.append(pltpu.VMEM(shape, array.dtype))
    for shape, kind, space in outs:
        if space is HBM:
            holds.append(pltpu.VMEM(shape, kind))
    n_in, n_out = len(ins), len(outs)

    def run(*refs):
        in_refs = []
        for ref, (_, _, index) in zip(refs, ins):
            if index is not None:
                ref = ref.at[index] if isinstance(index, int) else index[1](ref)
            in_refs.append(ref)
        out_refs = refs[n_in : n_in + n_out]
        spare = list(refs[n_in + n_out : n_in + n_out + len(holds)])
        in_sems, out_sems, *rest = refs[n_in + n_out + len(holds) :]
        in_holds = [spare.pop(0) if space is HBM else None for _, space, _ in ins]
        out_holds = [spare.pop(0) if space is HBM else None for _, _, space in outs]
        blocks = Blocks(in_refs, in_holds, out_refs, out_holds, in_sems, out_sems)
        kernel(blocks, *rest)
        for copy in blocks.leaving:
            copy.wait()

    return pl.pallas_call(
        run,
        out_shape=[jax.ShapeDtypeStruct(shape, kind) for shape, kind, _ in outs],
        in_specs=[pl.BlockSpec(memory_space=space) for _, space, _ in ins],
        out_specs=[pl.BlockSpec(memory_space=space) for _, _, space in outs],
        scratch_shapes=holds
        + [pltpu.SemaphoreType.DMA((n_in,)), pltpu.SemaphoreType.DMA((n_out,))]
        + scratch,
        compiler_params=pltpu.CompilerParams(vmem_limit_bytes=mib * 1024 * 1024),
        cost_estimate=pl.CostEstimate(flops=flops, bytes_accessed=4_000_000, transcendentals=0),
        name=name,
    )(*[array for array, _, _ in ins])


def exchange(quads, forward):
    n_lat, n_pair, n_core = (lax.axis_size(axis) for axis in ("lat", "pair", "core"))
    n_lon = n_pair * n_core
    by = -1 if forward else 1

    def moved(shard, over_lat, over_lon):
        pairs = []
        for row in range(n_lat):
            for col in range(n_lon):
                to = (row + by * over_lat) % n_lat * n_lon + (col + by * over_lon) % n_lon
                pairs.append((row * n_lon + col, to))
        return lax.ppermute(shard, ("lat", "pair", "core"), pairs)

    if forward:
        return (
            quads[3],
            moved(quads[2], 0, 1),
            moved(quads[1], 1, 0),
            moved(quads[0], 1, 1),
        )
    return (
        moved(quads[3], 1, 1),
        moved(quads[2], 1, 0),
        moved(quads[1], 0, 1),
        quads[0],
    )


def reduce_terms(own, other, returned, after, scale):
    n_lat, n_member = lax.axis_size("lat"), lax.axis_size("member")
    n_pair, n_core = lax.axis_size("pair"), lax.axis_size("core")
    rows = D // (n_pair * n_core)
    width = D // n_lat
    partner = lax.ppermute(other, "core", [(i, (i + 1) % n_core) for i in range(n_core)])
    (terms,) = call(
        weight_terms,
        [(own, HBM, None), (partner, HBM, None)],
        [((n_member * n_pair, rows, D), bf16, HBM)],
        [pltpu.SemaphoreType.DMA((2,))],
        3_000_000_000,
        "weight_terms",
        16,
    )
    terms, *_ = lax.optimization_barrier((terms, *returned))
    parts = lax.all_to_all(terms, ("member", "pair"), 0, 0, tiled=True)
    (plane_sum,) = call(
        sum_plane,
        [(parts, HBM, None), (after, pl.ANY, None)],
        [((n_member * n_lat, rows, -(-width // 128) * 128), bf16, HBM)],
        [],
        5_000_000,
        "sum_plane",
        16,
    )
    parts = lax.all_to_all(plane_sum, ("member", "lat"), 0, 0, tiled=True)
    (total,) = call(
        functools.partial(sum_lat, scale),
        [(parts, HBM, None)],
        [((2, rows, width), f32, HBM)],
        [],
        1_000_000,
        "sum_lat",
        8,
    )
    return total.transpose(0, 2, 1)


def body(fields, cotangent, qkv_weight, out_weight, norm_gain, bias_table, bias_index, region):
    order, window_order, at_line, at_col = constants()
    window_order = jnp.asarray(window_order, bf16)
    back_order = jnp.asarray(order.T, bf16)
    order = jnp.asarray(order, bf16)
    at_line, at_col = jnp.asarray(at_line, bf16), jnp.asarray(at_col, bf16)
    edge = (lax.axis_index("lat") == lax.axis_size("lat") - 1).astype(jnp.int32).reshape(1)
    n_pair, n_core = lax.axis_size("pair"), lax.axis_size("core")
    core = lax.axis_index("core")

    def qkv_parts(block):
        def part_of(part):
            return (D, D), lambda ref: ref.at[block, :, pl.ds(part * D, D)]

        return [(qkv_weight, HBM, part_of(part)) for part in range(3)]

    gather_scratch = [pltpu.VMEM((HEADS, 8, CHUNKS * 128), f32), pltpu.VMEM((HEADS, DEPTH, 128), f32)]
    hold = pltpu.VMEM((WIN, D), f32)
    mixed_scratch = pltpu.VMEM((WIN, D), bf16)
    back_scratch = [
        pltpu.VMEM((WIN, D), bf16),
        pltpu.VMEM((4, D, WIN), bf16),
        pltpu.VMEM((WIN, 3 * D), bf16),
    ]
    cells = (WIN_LAT * WIN_LON, LEVELS, D)
    table = bias_table.transpose(0, 1, 3, 2).reshape(2, HEADS, NREL)
    first = call(
        first_forward,
        [
            (window_order, HBM, None),
            (bias_index, HBM, None),
            (table, HBM, 0),
            (fields.transpose(0, 2, 3, 1, 4).reshape(cells), HBM, None),
            (order, HBM, None),
            (norm_gain, HBM, None),
            *qkv_parts(0),
            (out_weight, HBM, 0),
            (cotangent.transpose(0, 2, 3, 1, 4).reshape(cells), HBM, None),
        ],
        [((QUAD, 3 * D), bf16, HBM)] * 4
        + [
            ((WIN, 256), jnp.int32, HBM),
            ((WIN, D), bf16, HBM),
            ((WIN, 3 * D), bf16, HBM),
            ((HEADS, WIN, WIN), bf16, HBM),
        ],
        [pltpu.VMEM((HEADS, WIN, WIN), f32)] + gather_scratch + [hold, mixed_scratch],
        1_000_000_000,
        "first_forward",
    )
    wide, inputs, qkv_one, probs_one = first[4:]
    shifted = exchange(first[:4], True)
    (bias_two,) = call(
        second_bias,
        [
            (region.transpose(1, 0, 2), HBM, None),
            (edge, SMEM, None),
            (at_line, HBM, None),
            (at_col, HBM, None),
            (table, HBM, 1),
            (wide, HBM, None),
        ],
        [((HEADS, WIN, WIN), f32, HBM)],
        gather_scratch + [pltpu.VMEM((WIN, WIN), f32), pltpu.SemaphoreType.DMA((3,))],
        5_000_000_000,
        "second_bias",
    )
    second = call(
        functools.partial(second_block, D // (n_pair * n_core)),
        [(quad, HBM, None) for quad in shifted]
        + [
            (norm_gain, HBM, None),
            *qkv_parts(1),
            (bias_two, HBM, None),
            (out_weight, HBM, 1),
            (core.astype(jnp.int32).reshape(1), SMEM, None),
        ],
        [((QUAD, 2 * D), bf16, HBM)] * 4 + [((WIN, 3 * D), bf16, HBM)] * 2,
        [hold, mixed_scratch, pltpu.VMEM((WIN, 3 * D), bf16), pltpu.VMEM((HEADS, WIN, WIN), bf16)]
        + back_scratch,
        15_000_000_000,
        "second_block",
    )
    returned = exchange(second[:4], False)
    grad_fields, output = call(
        first_backward,
        [(quad, HBM, None) for quad in returned]
        + [
            (inputs, HBM, None),
            (qkv_one, HBM, None),
            (probs_one, HBM, None),
            (out_weight, HBM, 0),
            (norm_gain, HBM, None),
            (back_order, HBM, None),
        ]
        + qkv_parts(0),
        [(cells, bf16, HBM)] * 2,
        [hold] + back_scratch,
        9_000_000_000,
        "first_backward",
        61,
    )

    token_total = lax.axis_size("member") * lax.axis_size("lat") * n_pair * n_core * WIN
    scale = float(token_total) ** (-0.5)
    grad_out = reduce_terms(second[4], second[5], returned, grad_fields, scale)

    def whole(values):
        grid = values.reshape(1, WIN_LAT, WIN_LON, LEVELS, D)
        return grid.transpose(0, 3, 1, 2, 4)

    return whole(output), whole(grad_fields), grad_out


def solution(mesh):
    n_member, n_lat, n_lon = mesh.devices.shape
    split = mesh.devices.reshape(n_member, n_lat, n_lon // 2, 2)
    mesh = jax.sharding.Mesh(split, ("member", "lat", "pair", "core"))
    lon = ("pair", "core")
    grid = P("member", None, "lat", lon, None)
    placed = (grid, grid, P(), P(), P(), P(None, "lat", None, None), P(), P(None, "lat", lon))
    return jax.shard_map(
        body,
        mesh=mesh,
        in_specs=placed,
        out_specs=(grid, grid, P(None, "lat", lon)),
        check_vma=False,
    )
```

```python
import functools

import jax
import jax.numpy as jnp
import numpy as np
from jax import lax
from jax.experimental import pallas as pl
from jax.experimental.pallas import tpu as pltpu
from jax.sharding import PartitionSpec as P

LEVELS = 2
WIN_LAT = 6
WIN_LON = 12
HALF_LAT = WIN_LAT // 2
HALF_LON = WIN_LON // 2
WIN = LEVELS * WIN_LAT * WIN_LON
QUAD = WIN // 4
D = 768
HEADS = 24
HEAD_DIM = D // HEADS
GROUP = 128 // HEAD_DIM
GROUPS = HEADS // GROUP
NREL = 759
CHUNKS = 6
DEPTH = 24
TAIL = WIN - 128
SCALE = HEAD_DIM ** (-0.5)
EPS = 1e-05

bf16 = jnp.bfloat16
f32 = jnp.float32


def quad_order():
    token = np.arange(WIN)
    quad, inside = token // QUAD, token % QUAD
    level = inside // (HALF_LAT * HALF_LON)
    row = inside // HALF_LON % HALF_LAT + HALF_LAT * (quad // 2)
    col = inside % HALF_LON + HALF_LON * (quad % 2)
    stored = (row * WIN_LON + col) * LEVELS + level
    window = (level * WIN_LAT + row) * WIN_LON + col
    return row * LEVELS + level, col, stored, window


def constants():
    line, col, stored, window = quad_order()
    order = np.eye(WIN, dtype=np.float32)[stored]
    window_order = np.eye(WIN, dtype=np.float32)[window]
    at_line = np.eye(LEVELS * WIN_LAT, dtype=np.float32)[line]
    at_col = np.eye(WIN_LON, dtype=np.float32)[col]
    return order, window_order, at_line, at_col


def contract(left, right, dims):
    return lax.dot_general(left, right, ((dims[:1], dims[1:]), ((), ())), preferred_element_type=f32)


def mm(left, right):
    return contract(left, right, (1, 0))


def mm_t(left, right):
    return contract(left, right, (1, 1))


def eye(size):
    rows = lax.broadcasted_iota(jnp.int32, (size, size), 0)
    cols = lax.broadcasted_iota(jnp.int32, (size, size), 1)
    return (rows == cols).astype(f32).astype(bf16)


def head_masks():
    lane = lax.broadcasted_iota(jnp.int32, (1, 128), 1)
    masks = []
    for head in range(GROUP):
        inside = jnp.logical_and(lane >= head * HEAD_DIM, lane < (head + 1) * HEAD_DIM)
        masks.append(inside.astype(f32).astype(bf16))
    return masks


def layer_norm(values_f):
    centred = values_f - jnp.mean(values_f, axis=-1, keepdims=True)
    variance = jnp.mean(centred * centred, axis=-1, keepdims=True)
    inv_std = lax.rsqrt(variance + EPS)
    return centred * inv_std, inv_std


def place_index(index_ref, order, wide_ref):
    index_f = index_ref[...].astype(f32)
    high = jnp.floor(index_f * 0.125)
    low = index_f - high * 8.0
    parts = []
    for part in (high, low):
        half = mm(order, part.astype(bf16)).astype(bf16)
        parts.append(mm_t(half, order))
    moved = parts[0] * 8.0 + parts[1]
    wide_ref[:, :WIN] = (moved + 0.5).astype(jnp.int32)
    wide_ref[:, WIN:] = jnp.zeros((WIN, 256 - WIN), jnp.int32)
    lane = lax.broadcasted_iota(jnp.int32, (DEPTH, 128), 1)
    packed = jnp.zeros((DEPTH, 128), jnp.int32)
    for strip in range(WIN // DEPTH):
        piece = wide_ref[strip * DEPTH : (strip + 1) * DEPTH, 128:256]
        if strip:
            piece = pltpu.roll(piece, strip * TAIL, axis=1)
        inside = jnp.logical_and(lane >= strip * TAIL, lane < (strip + 1) * TAIL)
        packed = jnp.where(inside, piece, packed)
    wide_ref[:DEPTH, 128:256] = packed


def lane_gather(row, index):
    numbers = lax.GatherDimensionNumbers(
        offset_dims=(),
        collapsed_slice_dims=(1,),
        start_index_map=(1,),
        operand_batching_dims=(0,),
        start_indices_batching_dims=(0,),
    )
    mode = lax.GatherScatterMode.PROMISE_IN_BOUNDS
    return lax.gather(row, index[..., None], numbers, slice_sizes=(1, 1), mode=mode)


def gather_bias(wide_ref, table_ref, bias_ref, rows_ref, tail_ref, mask_ref, done=None):
    for head in range(HEADS):
        rows_ref[head, :, :NREL] = jnp.broadcast_to(table_ref[head : head + 1, :], (8, NREL))

    def look_up(index, store):
        low_part = jnp.bitwise_and(index, 127)
        high_part = jnp.right_shift(index, 7)
        for head in range(HEADS):
            found = jnp.zeros((8, 128), f32)
            for chunk in range(CHUNKS):
                row = rows_ref[head, :, chunk * 128 : (chunk + 1) * 128]
                found = jnp.where(high_part == chunk, lane_gather(row, low_part), found)
            store(head, found)

    def main_strip(strip, carry):
        lines = pl.ds(pl.multiple_of(strip * 8, 8), 8)
        mask = None if mask_ref is None else mask_ref[lines, :128]

        def store(head, found):
            bias_ref[head, lines, :128] = found if mask is None else found + mask

        look_up(wide_ref[lines, :128], store)
        return carry

    def tail_strip(strip, carry):
        lines = pl.ds(pl.multiple_of(strip * 8, 8), 8)

        def store(head, found):
            tail_ref[head, lines, :] = found

        look_up(wide_ref[lines, 128:256], store)
        return carry

    def unpack(head, carry):
        rest = tail_ref[head]
        for strip in range(WIN // DEPTH):
            lines = slice(strip * DEPTH, (strip + 1) * DEPTH)
            piece = rest if strip == 0 else pltpu.roll(rest, 128 - strip * TAIL, axis=1)
            piece = piece[:, :TAIL]
            if mask_ref is not None:
                piece = piece + mask_ref[lines, 128:WIN]
            bias_ref[head, lines, 128:WIN] = piece
        return carry

    lax.fori_loop(0, DEPTH // 8, tail_strip, 0, unroll=3)
    lax.fori_loop(0, HEADS, unpack, 0, unroll=4)
    for third in range(3):
        lax.fori_loop(third * 6, third * 6 + 6, main_strip, 0, unroll=6)
        if done is not None:
            done(third)


def project_qkv(hidden, w_parts, qkv_ref):
    for part in range(3):
        qkv_ref[:, part * D : (part + 1) * D] = mm(hidden, w_parts(part)[...]).astype(bf16)


def stack_heads(values, masks):
    return jnp.concatenate([values * mask for mask in masks], axis=0)


def merge_heads(stacked):
    lane = lax.broadcasted_iota(jnp.int32, (1, 128), 1)
    merged = stacked[:WIN]
    for head in range(1, GROUP):
        later = lane >= head * HEAD_DIM
        merged = jnp.where(later, stacked[head * WIN : (head + 1) * WIN], merged)
    return merged


def group_cols(group, part):
    return slice(part * D + group * 128, part * D + (group + 1) * 128)


def attend(qkv_ref, bias_ref, probs_ref, mixed_ref):
    masks = head_masks()
    ones = jnp.ones((WIN, 128), bf16)
    for group in range(GROUPS):
        heads = slice(group * GROUP, (group + 1) * GROUP)
        query = qkv_ref[:, group_cols(group, 0)]
        key = qkv_ref[:, group_cols(group, 1)]
        value = qkv_ref[:, group_cols(group, 2)]
        scores = mm_t(stack_heads(query, masks), key) * SCALE
        scores = scores + bias_ref[heads].reshape(GROUP * WIN, WIN)
        exponent = jnp.exp(scores - jnp.max(scores, axis=-1, keepdims=True)).astype(bf16)
        product = mm(exponent, jnp.concatenate([value, ones], axis=1))
        share = 1.0 / product[:, 128:]
        weights = exponent.astype(f32) * jnp.concatenate([share, share[:, : WIN - 128]], axis=1)
        probs_ref[heads] = weights.astype(bf16).reshape(GROUP, WIN, WIN)
        mixed = merge_heads(product[:, :128] * share)
        mixed_ref[:, group_cols(group, 0)] = mixed.astype(bf16)


def back_attend(grad, qkv_ref, probs_ref, mixed_ref, w_out_ref, grad_mixed_ref, turned_ref, rows_ref):
    masks = head_masks()
    unit = eye(256)
    small = eye(WIN)
    minus = -jnp.ones((WIN, 128), bf16)
    grad_mixed_ref[...] = mm_t(grad, w_out_ref[...]).astype(bf16)
    for part in range(3):
        cols = slice(part * 256, (part + 1) * 256)
        turned_ref[0, cols, :] = mm_t(unit, grad_mixed_ref[:, cols]).astype(bf16)
        turned_ref[1, cols, :] = mm_t(unit, qkv_ref[:, cols]).astype(bf16)
    for group in range(GROUPS):
        heads = slice(group * GROUP, (group + 1) * GROUP)
        cols = group_cols(group, 0)
        grad_mixed = grad_mixed_ref[:, cols]
        key = qkv_ref[:, group_cols(group, 1)]
        value = qkv_ref[:, group_cols(group, 2)]
        weights = probs_ref[heads].reshape(GROUP * WIN, WIN)
        probs = weights.astype(f32)
        left = stack_heads(grad_mixed, masks)
        if mixed_ref is None:
            grad_weights = mm_t(left, value)
            moved = grad_weights - jnp.sum(grad_weights * probs, axis=-1, keepdims=True)
        else:
            inner = grad_mixed.astype(f32) * mixed_ref[:, cols].astype(f32)
            left = jnp.concatenate([left, stack_heads(inner.astype(bf16), masks)], axis=1)
            moved = mm_t(left, jnp.concatenate([value, minus], axis=1))
        grad_scores = (probs * moved * SCALE).astype(bf16)
        rows_ref[:, cols] = merge_heads(mm(grad_scores, key)).astype(bf16)
        for inner in range(GROUP):
            head = group * GROUP + inner
            lines = slice(head * HEAD_DIM, (head + 1) * HEAD_DIM)
            tokens = slice(inner * WIN, (inner + 1) * WIN)
            turned_ref[2, lines, :] = mm(turned_ref[1, lines, :], grad_scores[tokens]).astype(bf16)
            turned_ref[3, lines, :] = mm(turned_ref[0, lines, :], weights[tokens]).astype(bf16)
    for part in range(3):
        cols = slice(part * 256, (part + 1) * 256)
        for which in (1, 2):
            out = slice(which * D + part * 256, which * D + (part + 1) * 256)
            rows_ref[:, out] = mm_t(small, turned_ref[1 + which, cols, :]).astype(bf16)


def back_norm(grad_f, normed, inv_std, gain, rows_ref, w_parts):
    grad_hidden = jnp.zeros((WIN, D), f32)
    for part in range(3):
        grad_hidden += mm_t(rows_ref[:, part * D : (part + 1) * D], w_parts(part)[...])
    grad_normed = grad_hidden * gain
    mean_one = jnp.mean(grad_normed, axis=-1, keepdims=True)
    mean_two = jnp.mean(grad_normed * normed, axis=-1, keepdims=True)
    return grad_f + inv_std * (grad_normed - mean_one - normed * mean_two)


def put_quads(values_f, hold_ref, quad_refs, section):
    hold_ref[...] = values_f
    cols = slice(section * D, (section + 1) * D)
    for quad in range(4):
        quad_refs[quad][:, cols] = hold_ref[quad * QUAD : (quad + 1) * QUAD, :].astype(bf16)


def take_quads(quad_refs, hold_ref, section):
    cols = slice(section * D, (section + 1) * D)
    for quad in range(4):
        hold_ref[quad * QUAD : (quad + 1) * QUAD, :] = quad_refs[quad][:, cols].astype(f32)
    return hold_ref[...]


def first_forward(
    blocks, bias_ref, rows_ref, tail_ref, hold_ref, mixed_ref,
):
    quads = blocks.outs[:4]
    wide_ref, input_ref, qkv_ref, probs_ref = blocks.outs[4:]
    place_index(blocks.get(1), blocks.get(0)[...], wide_ref)
    blocks.put(4)
    order = blocks.get(4)[...]
    values_f = mm(order, blocks.get(3)[...].reshape(WIN, D))
    input_ref[...] = values_f.astype(bf16)
    blocks.put(5)
    normed, _ = layer_norm(values_f)
    hidden = (normed * blocks.get(5)[0:1, :]).astype(bf16)

    def project(third):
        cols = slice(third * D, (third + 1) * D)
        qkv_ref[:, cols] = mm(hidden, blocks.get(6 + third)[...]).astype(bf16)

    gather_bias(wide_ref, blocks.get(2), bias_ref, rows_ref, tail_ref, None, project)
    blocks.put(6)
    attend(qkv_ref, bias_ref, probs_ref, mixed_ref)
    blocks.put(7)
    put_quads(mm(order, blocks.get(10)[...].reshape(WIN, D)), hold_ref, quads, 1)
    mixed = mixed_ref[...]
    put_quads(mixed.astype(f32), hold_ref, quads, 2)
    result = input_ref[...].astype(f32) + mm(mixed, blocks.get(9)[...])
    put_quads(result, hold_ref, quads, 0)
    for quad in range(4):
        blocks.put(quad)


def pick_columns(core, width):
    rows = lax.broadcasted_iota(jnp.int32, (D // 2, D), 0)
    cols = lax.broadcasted_iota(jnp.int32, (D // 2, D), 1)
    part = jnp.floor((rows.astype(f32) + 0.5) * (1.0 / width)).astype(jnp.int32)
    return (cols == rows + width * (part + core)).astype(f32).astype(bf16)


def second_bias(width, blocks, rows_ref, tail_ref, mask_ref, sems):
    region_ref, edge_ref, bias_ref = blocks.get(0), blocks.get(1), blocks.outs[0]
    labels = jnp.concatenate([region_ref[row] for row in range(WIN_LAT)], axis=0)
    labels = labels.astype(f32) * 2.0 - 1.0
    at_line, at_col = blocks.get(2)[...], blocks.get(3)[...]
    column = jnp.sum(mm(at_line, labels.astype(bf16)) * at_col.astype(f32), axis=1, keepdims=True)
    signs = jnp.broadcast_to(column, (WIN, 128)).astype(bf16)
    same = mm_t(signs, signs) > 0.0
    half = WIN // 2
    rows = lax.broadcasted_iota(jnp.int32, (WIN, WIN), 0) >= half
    cols = lax.broadcasted_iota(jnp.int32, (WIN, WIN), 1) >= half
    across = jnp.logical_and(jnp.logical_xor(rows, cols), edge_ref[0] != 0)
    allowed = jnp.logical_and(same, jnp.logical_not(across))
    mask_ref[...] = jnp.where(allowed, 0.0, -jnp.inf)

    def done(third):
        rows = pl.ds(third * (WIN // 3), WIN // 3)
        blocks.put(0, (slice(None), rows), sems.at[third])

    core = blocks.get(6)[0]
    blocks.outs[1][0] = pick_columns(core, width)
    blocks.outs[1][1] = pick_columns(1 - core, width)
    blocks.put(1)
    gather_bias(blocks.get(5), blocks.get(4), bias_ref, rows_ref, tail_ref, mask_ref, done)


def second_block(
    blocks, hold_ref, mixed_ref, qkv_ref, probs_ref, grad_mixed_ref, turned_ref, grad_rows_ref,
    sems,
):
    leaving = blocks.outs[:4]
    own_ref, other_ref = blocks.outs[4:]
    arrived = [blocks.get(quad) for quad in range(4)]
    values_f = take_quads(arrived, hold_ref, 0)
    normed, inv_std = layer_norm(values_f)
    gain = blocks.get(4)[1:2, :]
    hidden = (normed * gain).astype(bf16)

    def w_parts(part):
        return blocks.get(5 + part)

    project_qkv(hidden, w_parts, qkv_ref)
    attend(qkv_ref, blocks.get(8), probs_ref, mixed_ref)
    w_out_ref = blocks.get(9)
    result = values_f + mm(mixed_ref[...], w_out_ref[...])
    put_quads(result, hold_ref, leaving, 1)
    for quad in range(4):
        blocks.put(quad, (slice(None), pl.ds(D, D)), sems.at[quad])
    grad_f = take_quads(arrived, hold_ref, 1)
    grad = grad_f.astype(bf16)
    first_mixed = take_quads(arrived, hold_ref, 2).astype(bf16)
    half = D // 2
    own, other = blocks.get(10)[0], blocks.get(10)[1]
    for ref, pick in ((own_ref, own), (other_ref, other)):
        ref[:, :D] = first_mixed
        ref[:, D : 2 * D] = mixed_ref[...]
        ref[:, 2 * D + half :] = mm_t(grad, pick).astype(bf16)
    early = ((0, 2 * D), (2 * D + half, half))
    for place in (4, 5):
        for part, (start, size) in enumerate(early):
            blocks.put(place, (slice(None), pl.ds(start, size)), sems.at[2 * place - 4 + part])
    back_attend(
        grad, qkv_ref, probs_ref, mixed_ref, w_out_ref, grad_mixed_ref, turned_ref, grad_rows_ref
    )
    grad_input = back_norm(grad_f, normed, inv_std, gain, grad_rows_ref, w_parts)
    first_grad = grad_input.astype(bf16)
    other_ref[:, 2 * D : 2 * D + half] = mm_t(first_grad, other).astype(bf16)
    late = (slice(None), pl.ds(2 * D, half))
    blocks.put(5, late)
    put_quads(grad_input, hold_ref, leaving, 0)
    for quad in range(4):
        blocks.put(quad, (slice(None), pl.ds(0, D)))
    own_ref[:, 2 * D : 2 * D + half] = mm_t(first_grad, own).astype(bf16)
    blocks.put(4, late)


def weight_terms(blocks, sems):
    terms_ref = blocks.outs[0]
    n_parts, rows, _ = terms_ref.shape
    n_parts //= 2
    half = n_parts * rows
    unit = eye(half)
    packs = (blocks.get(0), blocks.get(1))
    for block in range(2):
        cols = slice(2 * D + block * half, 2 * D + (block + 1) * half)
        total = jnp.zeros((half, D), f32)
        for pack in packs:
            turned = mm_t(unit, pack[:, cols]).astype(bf16)
            total += mm(turned, pack[:, block * D : (block + 1) * D])
        for part in range(n_parts):
            piece = total[part * rows : (part + 1) * rows, :].astype(bf16)
            terms_ref[block * n_parts + part] = piece
        blocks.put(0, pl.ds(block * n_parts, n_parts), sems.at[block])


def sum_plane(blocks):
    parts_ref, out_ref = blocks.get(0), blocks.outs[0]
    total = parts_ref[0].astype(f32)
    for part in range(1, parts_ref.shape[0]):
        total += parts_ref[part].astype(f32)
    copies = 2
    places = out_ref.shape[0] // copies
    width = D // places
    for place in range(places):
        piece = total[:, place * width : (place + 1) * width].astype(bf16)
        for copy in range(copies):
            out_ref[copy * places + place, :, :width] = piece
    blocks.put(0)


def sum_lat(scale, blocks):
    parts_ref, out_ref = blocks.get(0), blocks.outs[0]
    width = out_ref.shape[2]
    count = parts_ref.shape[0] // 2
    for block in range(2):
        total = parts_ref[block * count].astype(f32)
        for part in range(1, count):
            total += parts_ref[block * count + part].astype(f32)
        out_ref[block] = total[:, :width] * scale
    blocks.put(0)


def first_backward(blocks, hold_ref, grad_mixed_ref, turned_ref, grad_rows_ref):
    grad_fields_ref, output_ref = blocks.outs
    normed, inv_std = layer_norm(blocks.get(4)[...].astype(f32))
    arrived = [blocks.get(quad) for quad in range(4)]
    grad_f = take_quads(arrived, hold_ref, 0)
    qkv_ref, probs_ref, w_out_ref = blocks.get(5), blocks.get(6), blocks.get(7)
    back_attend(
        grad_f.astype(bf16), qkv_ref, probs_ref, None, w_out_ref, grad_mixed_ref, turned_ref,
        grad_rows_ref,
    )
    gain = blocks.get(8)[0:1, :]
    grad_input = back_norm(
        grad_f, normed, inv_std, gain, grad_rows_ref, lambda part: blocks.get(10 + part)
    )
    back_order = blocks.get(9)[...]
    shape = grad_fields_ref.shape
    grad_input = mm(back_order, grad_input.astype(bf16))
    grad_fields_ref[...] = grad_input.astype(bf16).reshape(shape)
    blocks.put(0)
    result = mm(back_order, take_quads(arrived, hold_ref, 1).astype(bf16))
    output_ref[...] = result.astype(bf16).reshape(shape)
    blocks.put(1)


class Blocks:
    def __init__(self, in_refs, in_holds, out_refs, out_holds, in_sems, out_sems):
        self.ins, self.outs, self.waiting, self.leaving = [], [], {}, []
        self.out_refs, self.out_sems = out_refs, out_sems
        for place, (ref, hold) in enumerate(zip(in_refs, in_holds)):
            if hold is not None:
                copy = pltpu.make_async_copy(ref, hold, in_sems.at[place])
                copy.start()
                self.waiting[place] = copy
            self.ins.append(ref if hold is None else hold)
        for ref, hold in zip(out_refs, out_holds):
            self.outs.append(ref if hold is None else hold)

    def get(self, place):
        if place in self.waiting:
            self.waiting.pop(place).wait()
        return self.ins[place]

    def put(self, place, part=None, sem=None):
        source, target = self.outs[place], self.out_refs[place]
        if part is not None:
            source, target = source.at[part], target.at[part]
        sem = self.out_sems.at[place] if sem is None else sem
        copy = pltpu.make_async_copy(source, target, sem)
        copy.start()
        self.leaving.append(copy)


HBM, SMEM = pltpu.HBM, pltpu.SMEM


def call(kernel, ins, outs, scratch, flops, name, mib=63):
    holds = []
    for array, space, index in ins:
        if space is HBM:
            shape = array.shape
            if index is not None:
                shape = array.shape[1:] if isinstance(index, int) else index[0]
            holds.append(pltpu.VMEM(shape, array.dtype))
    for shape, kind, space in outs:
        if space is HBM:
            holds.append(pltpu.VMEM(shape, kind))
    n_in, n_out = len(ins), len(outs)

    def run(*refs):
        in_refs = []
        for ref, (_, _, index) in zip(refs, ins):
            if index is not None:
                ref = ref.at[index] if isinstance(index, int) else index[1](ref)
            in_refs.append(ref)
        out_refs = refs[n_in : n_in + n_out]
        spare = list(refs[n_in + n_out : n_in + n_out + len(holds)])
        in_sems, out_sems, *rest = refs[n_in + n_out + len(holds) :]
        in_holds = [spare.pop(0) if space is HBM else None for _, space, _ in ins]
        out_holds = [spare.pop(0) if space is HBM else None for _, _, space in outs]
        blocks = Blocks(in_refs, in_holds, out_refs, out_holds, in_sems, out_sems)
        kernel(blocks, *rest)
        for copy in blocks.leaving:
            copy.wait()

    return pl.pallas_call(
        run,
        out_shape=[jax.ShapeDtypeStruct(shape, kind) for shape, kind, _ in outs],
        in_specs=[pl.BlockSpec(memory_space=space) for _, space, _ in ins],
        out_specs=[pl.BlockSpec(memory_space=space) for _, _, space in outs],
        scratch_shapes=holds
        + [pltpu.SemaphoreType.DMA((n_in,)), pltpu.SemaphoreType.DMA((n_out,))]
        + scratch,
        compiler_params=pltpu.CompilerParams(vmem_limit_bytes=mib * 1024 * 1024),
        cost_estimate=pl.CostEstimate(flops=flops, bytes_accessed=4_000_000, transcendentals=0),
        name=name,
    )(*[array for array, _, _ in ins])


def exchange(quads, forward):
    n_lat, n_pair, n_core = (lax.axis_size(axis) for axis in ("lat", "pair", "core"))
    n_lon = n_pair * n_core
    by = -1 if forward else 1

    def moved(shard, over_lat, over_lon):
        pairs = []
        for row in range(n_lat):
            for col in range(n_lon):
                to = (row + by * over_lat) % n_lat * n_lon + (col + by * over_lon) % n_lon
                pairs.append((row * n_lon + col, to))
        return lax.ppermute(shard, ("lat", "pair", "core"), pairs)

    if forward:
        return (
            quads[3],
            moved(quads[2], 0, 1),
            moved(quads[1], 1, 0),
            moved(quads[0], 1, 1),
        )
    return (
        moved(quads[3], 1, 1),
        moved(quads[2], 1, 0),
        moved(quads[1], 0, 1),
        quads[0],
    )


def reduce_terms(own, other, returned, after, scale):
    n_lat, n_member = lax.axis_size("lat"), lax.axis_size("member")
    n_pair, n_core = lax.axis_size("pair"), lax.axis_size("core")
    rows = D // (n_pair * n_core)
    width = D // n_lat
    partner = lax.ppermute(other, "core", [(i, (i + 1) % n_core) for i in range(n_core)])
    (terms,) = call(
        weight_terms,
        [(own, HBM, None), (partner, HBM, None)],
        [((n_member * n_pair, rows, D), bf16, HBM)],
        [pltpu.SemaphoreType.DMA((2,))],
        3_000_000_000,
        "weight_terms",
        16,
    )
    terms, *_ = lax.optimization_barrier((terms, *returned))
    parts = lax.all_to_all(terms, ("member", "pair"), 0, 0, tiled=True)
    (plane_sum,) = call(
        sum_plane,
        [(parts, HBM, None), (after, pl.ANY, None)],
        [((n_member * n_lat, rows, -(-width // 128) * 128), bf16, HBM)],
        [],
        5_000_000,
        "sum_plane",
        16,
    )
    parts = lax.all_to_all(plane_sum, ("member", "lat"), 0, 0, tiled=True)
    (total,) = call(
        functools.partial(sum_lat, scale),
        [(parts, HBM, None)],
        [((2, rows, width), f32, HBM)],
        [],
        1_000_000,
        "sum_lat",
        8,
    )
    return total.transpose(0, 2, 1)


def body(fields, cotangent, qkv_weight, out_weight, norm_gain, bias_table, bias_index, region):
    order, window_order, at_line, at_col = constants()
    window_order = jnp.asarray(window_order, bf16)
    back_order = jnp.asarray(order.T, bf16)
    order = jnp.asarray(order, bf16)
    at_line, at_col = jnp.asarray(at_line, bf16), jnp.asarray(at_col, bf16)
    edge = (lax.axis_index("lat") == lax.axis_size("lat") - 1).astype(jnp.int32)
    n_pair, n_core = lax.axis_size("pair"), lax.axis_size("core")
    core = lax.axis_index("core").astype(jnp.int32)

    def qkv_parts(block):
        def part_of(part):
            return (D, D), lambda ref: ref.at[block, :, pl.ds(part * D, D)]

        return [(qkv_weight, HBM, part_of(part)) for part in range(3)]

    gather_scratch = [pltpu.VMEM((HEADS, 8, CHUNKS * 128), f32), pltpu.VMEM((HEADS, DEPTH, 128), f32)]
    hold = pltpu.VMEM((WIN, D), f32)
    mixed_scratch = pltpu.VMEM((WIN, D), bf16)
    back_scratch = [
        pltpu.VMEM((WIN, D), bf16),
        pltpu.VMEM((4, D, WIN), bf16),
        pltpu.VMEM((WIN, 3 * D), bf16),
    ]
    cells = (WIN_LAT * WIN_LON, LEVELS, D)
    table = bias_table.transpose(0, 1, 3, 2).reshape(2, HEADS, NREL)
    first = call(
        first_forward,
        [
            (window_order, HBM, None),
            (bias_index, HBM, None),
            (table, HBM, 0),
            (fields.transpose(0, 2, 3, 1, 4).reshape(cells), HBM, None),
            (order, HBM, None),
            (norm_gain, HBM, None),
            *qkv_parts(0),
            (out_weight, HBM, 0),
            (cotangent.transpose(0, 2, 3, 1, 4).reshape(cells), HBM, None),
        ],
        [((QUAD, 3 * D), bf16, HBM)] * 4
        + [
            ((WIN, 256), jnp.int32, HBM),
            ((WIN, D), bf16, HBM),
            ((WIN, 3 * D), bf16, HBM),
            ((HEADS, WIN, WIN), bf16, HBM),
        ],
        [pltpu.VMEM((HEADS, WIN, WIN), f32)] + gather_scratch + [hold, mixed_scratch],
        1_000_000_000,
        "first_forward",
    )
    wide, inputs, qkv_one, probs_one = first[4:]
    shifted = exchange(first[:4], True)
    bias_two, picks = call(
        functools.partial(second_bias, D // (n_pair * n_core)),
        [
            (region.transpose(1, 0, 2), HBM, None),
            (edge.reshape(1), SMEM, None),
            (at_line, HBM, None),
            (at_col, HBM, None),
            (table, HBM, 1),
            (wide, HBM, None),
            (core.reshape(1), SMEM, None),
        ],
        [((HEADS, WIN, WIN), f32, HBM), ((2, D // 2, D), bf16, HBM)],
        gather_scratch + [pltpu.VMEM((WIN, WIN), f32), pltpu.SemaphoreType.DMA((3,))],
        5_000_000_000,
        "second_bias",
    )
    second = call(
        second_block,
        [(quad, HBM, None) for quad in shifted]
        + [
            (norm_gain, HBM, None),
            *qkv_parts(1),
            (bias_two, HBM, None),
            (out_weight, HBM, 1),
            (picks, HBM, None),
        ],
        [((QUAD, 2 * D), bf16, HBM)] * 4 + [((WIN, 3 * D), bf16, HBM)] * 2,
        [hold, mixed_scratch, pltpu.VMEM((WIN, 3 * D), bf16), pltpu.VMEM((HEADS, WIN, WIN), bf16)]
        + back_scratch
        + [pltpu.SemaphoreType.DMA((8,))],
        15_000_000_000,
        "second_block",
    )
    returned = exchange(second[:4], False)
    grad_fields, output = call(
        first_backward,
        [(quad, HBM, None) for quad in returned]
        + [
            (inputs, HBM, None),
            (qkv_one, HBM, None),
            (probs_one, HBM, None),
            (out_weight, HBM, 0),
            (norm_gain, HBM, None),
            (back_order, HBM, None),
        ]
        + qkv_parts(0),
        [(cells, bf16, HBM)] * 2,
        [hold] + back_scratch,
        9_000_000_000,
        "first_backward",
        61,
    )

    token_total = lax.axis_size("member") * lax.axis_size("lat") * n_pair * n_core * WIN
    scale = float(token_total) ** (-0.5)
    grad_out = reduce_terms(second[4], second[5], returned, grad_fields, scale)

    def whole(values):
        grid = values.reshape(1, WIN_LAT, WIN_LON, LEVELS, D)
        return grid.transpose(0, 3, 1, 2, 4)

    return whole(output), whole(grad_fields), grad_out


def solution(mesh):
    n_member, n_lat, n_lon = mesh.devices.shape
    split = mesh.devices.reshape(n_member, n_lat, n_lon // 2, 2)
    mesh = jax.sharding.Mesh(split, ("member", "lat", "pair", "core"))
    lon = ("pair", "core")
    grid = P("member", None, "lat", lon, None)
    placed = (grid, grid, P(), P(), P(), P(None, "lat", None, None), P(), P(None, "lat", lon))
    return jax.shard_map(
        body,
        mesh=mesh,
        in_specs=placed,
        out_specs=(grid, grid, P(None, "lat", lon)),
        check_vma=False,
    )
```

```python
import functools

import jax
import jax.numpy as jnp
import numpy as np
from jax import lax
from jax.experimental import pallas as pl
from jax.experimental.pallas import tpu as pltpu
from jax.sharding import PartitionSpec as P

LEVELS = 2
WIN_LAT = 6
WIN_LON = 12
HALF_LAT = WIN_LAT // 2
HALF_LON = WIN_LON // 2
WIN = LEVELS * WIN_LAT * WIN_LON
QUAD = WIN // 4
D = 768
HEADS = 24
HEAD_DIM = D // HEADS
GROUP = 128 // HEAD_DIM
GROUPS = HEADS // GROUP
NREL = 759
CHUNKS = 6
DEPTH = 24
TAIL = WIN - 128
SCALE = HEAD_DIM ** (-0.5)
EPS = 1e-05

bf16 = jnp.bfloat16
f32 = jnp.float32


def quad_order():
    token = np.arange(WIN)
    quad, inside = token // QUAD, token % QUAD
    level = inside // (HALF_LAT * HALF_LON)
    row = inside // HALF_LON % HALF_LAT + HALF_LAT * (quad // 2)
    col = inside % HALF_LON + HALF_LON * (quad % 2)
    stored = (row * WIN_LON + col) * LEVELS + level
    window = (level * WIN_LAT + row) * WIN_LON + col
    return row * LEVELS + level, col, stored, window


def constants():
    line, col, stored, window = quad_order()
    order = np.eye(WIN, dtype=np.float32)[stored]
    window_order = np.eye(WIN, dtype=np.float32)[window]
    at_line = np.eye(LEVELS * WIN_LAT, dtype=np.float32)[line]
    at_col = np.eye(WIN_LON, dtype=np.float32)[col]
    return order, window_order, at_line, at_col


def contract(left, right, dims):
    return lax.dot_general(left, right, ((dims[:1], dims[1:]), ((), ())), preferred_element_type=f32)


def mm(left, right):
    return contract(left, right, (1, 0))


def mm_t(left, right):
    return contract(left, right, (1, 1))


def eye(size):
    rows = lax.broadcasted_iota(jnp.int32, (size, size), 0)
    cols = lax.broadcasted_iota(jnp.int32, (size, size), 1)
    return (rows == cols).astype(f32).astype(bf16)


def head_masks():
    lane = lax.broadcasted_iota(jnp.int32, (1, 128), 1)
    masks = []
    for head in range(GROUP):
        inside = jnp.logical_and(lane >= head * HEAD_DIM, lane < (head + 1) * HEAD_DIM)
        masks.append(inside.astype(f32).astype(bf16))
    return masks


def layer_norm(values_f):
    centred = values_f - jnp.mean(values_f, axis=-1, keepdims=True)
    variance = jnp.mean(centred * centred, axis=-1, keepdims=True)
    inv_std = lax.rsqrt(variance + EPS)
    return centred * inv_std, inv_std


def place_index(index_ref, order, wide_ref):
    index_f = index_ref[...].astype(f32)
    high = jnp.floor(index_f * 0.125)
    low = index_f - high * 8.0
    parts = []
    for part in (high, low):
        half = mm(order, part.astype(bf16)).astype(bf16)
        parts.append(mm_t(half, order))
    moved = parts[0] * 8.0 + parts[1]
    wide_ref[:, :WIN] = (moved + 0.5).astype(jnp.int32)
    wide_ref[:, WIN:] = jnp.zeros((WIN, 256 - WIN), jnp.int32)
    lane = lax.broadcasted_iota(jnp.int32, (DEPTH, 128), 1)
    packed = jnp.zeros((DEPTH, 128), jnp.int32)
    for strip in range(WIN // DEPTH):
        piece = wide_ref[strip * DEPTH : (strip + 1) * DEPTH, 128:256]
        if strip:
            piece = pltpu.roll(piece, strip * TAIL, axis=1)
        inside = jnp.logical_and(lane >= strip * TAIL, lane < (strip + 1) * TAIL)
        packed = jnp.where(inside, piece, packed)
    wide_ref[:DEPTH, 128:256] = packed


def lane_gather(row, index):
    numbers = lax.GatherDimensionNumbers(
        offset_dims=(),
        collapsed_slice_dims=(1,),
        start_index_map=(1,),
        operand_batching_dims=(0,),
        start_indices_batching_dims=(0,),
    )
    mode = lax.GatherScatterMode.PROMISE_IN_BOUNDS
    return lax.gather(row, index[..., None], numbers, slice_sizes=(1, 1), mode=mode)


def gather_bias(wide_ref, table_ref, bias_ref, rows_ref, tail_ref, mask_ref, done=None):
    for head in range(HEADS):
        rows_ref[head, :, :NREL] = jnp.broadcast_to(table_ref[head : head + 1, :], (8, NREL))

    def look_up(index, store):
        low_part = jnp.bitwise_and(index, 127)
        high_part = jnp.right_shift(index, 7)
        for head in range(HEADS):
            found = jnp.zeros((8, 128), f32)
            for chunk in range(CHUNKS):
                row = rows_ref[head, :, chunk * 128 : (chunk + 1) * 128]
                found = jnp.where(high_part == chunk, lane_gather(row, low_part), found)
            store(head, found)

    def main_strip(strip, carry):
        lines = pl.ds(pl.multiple_of(strip * 8, 8), 8)
        mask = None if mask_ref is None else mask_ref[lines, :128]

        def store(head, found):
            bias_ref[head, lines, :128] = found if mask is None else found + mask

        look_up(wide_ref[lines, :128], store)
        return carry

    def tail_strip(strip, carry):
        lines = pl.ds(pl.multiple_of(strip * 8, 8), 8)

        def store(head, found):
            tail_ref[head, lines, :] = found

        look_up(wide_ref[lines, 128:256], store)
        return carry

    def unpack(head, carry):
        rest = tail_ref[head]
        for strip in range(WIN // DEPTH):
            lines = slice(strip * DEPTH, (strip + 1) * DEPTH)
            piece = rest if strip == 0 else pltpu.roll(rest, 128 - strip * TAIL, axis=1)
            piece = piece[:, :TAIL]
            if mask_ref is not None:
                piece = piece + mask_ref[lines, 128:WIN]
            bias_ref[head, lines, 128:WIN] = piece
        return carry

    lax.fori_loop(0, DEPTH // 8, tail_strip, 0, unroll=3)
    lax.fori_loop(0, HEADS, unpack, 0, unroll=4)
    for third in range(3):
        lax.fori_loop(third * 6, third * 6 + 6, main_strip, 0, unroll=6)
        if done is not None:
            done(third)


def project_qkv(hidden, w_parts, qkv_ref):
    for part in range(3):
        qkv_ref[:, part * D : (part + 1) * D] = mm(hidden, w_parts(part)[...]).astype(bf16)


def stack_heads(values, masks):
    return jnp.concatenate([values * mask for mask in masks], axis=0)


def merge_heads(stacked):
    lane = lax.broadcasted_iota(jnp.int32, (1, 128), 1)
    merged = stacked[:WIN]
    for head in range(1, GROUP):
        later = lane >= head * HEAD_DIM
        merged = jnp.where(later, stacked[head * WIN : (head + 1) * WIN], merged)
    return merged


def group_cols(group, part):
    return slice(part * D + group * 128, part * D + (group + 1) * 128)


def attend(qkv_ref, bias_ref, probs_ref, mixed_ref, beside=None):
    masks = head_masks()
    ones = jnp.ones((WIN, 128), bf16)
    for group in range(GROUPS):
        heads = slice(group * GROUP, (group + 1) * GROUP)
        query = qkv_ref[:, group_cols(group, 0)]
        key = qkv_ref[:, group_cols(group, 1)]
        value = qkv_ref[:, group_cols(group, 2)]
        scores = mm_t(stack_heads(query, masks), key) * SCALE
        scores = scores + bias_ref[heads].reshape(GROUP * WIN, WIN)
        exponent = jnp.exp(scores - jnp.max(scores, axis=-1, keepdims=True)).astype(bf16)
        product = mm(exponent, jnp.concatenate([value, ones], axis=1))
        share = 1.0 / product[:, 128:]
        weights = exponent.astype(f32) * jnp.concatenate([share, share[:, : WIN - 128]], axis=1)
        probs_ref[heads] = weights.astype(bf16).reshape(GROUP, WIN, WIN)
        mixed = merge_heads(product[:, :128] * share)
        mixed_ref[:, group_cols(group, 0)] = mixed.astype(bf16)
        if beside is not None:
            beside(group)


def prepare_back(part, grad, qkv_ref, w_out_ref, grad_mixed_ref, turned_ref):
    unit = eye(256)
    cols = slice(part * 256, (part + 1) * 256)
    grad_mixed_ref[:, cols] = mm_t(grad, w_out_ref[cols, :]).astype(bf16)
    turned_ref[0, cols, :] = mm_t(unit, grad_mixed_ref[:, cols]).astype(bf16)
    turned_ref[1, cols, :] = mm_t(unit, qkv_ref[:, cols]).astype(bf16)


def back_attend(qkv_ref, probs_ref, mixed_ref, grad_mixed_ref, turned_ref, rows_ref, beside=None):
    masks = head_masks()
    small = eye(WIN)
    minus = -jnp.ones((WIN, 128), bf16)
    for group in range(GROUPS):
        heads = slice(group * GROUP, (group + 1) * GROUP)
        cols = group_cols(group, 0)
        grad_mixed = grad_mixed_ref[:, cols]
        key = qkv_ref[:, group_cols(group, 1)]
        value = qkv_ref[:, group_cols(group, 2)]
        weights = probs_ref[heads].reshape(GROUP * WIN, WIN)
        probs = weights.astype(f32)
        left = stack_heads(grad_mixed, masks)
        if mixed_ref is None:
            grad_weights = mm_t(left, value)
            moved = grad_weights - jnp.sum(grad_weights * probs, axis=-1, keepdims=True)
        else:
            inner = grad_mixed.astype(f32) * mixed_ref[:, cols].astype(f32)
            left = jnp.concatenate([left, stack_heads(inner.astype(bf16), masks)], axis=1)
            moved = mm_t(left, jnp.concatenate([value, minus], axis=1))
        grad_scores = (probs * moved * SCALE).astype(bf16)
        rows_ref[:, cols] = merge_heads(mm(grad_scores, key)).astype(bf16)
        for inner in range(GROUP):
            head = group * GROUP + inner
            lines = slice(head * HEAD_DIM, (head + 1) * HEAD_DIM)
            tokens = slice(inner * WIN, (inner + 1) * WIN)
            turned_ref[2, lines, :] = mm(turned_ref[1, lines, :], grad_scores[tokens]).astype(bf16)
            turned_ref[3, lines, :] = mm(turned_ref[0, lines, :], weights[tokens]).astype(bf16)
        if beside is not None:
            beside(group)
    for part in range(3):
        cols = slice(part * 256, (part + 1) * 256)
        for which in (1, 2):
            out = slice(which * D + part * 256, which * D + (part + 1) * 256)
            rows_ref[:, out] = mm_t(small, turned_ref[1 + which, cols, :]).astype(bf16)


def back_norm(grad_f, normed, inv_std, gain, rows_ref, w_parts):
    grad_hidden = jnp.zeros((WIN, D), f32)
    for part in range(3):
        grad_hidden += mm_t(rows_ref[:, part * D : (part + 1) * D], w_parts(part)[...])
    grad_normed = grad_hidden * gain
    mean_one = jnp.mean(grad_normed, axis=-1, keepdims=True)
    mean_two = jnp.mean(grad_normed * normed, axis=-1, keepdims=True)
    return grad_f + inv_std * (grad_normed - mean_one - normed * mean_two)


def put_quads(values_f, hold_ref, quad_refs, section):
    hold_ref[...] = values_f
    cols = slice(section * D, (section + 1) * D)
    for quad in range(4):
        quad_refs[quad][:, cols] = hold_ref[quad * QUAD : (quad + 1) * QUAD, :].astype(bf16)


def take_quads(quad_refs, hold_ref, section):
    cols = slice(section * D, (section + 1) * D)
    for quad in range(4):
        hold_ref[quad * QUAD : (quad + 1) * QUAD, :] = quad_refs[quad][:, cols].astype(f32)
    return hold_ref[...]


def first_forward(
    blocks, bias_ref, rows_ref, tail_ref, hold_ref, mixed_ref,
):
    quads = blocks.outs[:4]
    wide_ref, input_ref, qkv_ref, probs_ref = blocks.outs[4:]
    place_index(blocks.get(1), blocks.get(0)[...], wide_ref)
    blocks.put(4)
    order = blocks.get(4)[...]
    values_f = mm(order, blocks.get(3)[...].reshape(WIN, D))
    input_ref[...] = values_f.astype(bf16)
    blocks.put(5)
    normed, _ = layer_norm(values_f)
    hidden = (normed * blocks.get(5)[0:1, :]).astype(bf16)

    def project(third):
        cols = slice(third * D, (third + 1) * D)
        qkv_ref[:, cols] = mm(hidden, blocks.get(6 + third)[...]).astype(bf16)

    gather_bias(wide_ref, blocks.get(2), bias_ref, rows_ref, tail_ref, None, project)
    blocks.put(6)
    attend(qkv_ref, bias_ref, probs_ref, mixed_ref)
    blocks.put(7)
    put_quads(mm(order, blocks.get(10)[...].reshape(WIN, D)), hold_ref, quads, 1)
    mixed = mixed_ref[...]
    put_quads(mixed.astype(f32), hold_ref, quads, 2)
    result = input_ref[...].astype(f32) + mm(mixed, blocks.get(9)[...])
    put_quads(result, hold_ref, quads, 0)
    for quad in range(4):
        blocks.put(quad)


def pick_columns(core, width):
    rows = lax.broadcasted_iota(jnp.int32, (D // 2, D), 0)
    cols = lax.broadcasted_iota(jnp.int32, (D // 2, D), 1)
    part = jnp.floor((rows.astype(f32) + 0.5) * (1.0 / width)).astype(jnp.int32)
    return (cols == rows + width * (part + core)).astype(f32).astype(bf16)


def second_bias(width, blocks, rows_ref, tail_ref, mask_ref):
    region_ref, edge_ref, bias_ref = blocks.get(0), blocks.get(1), blocks.outs[0]
    labels = jnp.concatenate([region_ref[row] for row in range(WIN_LAT)], axis=0)
    labels = labels.astype(f32) * 2.0 - 1.0
    at_line, at_col = blocks.get(2)[...], blocks.get(3)[...]
    column = jnp.sum(mm(at_line, labels.astype(bf16)) * at_col.astype(f32), axis=1, keepdims=True)
    signs = jnp.broadcast_to(column, (WIN, 128)).astype(bf16)
    same = mm_t(signs, signs) > 0.0
    half = WIN // 2
    rows = lax.broadcasted_iota(jnp.int32, (WIN, WIN), 0) >= half
    cols = lax.broadcasted_iota(jnp.int32, (WIN, WIN), 1) >= half
    across = jnp.logical_and(jnp.logical_xor(rows, cols), edge_ref[0] != 0)
    allowed = jnp.logical_and(same, jnp.logical_not(across))
    mask_ref[...] = jnp.where(allowed, 0.0, -jnp.inf)

    core = blocks.get(6)[0]
    blocks.outs[1][0] = pick_columns(core, width)
    blocks.outs[1][1] = pick_columns(1 - core, width)
    gather_bias(blocks.get(5), blocks.get(4), bias_ref, rows_ref, tail_ref, mask_ref)


def second_block(
    blocks, hold_ref, mixed_ref, qkv_ref, probs_ref, grad_mixed_ref, turned_ref, grad_rows_ref,
    sems,
):
    leaving = blocks.outs[:4]
    own_ref, other_ref = blocks.outs[4:]
    arrived = [blocks.get(quad) for quad in range(4)]
    values_f = take_quads(arrived, hold_ref, 0)
    normed, inv_std = layer_norm(values_f)
    gain = blocks.get(4)[1:2, :]
    hidden = (normed * gain).astype(bf16)

    def w_parts(part):
        return blocks.get(5).at[1, :, pl.ds(part * D, D)]

    project_qkv(hidden, w_parts, qkv_ref)
    grad_f = take_quads(arrived, hold_ref, 1)
    grad = grad_f.astype(bf16)
    first_mixed = take_quads(arrived, hold_ref, 2).astype(bf16)
    half = D // 2
    bias_ref, w_out_ref, picks_ref = blocks.get(7), blocks.get(6).at[1], blocks.get(8)

    def beside_forward(group):
        if group < 3:
            prepare_back(group, grad, qkv_ref, w_out_ref, grad_mixed_ref, turned_ref)
        elif group < 5:
            ref = (own_ref, other_ref)[group - 3]
            ref[:, :D] = first_mixed
            ref[:, 2 * D + half :] = mm_t(grad, picks_ref[group - 3]).astype(bf16)

    attend(qkv_ref, bias_ref, probs_ref, mixed_ref, beside_forward)
    early = ((0, 2 * D), (2 * D + half, half))
    for place, ref in ((4, own_ref), (5, other_ref)):
        ref[:, D : 2 * D] = mixed_ref[...]
        for part, (start, size) in enumerate(early):
            blocks.put(place, (slice(None), pl.ds(start, size)), sems.at[2 * place - 4 + part])

    def beside_back(group):
        if group < 3:
            cols = slice(group * 256, (group + 1) * 256)
            hold_ref[:, cols] = values_f[:, cols] + mm(mixed_ref[...], w_out_ref[:, cols])
        elif group == 3:
            for quad in range(4):
                rows = slice(quad * QUAD, (quad + 1) * QUAD)
                leaving[quad][:, D:] = hold_ref[rows, :].astype(bf16)
                blocks.put(quad, (slice(None), pl.ds(D, D)), sems.at[quad])

    back_attend(
        qkv_ref, probs_ref, mixed_ref, grad_mixed_ref, turned_ref, grad_rows_ref, beside_back
    )
    grad_input = back_norm(grad_f, normed, inv_std, gain, grad_rows_ref, w_parts)
    first_grad = grad_input.astype(bf16)
    other_ref[:, 2 * D : 2 * D + half] = mm_t(first_grad, picks_ref[1]).astype(bf16)
    late = (slice(None), pl.ds(2 * D, half))
    blocks.put(5, late)
    put_quads(grad_input, hold_ref, leaving, 0)
    for quad in range(4):
        blocks.put(quad, (slice(None), pl.ds(0, D)))
    own_ref[:, 2 * D : 2 * D + half] = mm_t(first_grad, picks_ref[0]).astype(bf16)
    blocks.put(4, late)


def weight_terms(blocks, sems):
    terms_ref = blocks.outs[0]
    n_parts, rows, _ = terms_ref.shape
    n_parts //= 2
    half = n_parts * rows
    unit = eye(half)
    packs = (blocks.get(0), blocks.get(1))
    for block in range(2):
        cols = slice(2 * D + block * half, 2 * D + (block + 1) * half)
        total = jnp.zeros((half, D), f32)
        for pack in packs:
            turned = mm_t(unit, pack[:, cols]).astype(bf16)
            total += mm(turned, pack[:, block * D : (block + 1) * D])
        for part in range(n_parts):
            piece = total[part * rows : (part + 1) * rows, :].astype(bf16)
            terms_ref[block * n_parts + part] = piece
        blocks.put(0, pl.ds(block * n_parts, n_parts), sems.at[block])


def sum_plane(blocks):
    parts_ref, out_ref = blocks.get(0), blocks.outs[0]
    total = parts_ref[0].astype(f32)
    for part in range(1, parts_ref.shape[0]):
        total += parts_ref[part].astype(f32)
    copies = 2
    places = out_ref.shape[0] // copies
    width = D // places
    for place in range(places):
        piece = total[:, place * width : (place + 1) * width].astype(bf16)
        for copy in range(copies):
            out_ref[copy * places + place, :, :width] = piece


def sum_lat(scale, blocks):
    parts_ref, out_ref = blocks.get(0), blocks.outs[0]
    width = out_ref.shape[2]
    count = parts_ref.shape[0] // 2
    for block in range(2):
        total = parts_ref[block * count].astype(f32)
        for part in range(1, count):
            total += parts_ref[block * count + part].astype(f32)
        out_ref[block] = total[:, :width] * scale
    blocks.put(0)


def first_backward(blocks, hold_ref, grad_mixed_ref, turned_ref, grad_rows_ref):
    grad_fields_ref, output_ref = blocks.outs
    normed, inv_std = layer_norm(blocks.get(4)[...].astype(f32))
    arrived = [blocks.get(quad) for quad in range(4)]
    grad_f = take_quads(arrived, hold_ref, 0)
    qkv_ref, probs_ref, w_out_ref = blocks.get(5), blocks.get(6), blocks.get(7)
    for part in range(3):
        prepare_back(part, grad_f.astype(bf16), qkv_ref, w_out_ref, grad_mixed_ref, turned_ref)
    back_attend(qkv_ref, probs_ref, None, grad_mixed_ref, turned_ref, grad_rows_ref)
    gain = blocks.get(8)[0:1, :]
    grad_input = back_norm(
        grad_f, normed, inv_std, gain, grad_rows_ref, lambda part: blocks.get(10 + part)
    )
    back_order = blocks.get(9)[...]
    shape = grad_fields_ref.shape
    grad_input = mm(back_order, grad_input.astype(bf16))
    grad_fields_ref[...] = grad_input.astype(bf16).reshape(shape)
    blocks.put(0)
    result = mm(back_order, take_quads(arrived, hold_ref, 1).astype(bf16))
    output_ref[...] = result.astype(bf16).reshape(shape)
    blocks.put(1)


class Blocks:
    def __init__(self, in_refs, in_holds, out_refs, out_holds, in_sems, out_sems):
        self.ins, self.outs, self.waiting, self.leaving = [], [], {}, []
        self.out_refs, self.out_sems = out_refs, out_sems
        for place, (ref, hold) in enumerate(zip(in_refs, in_holds)):
            if hold is not None:
                copy = pltpu.make_async_copy(ref, hold, in_sems.at[place])
                copy.start()
                self.waiting[place] = copy
            self.ins.append(ref if hold is None else hold)
        for ref, hold in zip(out_refs, out_holds):
            self.outs.append(ref if hold is None else hold)

    def get(self, place):
        if place in self.waiting:
            self.waiting.pop(place).wait()
        return self.ins[place]

    def put(self, place, part=None, sem=None):
        source, target = self.outs[place], self.out_refs[place]
        if part is not None:
            source, target = source.at[part], target.at[part]
        sem = self.out_sems.at[place] if sem is None else sem
        copy = pltpu.make_async_copy(source, target, sem)
        copy.start()
        self.leaving.append(copy)


HBM, SMEM = pltpu.HBM, pltpu.SMEM


def call(kernel, ins, outs, scratch, flops, name, mib=63):
    holds = []
    for array, space, index in ins:
        if space is HBM:
            shape = array.shape
            if index is not None:
                shape = array.shape[1:] if isinstance(index, int) else index[0]
            holds.append(pltpu.VMEM(shape, array.dtype))
    for shape, kind, space in outs:
        if space is HBM:
            holds.append(pltpu.VMEM(shape, kind))
    n_in, n_out = len(ins), len(outs)

    def run(*refs):
        in_refs = []
        for ref, (_, _, index) in zip(refs, ins):
            if index is not None:
                ref = ref.at[index] if isinstance(index, int) else index[1](ref)
            in_refs.append(ref)
        out_refs = refs[n_in : n_in + n_out]
        spare = list(refs[n_in + n_out : n_in + n_out + len(holds)])
        in_sems, out_sems, *rest = refs[n_in + n_out + len(holds) :]
        in_holds = [spare.pop(0) if space is HBM else None for _, space, _ in ins]
        out_holds = [spare.pop(0) if space is HBM else None for _, _, space in outs]
        blocks = Blocks(in_refs, in_holds, out_refs, out_holds, in_sems, out_sems)
        kernel(blocks, *rest)
        for copy in blocks.leaving:
            copy.wait()

    return pl.pallas_call(
        run,
        out_shape=[jax.ShapeDtypeStruct(shape, kind) for shape, kind, _ in outs],
        in_specs=[pl.BlockSpec(memory_space=space) for _, space, _ in ins],
        out_specs=[pl.BlockSpec(memory_space=space) for _, _, space in outs],
        scratch_shapes=holds
        + [pltpu.SemaphoreType.DMA((n_in,)), pltpu.SemaphoreType.DMA((n_out,))]
        + scratch,
        compiler_params=pltpu.CompilerParams(vmem_limit_bytes=mib * 1024 * 1024),
        cost_estimate=pl.CostEstimate(flops=flops, bytes_accessed=4_000_000, transcendentals=0),
        name=name,
    )(*[array for array, _, _ in ins])


def exchange(quads, forward):
    n_lat, n_pair, n_core = (lax.axis_size(axis) for axis in ("lat", "pair", "core"))
    n_lon = n_pair * n_core
    by = -1 if forward else 1

    def moved(shard, over_lat, over_lon):
        pairs = []
        for row in range(n_lat):
            for col in range(n_lon):
                to = (row + by * over_lat) % n_lat * n_lon + (col + by * over_lon) % n_lon
                pairs.append((row * n_lon + col, to))
        return lax.ppermute(shard, ("lat", "pair", "core"), pairs)

    if forward:
        return (
            quads[3],
            moved(quads[2], 0, 1),
            moved(quads[1], 1, 0),
            moved(quads[0], 1, 1),
        )
    return (
        moved(quads[3], 1, 1),
        moved(quads[2], 1, 0),
        moved(quads[1], 0, 1),
        quads[0],
    )


def reduce_terms(own, other, returned, after, scale):
    n_lat, n_member = lax.axis_size("lat"), lax.axis_size("member")
    n_pair, n_core = lax.axis_size("pair"), lax.axis_size("core")
    rows = D // (n_pair * n_core)
    width = D // n_lat
    partner = lax.ppermute(other, "core", [(i, (i + 1) % n_core) for i in range(n_core)])
    (terms,) = call(
        weight_terms,
        [(own, pltpu.VMEM, None), (partner, pltpu.VMEM, None)],
        [((n_member * n_pair, rows, D), bf16, HBM)],
        [pltpu.SemaphoreType.DMA((2,))],
        3_000_000_000,
        "weight_terms",
        16,
    )
    terms, *_ = lax.optimization_barrier((terms, *returned))
    parts = lax.all_to_all(terms, ("member", "pair"), 0, 0, tiled=True)
    (plane_sum,) = call(
        sum_plane,
        [(parts, pltpu.VMEM, None), (after, pl.ANY, None)],
        [((n_member * n_lat, rows, -(-width // 128) * 128), bf16, pltpu.VMEM)],
        [],
        5_000_000,
        "sum_plane",
        16,
    )
    parts = lax.all_to_all(plane_sum, ("member", "lat"), 0, 0, tiled=True)
    (total,) = call(
        functools.partial(sum_lat, scale),
        [(parts, pltpu.VMEM, None)],
        [((2, rows, width), f32, HBM)],
        [],
        1_000_000,
        "sum_lat",
        8,
    )
    return total.transpose(0, 2, 1)


def body(fields, cotangent, qkv_weight, out_weight, norm_gain, bias_table, bias_index, region):
    order, window_order, at_line, at_col = constants()
    window_order = jnp.asarray(window_order, bf16)
    back_order = jnp.asarray(order.T, bf16)
    order = jnp.asarray(order, bf16)
    at_line, at_col = jnp.asarray(at_line, bf16), jnp.asarray(at_col, bf16)
    edge = (lax.axis_index("lat") == lax.axis_size("lat") - 1).astype(jnp.int32)
    n_pair, n_core = lax.axis_size("pair"), lax.axis_size("core")
    core = lax.axis_index("core").astype(jnp.int32)

    def qkv_parts(block):
        def part_of(part):
            return (D, D), lambda ref: ref.at[block, :, pl.ds(part * D, D)]

        return [(qkv_weight, HBM, part_of(part)) for part in range(3)]

    gather_scratch = [pltpu.VMEM((HEADS, 8, CHUNKS * 128), f32), pltpu.VMEM((HEADS, DEPTH, 128), f32)]
    hold = pltpu.VMEM((WIN, D), f32)
    mixed_scratch = pltpu.VMEM((WIN, D), bf16)
    back_scratch = [
        pltpu.VMEM((WIN, D), bf16),
        pltpu.VMEM((4, D, WIN), bf16),
        pltpu.VMEM((WIN, 3 * D), bf16),
    ]
    cells = (WIN_LAT * WIN_LON, LEVELS, D)
    table = bias_table.transpose(0, 1, 3, 2).reshape(2, HEADS, NREL)
    first = call(
        first_forward,
        [
            (window_order, HBM, None),
            (bias_index, HBM, None),
            (table, HBM, 0),
            (fields.transpose(0, 2, 3, 1, 4).reshape(cells), HBM, None),
            (order, HBM, None),
            (norm_gain, HBM, None),
            *qkv_parts(0),
            (out_weight, HBM, 0),
            (cotangent.transpose(0, 2, 3, 1, 4).reshape(cells), HBM, None),
        ],
        [((QUAD, 3 * D), bf16, HBM)] * 4
        + [
            ((WIN, 256), jnp.int32, HBM),
            ((WIN, D), bf16, HBM),
            ((WIN, 3 * D), bf16, HBM),
            ((HEADS, WIN, WIN), bf16, HBM),
        ],
        [pltpu.VMEM((HEADS, WIN, WIN), f32)] + gather_scratch + [hold, mixed_scratch],
        1_000_000_000,
        "first_forward",
    )
    wide, inputs, qkv_one, probs_one = first[4:]
    shifted = exchange(first[:4], True)
    bias_two, picks = call(
        functools.partial(second_bias, D // (n_pair * n_core)),
        [
            (region.transpose(1, 0, 2), HBM, None),
            (edge.reshape(1), SMEM, None),
            (at_line, HBM, None),
            (at_col, HBM, None),
            (table, HBM, 1),
            (wide, HBM, None),
            (core.reshape(1), SMEM, None),
        ],
        [
            ((HEADS, WIN, WIN), f32, pltpu.VMEM),
            ((2, D // 2, D), bf16, pltpu.VMEM),
        ],
        gather_scratch + [pltpu.VMEM((WIN, WIN), f32)],
        5_000_000_000,
        "second_bias",
        12,
    )
    second = call(
        second_block,
        [(quad, pltpu.VMEM, None) for quad in shifted]
        + [
            (norm_gain, HBM, None),
            (qkv_weight, pltpu.VMEM, None),
            (out_weight, pltpu.VMEM, None),
            (bias_two, pltpu.VMEM, None),
            (picks, pltpu.VMEM, None),
        ],
        [((QUAD, 2 * D), bf16, HBM)] * 4 + [((WIN, 3 * D), bf16, HBM)] * 2,
        [hold, mixed_scratch, pltpu.VMEM((WIN, 3 * D), bf16), pltpu.VMEM((HEADS, WIN, WIN), bf16)]
        + back_scratch
        + [pltpu.SemaphoreType.DMA((8,))],
        15_000_000_000,
        "second_block",
        16,
    )
    returned = exchange(second[:4], False)
    grad_fields, output = call(
        first_backward,
        [(quad, HBM, None) for quad in returned]
        + [
            (inputs, HBM, None),
            (qkv_one, HBM, None),
            (probs_one, HBM, None),
            (out_weight, HBM, 0),
            (norm_gain, HBM, None),
            (back_order, HBM, None),
        ]
        + qkv_parts(0),
        [(cells, bf16, HBM)] * 2,
        [hold] + back_scratch,
        9_000_000_000,
        "first_backward",
        61,
    )

    token_total = lax.axis_size("member") * lax.axis_size("lat") * n_pair * n_core * WIN
    scale = float(token_total) ** (-0.5)
    grad_out = reduce_terms(second[4], second[5], returned, grad_fields, scale)

    def whole(values):
        grid = values.reshape(1, WIN_LAT, WIN_LON, LEVELS, D)
        return grid.transpose(0, 3, 1, 2, 4)

    return whole(output), whole(grad_fields), grad_out


def solution(mesh):
    n_member, n_lat, n_lon = mesh.devices.shape
    split = mesh.devices.reshape(n_member, n_lat, n_lon // 2, 2)
    mesh = jax.sharding.Mesh(split, ("member", "lat", "pair", "core"))
    lon = ("pair", "core")
    grid = P("member", None, "lat", lon, None)
    placed = (grid, grid, P(), P(), P(), P(None, "lat", None, None), P(), P(None, "lat", lon))
    return jax.shard_map(
        body,
        mesh=mesh,
        in_specs=placed,
        out_specs=(grid, grid, P(None, "lat", lon)),
        check_vma=False,
    )
```

```python
import functools

import jax
import jax.numpy as jnp
import numpy as np
from jax import lax
from jax.experimental import pallas as pl
from jax.experimental.pallas import tpu as pltpu
from jax.sharding import PartitionSpec as P

LEVELS = 2
WIN_LAT = 6
WIN_LON = 12
HALF_LAT = WIN_LAT // 2
HALF_LON = WIN_LON // 2
WIN = LEVELS * WIN_LAT * WIN_LON
QUAD = WIN // 4
D = 768
HEADS = 24
HEAD_DIM = D // HEADS
GROUP = 128 // HEAD_DIM
GROUPS = HEADS // GROUP
NREL = 759
CHUNKS = 6
DEPTH = 24
TAIL = WIN - 128
SCALE = HEAD_DIM ** (-0.5)
EPS = 1e-05

bf16 = jnp.bfloat16
f32 = jnp.float32


def quad_order():
    token = np.arange(WIN)
    quad, inside = token // QUAD, token % QUAD
    level = inside // (HALF_LAT * HALF_LON)
    row = inside // HALF_LON % HALF_LAT + HALF_LAT * (quad // 2)
    col = inside % HALF_LON + HALF_LON * (quad % 2)
    stored = (row * WIN_LON + col) * LEVELS + level
    window = (level * WIN_LAT + row) * WIN_LON + col
    return row * LEVELS + level, col, stored, window


def constants():
    line, col, stored, window = quad_order()
    order = np.eye(WIN, dtype=np.float32)[stored]
    window_order = np.eye(WIN, dtype=np.float32)[window]
    at_line = np.eye(LEVELS * WIN_LAT, dtype=np.float32)[line]
    at_col = np.eye(WIN_LON, dtype=np.float32)[col]
    return order, window_order, at_line, at_col


def contract(left, right, dims):
    return lax.dot_general(left, right, ((dims[:1], dims[1:]), ((), ())), preferred_element_type=f32)


def mm(left, right):
    return contract(left, right, (1, 0))


def mm_t(left, right):
    return contract(left, right, (1, 1))


def eye(size):
    rows = lax.broadcasted_iota(jnp.int32, (size, size), 0)
    cols = lax.broadcasted_iota(jnp.int32, (size, size), 1)
    return (rows == cols).astype(f32).astype(bf16)


def head_masks():
    lane = lax.broadcasted_iota(jnp.int32, (1, 128), 1)
    masks = []
    for head in range(GROUP):
        inside = jnp.logical_and(lane >= head * HEAD_DIM, lane < (head + 1) * HEAD_DIM)
        masks.append(inside.astype(f32).astype(bf16))
    return masks


def layer_norm(values_f):
    centred = values_f - jnp.mean(values_f, axis=-1, keepdims=True)
    variance = jnp.mean(centred * centred, axis=-1, keepdims=True)
    inv_std = lax.rsqrt(variance + EPS)
    return centred * inv_std, inv_std


def place_index(index_ref, order, wide_ref):
    index_f = index_ref[...].astype(f32)
    high = jnp.floor(index_f * 0.125)
    low = index_f - high * 8.0
    parts = []
    for part in (high, low):
        half = mm(order, part.astype(bf16)).astype(bf16)
        parts.append(mm_t(half, order))
    moved = parts[0] * 8.0 + parts[1]
    wide_ref[:, :WIN] = (moved + 0.5).astype(jnp.int32)
    wide_ref[:, WIN:] = jnp.zeros((WIN, 256 - WIN), jnp.int32)
    lane = lax.broadcasted_iota(jnp.int32, (DEPTH, 128), 1)
    packed = jnp.zeros((DEPTH, 128), jnp.int32)
    for strip in range(WIN // DEPTH):
        piece = wide_ref[strip * DEPTH : (strip + 1) * DEPTH, 128:256]
        if strip:
            piece = pltpu.roll(piece, strip * TAIL, axis=1)
        inside = jnp.logical_and(lane >= strip * TAIL, lane < (strip + 1) * TAIL)
        packed = jnp.where(inside, piece, packed)
    wide_ref[:DEPTH, 128:256] = packed


def lane_gather(row, index):
    numbers = lax.GatherDimensionNumbers(
        offset_dims=(),
        collapsed_slice_dims=(1,),
        start_index_map=(1,),
        operand_batching_dims=(0,),
        start_indices_batching_dims=(0,),
    )
    mode = lax.GatherScatterMode.PROMISE_IN_BOUNDS
    return lax.gather(row, index[..., None], numbers, slice_sizes=(1, 1), mode=mode)


def gather_bias(wide_ref, table_ref, bias_ref, rows_ref, tail_ref, mask_ref, done=None):
    for head in range(HEADS):
        rows_ref[head, :, :NREL] = jnp.broadcast_to(table_ref[head : head + 1, :], (8, NREL))

    def look_up(index, store):
        low_part = jnp.bitwise_and(index, 127)
        high_part = jnp.right_shift(index, 7)
        for head in range(HEADS):
            found = jnp.zeros((8, 128), f32)
            for chunk in range(CHUNKS):
                row = rows_ref[head, :, chunk * 128 : (chunk + 1) * 128]
                found = jnp.where(high_part == chunk, lane_gather(row, low_part), found)
            store(head, found)

    def main_strip(strip, carry):
        lines = pl.ds(pl.multiple_of(strip * 8, 8), 8)
        mask = None if mask_ref is None else mask_ref[lines, :128]

        def store(head, found):
            bias_ref[head, lines, :128] = found if mask is None else found + mask

        look_up(wide_ref[lines, :128], store)
        return carry

    def tail_strip(strip, carry):
        lines = pl.ds(pl.multiple_of(strip * 8, 8), 8)

        def store(head, found):
            tail_ref[head, lines, :] = found

        look_up(wide_ref[lines, 128:256], store)
        return carry

    def unpack(head, carry):
        rest = tail_ref[head]
        for strip in range(WIN // DEPTH):
            lines = slice(strip * DEPTH, (strip + 1) * DEPTH)
            piece = rest if strip == 0 else pltpu.roll(rest, 128 - strip * TAIL, axis=1)
            piece = piece[:, :TAIL]
            if mask_ref is not None:
                piece = piece + mask_ref[lines, 128:WIN]
            bias_ref[head, lines, 128:WIN] = piece
        return carry

    lax.fori_loop(0, DEPTH // 8, tail_strip, 0, unroll=3)
    lax.fori_loop(0, HEADS, unpack, 0, unroll=4)
    for third in range(3):
        lax.fori_loop(third * 6, third * 6 + 6, main_strip, 0, unroll=6)
        if done is not None:
            done(third)


def project_qkv(hidden, w_parts, qkv_ref):
    for part in range(3):
        qkv_ref[:, part * D : (part + 1) * D] = mm(hidden, w_parts(part)[...]).astype(bf16)


def stack_heads(values, masks):
    return jnp.concatenate([values * mask for mask in masks], axis=0)


def merge_heads(stacked):
    lane = lax.broadcasted_iota(jnp.int32, (1, 128), 1)
    merged = stacked[:WIN]
    for head in range(1, GROUP):
        later = lane >= head * HEAD_DIM
        merged = jnp.where(later, stacked[head * WIN : (head + 1) * WIN], merged)
    return merged


def group_cols(group, part):
    return slice(part * D + group * 128, part * D + (group + 1) * 128)


def attend(qkv_ref, bias_ref, probs_ref, mixed_ref, beside=None):
    masks = head_masks()
    ones = jnp.ones((WIN, 128), bf16)
    for group in range(GROUPS):
        heads = slice(group * GROUP, (group + 1) * GROUP)
        query = qkv_ref[:, group_cols(group, 0)]
        key = qkv_ref[:, group_cols(group, 1)]
        value = qkv_ref[:, group_cols(group, 2)]
        scores = mm_t(stack_heads(query, masks), key) * SCALE
        scores = scores + bias_ref[heads].reshape(GROUP * WIN, WIN)
        exponent = jnp.exp(scores - jnp.max(scores, axis=-1, keepdims=True)).astype(bf16)
        product = mm(exponent, jnp.concatenate([value, ones], axis=1))
        share = 1.0 / product[:, 128:]
        weights = exponent.astype(f32) * jnp.concatenate([share, share[:, : WIN - 128]], axis=1)
        probs_ref[heads] = weights.astype(bf16).reshape(GROUP, WIN, WIN)
        mixed = merge_heads(product[:, :128] * share)
        mixed_ref[:, group_cols(group, 0)] = mixed.astype(bf16)
        if beside is not None:
            beside(group)


def prepare_back(part, grad, qkv_ref, w_out_ref, grad_mixed_ref, turned_ref):
    unit = eye(256)
    cols = slice(part * 256, (part + 1) * 256)
    grad_mixed_ref[:, cols] = mm_t(grad, w_out_ref[cols, :]).astype(bf16)
    turned_ref[0, cols, :] = mm_t(unit, grad_mixed_ref[:, cols]).astype(bf16)
    turned_ref[1, cols, :] = mm_t(unit, qkv_ref[:, cols]).astype(bf16)


def back_attend(qkv_ref, probs_ref, mixed_ref, grad_mixed_ref, turned_ref, rows_ref, beside=None):
    masks = head_masks()
    small = eye(WIN)
    minus = -jnp.ones((WIN, 128), bf16)
    for group in range(GROUPS):
        heads = slice(group * GROUP, (group + 1) * GROUP)
        cols = group_cols(group, 0)
        grad_mixed = grad_mixed_ref[:, cols]
        key = qkv_ref[:, group_cols(group, 1)]
        value = qkv_ref[:, group_cols(group, 2)]
        weights = probs_ref[heads].reshape(GROUP * WIN, WIN)
        probs = weights.astype(f32)
        left = stack_heads(grad_mixed, masks)
        if mixed_ref is None:
            grad_weights = mm_t(left, value)
            moved = grad_weights - jnp.sum(grad_weights * probs, axis=-1, keepdims=True)
        else:
            inner = grad_mixed.astype(f32) * mixed_ref[:, cols].astype(f32)
            left = jnp.concatenate([left, stack_heads(inner.astype(bf16), masks)], axis=1)
            moved = mm_t(left, jnp.concatenate([value, minus], axis=1))
        grad_scores = (probs * moved * SCALE).astype(bf16)
        rows_ref[:, cols] = merge_heads(mm(grad_scores, key)).astype(bf16)
        for inner in range(GROUP):
            head = group * GROUP + inner
            lines = slice(head * HEAD_DIM, (head + 1) * HEAD_DIM)
            tokens = slice(inner * WIN, (inner + 1) * WIN)
            turned_ref[2, lines, :] = mm(turned_ref[1, lines, :], grad_scores[tokens]).astype(bf16)
            turned_ref[3, lines, :] = mm(turned_ref[0, lines, :], weights[tokens]).astype(bf16)
        if beside is not None:
            beside(group)
    for part in range(3):
        cols = slice(part * 256, (part + 1) * 256)
        for which in (1, 2):
            out = slice(which * D + part * 256, which * D + (part + 1) * 256)
            rows_ref[:, out] = mm_t(small, turned_ref[1 + which, cols, :]).astype(bf16)


def back_norm(grad_f, normed, inv_std, gain, rows_ref, w_parts):
    grad_hidden = jnp.zeros((WIN, D), f32)
    for part in range(3):
        grad_hidden += mm_t(rows_ref[:, part * D : (part + 1) * D], w_parts(part)[...])
    grad_normed = grad_hidden * gain
    mean_one = jnp.mean(grad_normed, axis=-1, keepdims=True)
    mean_two = jnp.mean(grad_normed * normed, axis=-1, keepdims=True)
    return grad_f + inv_std * (grad_normed - mean_one - normed * mean_two)


def put_quads(values_f, hold_ref, quad_refs, section):
    hold_ref[...] = values_f
    cols = slice(section * D, (section + 1) * D)
    for quad in range(4):
        quad_refs[quad][:, cols] = hold_ref[quad * QUAD : (quad + 1) * QUAD, :].astype(bf16)


def take_quads(quad_refs, hold_ref, section):
    cols = slice(section * D, (section + 1) * D)
    for quad in range(4):
        hold_ref[quad * QUAD : (quad + 1) * QUAD, :] = quad_refs[quad][:, cols].astype(f32)
    return hold_ref[...]


def first_forward(
    blocks, bias_ref, rows_ref, tail_ref, hold_ref, mixed_ref,
):
    quads = blocks.outs[:4]
    wide_ref, input_ref, qkv_ref, probs_ref = blocks.outs[4:]
    place_index(blocks.get(1), blocks.get(0)[...], wide_ref)
    blocks.put(4)
    order = blocks.get(4)[...]
    values_f = mm(order, blocks.get(3)[...].reshape(WIN, D))
    input_ref[...] = values_f.astype(bf16)
    blocks.put(5)
    normed, _ = layer_norm(values_f)
    hidden = (normed * blocks.get(5)[0:1, :]).astype(bf16)

    def project(third):
        cols = slice(third * D, (third + 1) * D)
        qkv_ref[:, cols] = mm(hidden, blocks.get(6 + third)[...]).astype(bf16)

    gather_bias(wide_ref, blocks.get(2), bias_ref, rows_ref, tail_ref, None, project)
    blocks.put(6)
    attend(qkv_ref, bias_ref, probs_ref, mixed_ref)
    blocks.put(7)
    put_quads(mm(order, blocks.get(10)[...].reshape(WIN, D)), hold_ref, quads, 1)
    mixed = mixed_ref[...]
    put_quads(mixed.astype(f32), hold_ref, quads, 2)
    result = input_ref[...].astype(f32) + mm(mixed, blocks.get(9)[...])
    put_quads(result, hold_ref, quads, 0)
    for quad in range(4):
        blocks.put(quad)


def pick_columns(core, width):
    rows = lax.broadcasted_iota(jnp.int32, (D // 2, D), 0)
    cols = lax.broadcasted_iota(jnp.int32, (D // 2, D), 1)
    part = jnp.floor((rows.astype(f32) + 0.5) * (1.0 / width)).astype(jnp.int32)
    return (cols == rows + width * (part + core)).astype(f32).astype(bf16)


def second_bias(width, blocks, rows_ref, tail_ref, mask_ref):
    region_ref, edge_ref, bias_ref = blocks.get(0), blocks.get(1), blocks.outs[0]
    labels = jnp.concatenate([region_ref[row] for row in range(WIN_LAT)], axis=0)
    labels = labels.astype(f32) * 2.0 - 1.0
    at_line, at_col = blocks.get(2)[...], blocks.get(3)[...]
    column = jnp.sum(mm(at_line, labels.astype(bf16)) * at_col.astype(f32), axis=1, keepdims=True)
    signs = jnp.broadcast_to(column, (WIN, 128)).astype(bf16)
    same = mm_t(signs, signs) > 0.0
    half = WIN // 2
    rows = lax.broadcasted_iota(jnp.int32, (WIN, WIN), 0) >= half
    cols = lax.broadcasted_iota(jnp.int32, (WIN, WIN), 1) >= half
    across = jnp.logical_and(jnp.logical_xor(rows, cols), edge_ref[0] != 0)
    allowed = jnp.logical_and(same, jnp.logical_not(across))
    mask_ref[...] = jnp.where(allowed, 0.0, -jnp.inf)

    core = blocks.get(6)[0]
    blocks.outs[1][0] = pick_columns(core, width)
    blocks.outs[1][1] = pick_columns(1 - core, width)
    gather_bias(blocks.get(5), blocks.get(4), bias_ref, rows_ref, tail_ref, mask_ref)


def second_block(
    blocks, hold_ref, mixed_ref, qkv_ref, probs_ref, grad_mixed_ref, turned_ref, grad_rows_ref,
    sems,
):
    leaving = blocks.outs[:4]
    own_ref, other_ref = blocks.outs[4:]
    arrived = [blocks.get(quad) for quad in range(4)]
    values_f = take_quads(arrived, hold_ref, 0)
    normed, inv_std = layer_norm(values_f)
    gain = blocks.get(4)[1:2, :]
    hidden = (normed * gain).astype(bf16)

    def w_parts(part):
        return blocks.get(5).at[1, :, pl.ds(part * D, D)]

    project_qkv(hidden, w_parts, qkv_ref)
    grad_f = take_quads(arrived, hold_ref, 1)
    grad = grad_f.astype(bf16)
    first_mixed = take_quads(arrived, hold_ref, 2).astype(bf16)
    half = D // 2
    bias_ref, w_out_ref, picks_ref = blocks.get(7), blocks.get(6).at[1], blocks.get(8)

    def beside_forward(group):
        if group < 3:
            prepare_back(group, grad, qkv_ref, w_out_ref, grad_mixed_ref, turned_ref)
        elif group < 5:
            ref = (own_ref, other_ref)[group - 3]
            ref[:, :D] = first_mixed
            ref[:, 2 * D + half :] = mm_t(grad, picks_ref[group - 3]).astype(bf16)

    attend(qkv_ref, bias_ref, probs_ref, mixed_ref, beside_forward)
    early = ((0, 2 * D), (2 * D + half, half))
    for place, ref in ((4, own_ref), (5, other_ref)):
        ref[:, D : 2 * D] = mixed_ref[...]
        for part, (start, size) in enumerate(early):
            blocks.put(place, (slice(None), pl.ds(start, size)), sems.at[2 * place - 4 + part])

    def beside_back(group):
        if group < 3:
            cols = slice(group * 256, (group + 1) * 256)
            hold_ref[:, cols] = values_f[:, cols] + mm(mixed_ref[...], w_out_ref[:, cols])
        elif group == 3:
            for quad in range(4):
                rows = slice(quad * QUAD, (quad + 1) * QUAD)
                leaving[quad][:, D:] = hold_ref[rows, :].astype(bf16)
                blocks.put(quad, (slice(None), pl.ds(D, D)), sems.at[quad])

    back_attend(
        qkv_ref, probs_ref, mixed_ref, grad_mixed_ref, turned_ref, grad_rows_ref, beside_back
    )
    grad_input = back_norm(grad_f, normed, inv_std, gain, grad_rows_ref, w_parts)
    first_grad = grad_input.astype(bf16)
    other_ref[:, 2 * D : 2 * D + half] = mm_t(first_grad, picks_ref[1]).astype(bf16)
    late = (slice(None), pl.ds(2 * D, half))
    blocks.put(5, late)
    put_quads(grad_input, hold_ref, leaving, 0)
    for quad in range(4):
        blocks.put(quad, (slice(None), pl.ds(0, D)))
    own_ref[:, 2 * D : 2 * D + half] = mm_t(first_grad, picks_ref[0]).astype(bf16)
    blocks.put(4, late)


def weight_terms(blocks, sems):
    terms_ref = blocks.outs[0]
    n_parts, rows, _ = terms_ref.shape
    n_parts //= 2
    half = n_parts * rows
    unit = eye(128)
    packs = (blocks.get(0), blocks.get(1))
    for block in range(2):
        cols = slice(2 * D + block * half, 2 * D + (block + 1) * half)
        total = jnp.zeros((half, D), f32)
        for pack in packs:
            turned = [
                mm_t(unit, pack[:, start : start + 128]).astype(bf16)
                for start in range(cols.start, cols.stop, 128)
            ]
            turned = jnp.concatenate(turned, axis=0)
            total += mm(turned, pack[:, block * D : (block + 1) * D])
        for part in range(n_parts):
            piece = total[part * rows : (part + 1) * rows, :].astype(bf16)
            terms_ref[block * n_parts + part] = piece
        blocks.put(0, pl.ds(block * n_parts, n_parts), sems.at[block])


def sum_plane(blocks):
    parts_ref, out_ref = blocks.get(0), blocks.outs[0]
    total = parts_ref[0].astype(f32)
    for part in range(1, parts_ref.shape[0]):
        total += parts_ref[part].astype(f32)
    copies = 2
    places = out_ref.shape[0] // copies
    width = D // places
    for place in range(places):
        piece = total[:, place * width : (place + 1) * width].astype(bf16)
        for copy in range(copies):
            out_ref[copy * places + place, :, :width] = piece


def sum_lat(scale, blocks):
    parts_ref, out_ref = blocks.get(0), blocks.outs[0]
    width = out_ref.shape[2]
    count = parts_ref.shape[0] // 2
    for block in range(2):
        total = parts_ref[block * count].astype(f32)
        for part in range(1, count):
            total += parts_ref[block * count + part].astype(f32)
        out_ref[block] = total[:, :width] * scale
    blocks.put(0)


def first_backward(blocks, hold_ref, grad_mixed_ref, turned_ref, grad_rows_ref):
    grad_fields_ref, output_ref = blocks.outs
    normed, inv_std = layer_norm(blocks.get(4)[...].astype(f32))
    arrived = [blocks.get(quad) for quad in range(4)]
    grad_f = take_quads(arrived, hold_ref, 0)
    qkv_ref, probs_ref, w_out_ref = blocks.get(5), blocks.get(6), blocks.get(7)
    for part in range(3):
        prepare_back(part, grad_f.astype(bf16), qkv_ref, w_out_ref, grad_mixed_ref, turned_ref)
    back_attend(qkv_ref, probs_ref, None, grad_mixed_ref, turned_ref, grad_rows_ref)
    gain = blocks.get(8)[0:1, :]
    grad_input = back_norm(
        grad_f, normed, inv_std, gain, grad_rows_ref, lambda part: blocks.get(10 + part)
    )
    back_order = blocks.get(9)[...]
    shape = grad_fields_ref.shape
    grad_input = mm(back_order, grad_input.astype(bf16))
    grad_fields_ref[...] = grad_input.astype(bf16).reshape(shape)
    blocks.put(0)
    result = mm(back_order, take_quads(arrived, hold_ref, 1).astype(bf16))
    output_ref[...] = result.astype(bf16).reshape(shape)
    blocks.put(1)


class Blocks:
    def __init__(self, in_refs, in_holds, out_refs, out_holds, in_sems, out_sems):
        self.ins, self.outs, self.waiting, self.leaving = [], [], {}, []
        self.out_refs, self.out_sems = out_refs, out_sems
        for place, (ref, hold) in enumerate(zip(in_refs, in_holds)):
            if hold is not None:
                copy = pltpu.make_async_copy(ref, hold, in_sems.at[place])
                copy.start()
                self.waiting[place] = copy
            self.ins.append(ref if hold is None else hold)
        for ref, hold in zip(out_refs, out_holds):
            self.outs.append(ref if hold is None else hold)

    def get(self, place):
        if place in self.waiting:
            self.waiting.pop(place).wait()
        return self.ins[place]

    def put(self, place, part=None, sem=None):
        source, target = self.outs[place], self.out_refs[place]
        if part is not None:
            source, target = source.at[part], target.at[part]
        sem = self.out_sems.at[place] if sem is None else sem
        copy = pltpu.make_async_copy(source, target, sem)
        copy.start()
        self.leaving.append(copy)


HBM, SMEM = pltpu.HBM, pltpu.SMEM


def call(kernel, ins, outs, scratch, flops, name, mib=63):
    holds = []
    for array, space, index in ins:
        if space is HBM:
            shape = array.shape
            if index is not None:
                shape = array.shape[1:] if isinstance(index, int) else index[0]
            holds.append(pltpu.VMEM(shape, array.dtype))
    for shape, kind, space in outs:
        if space is HBM:
            holds.append(pltpu.VMEM(shape, kind))
    n_in, n_out = len(ins), len(outs)

    def run(*refs):
        in_refs = []
        for ref, (_, _, index) in zip(refs, ins):
            if index is not None:
                ref = ref.at[index] if isinstance(index, int) else index[1](ref)
            in_refs.append(ref)
        out_refs = refs[n_in : n_in + n_out]
        spare = list(refs[n_in + n_out : n_in + n_out + len(holds)])
        in_sems, out_sems, *rest = refs[n_in + n_out + len(holds) :]
        in_holds = [spare.pop(0) if space is HBM else None for _, space, _ in ins]
        out_holds = [spare.pop(0) if space is HBM else None for _, _, space in outs]
        blocks = Blocks(in_refs, in_holds, out_refs, out_holds, in_sems, out_sems)
        kernel(blocks, *rest)
        for copy in blocks.leaving:
            copy.wait()

    return pl.pallas_call(
        run,
        out_shape=[jax.ShapeDtypeStruct(shape, kind) for shape, kind, _ in outs],
        in_specs=[pl.BlockSpec(memory_space=space) for _, space, _ in ins],
        out_specs=[pl.BlockSpec(memory_space=space) for _, _, space in outs],
        scratch_shapes=holds
        + [pltpu.SemaphoreType.DMA((n_in,)), pltpu.SemaphoreType.DMA((n_out,))]
        + scratch,
        compiler_params=pltpu.CompilerParams(vmem_limit_bytes=mib * 1024 * 1024),
        cost_estimate=pl.CostEstimate(flops=flops, bytes_accessed=4_000_000, transcendentals=0),
        name=name,
    )(*[array for array, _, _ in ins])


def exchange(quads, forward):
    n_lat, n_pair, n_core = (lax.axis_size(axis) for axis in ("lat", "pair", "core"))
    n_lon = n_pair * n_core
    by = -1 if forward else 1

    def moved(shard, over_lat, over_lon):
        pairs = []
        for row in range(n_lat):
            for col in range(n_lon):
                to = (row + by * over_lat) % n_lat * n_lon + (col + by * over_lon) % n_lon
                pairs.append((row * n_lon + col, to))
        return lax.ppermute(shard, ("lat", "pair", "core"), pairs)

    if forward:
        corner = moved(quads[0], 1, 1)
        row = moved(quads[1], 1, 0)
        return quads[3], moved(quads[2], 0, 1), row, corner
    return (
        moved(quads[3], 1, 1),
        moved(quads[2], 1, 0),
        moved(quads[1], 0, 1),
        quads[0],
    )


def reduce_terms(own, other, returned, after, scale):
    n_lat, n_member = lax.axis_size("lat"), lax.axis_size("member")
    n_pair, n_core = lax.axis_size("pair"), lax.axis_size("core")
    rows = D // (n_pair * n_core)
    width = D // n_lat
    partner = lax.ppermute(other, "core", [(i, (i + 1) % n_core) for i in range(n_core)])
    (terms,) = call(
        weight_terms,
        [(own, pltpu.VMEM, None), (partner, pltpu.VMEM, None)],
        [((n_member * n_pair, rows, D), bf16, HBM)],
        [pltpu.SemaphoreType.DMA((2,))],
        3_000_000_000,
        "weight_terms",
        16,
    )
    terms, *_ = lax.optimization_barrier((terms, *returned))
    parts = lax.all_to_all(terms, ("member", "pair"), 0, 0, tiled=True)
    (plane_sum,) = call(
        sum_plane,
        [(parts, pltpu.VMEM, None), (after, pl.ANY, None)],
        [((n_member * n_lat, rows, -(-width // 128) * 128), bf16, pltpu.VMEM)],
        [],
        5_000_000,
        "sum_plane",
        16,
    )
    parts = lax.all_to_all(plane_sum, ("member", "lat"), 0, 0, tiled=True)
    (total,) = call(
        functools.partial(sum_lat, scale),
        [(parts, pltpu.VMEM, None)],
        [((2, rows, width), f32, HBM)],
        [],
        1_000_000,
        "sum_lat",
        8,
    )
    return total.transpose(0, 2, 1)


def body(fields, cotangent, qkv_weight, out_weight, norm_gain, bias_table, bias_index, region):
    order, window_order, at_line, at_col = constants()
    window_order = jnp.asarray(window_order, bf16)
    back_order = jnp.asarray(order.T, bf16)
    order = jnp.asarray(order, bf16)
    at_line, at_col = jnp.asarray(at_line, bf16), jnp.asarray(at_col, bf16)
    edge = (lax.axis_index("lat") == lax.axis_size("lat") - 1).astype(jnp.int32)
    n_pair, n_core = lax.axis_size("pair"), lax.axis_size("core")
    core = lax.axis_index("core").astype(jnp.int32)

    def qkv_parts(block):
        def part_of(part):
            return (D, D), lambda ref: ref.at[block, :, pl.ds(part * D, D)]

        return [(qkv_weight, HBM, part_of(part)) for part in range(3)]

    gather_scratch = [pltpu.VMEM((HEADS, 8, CHUNKS * 128), f32), pltpu.VMEM((HEADS, DEPTH, 128), f32)]
    hold = pltpu.VMEM((WIN, D), f32)
    mixed_scratch = pltpu.VMEM((WIN, D), bf16)
    back_scratch = [
        pltpu.VMEM((WIN, D), bf16),
        pltpu.VMEM((4, D, WIN), bf16),
        pltpu.VMEM((WIN, 3 * D), bf16),
    ]
    cells = (WIN_LAT * WIN_LON, LEVELS, D)
    table = bias_table.transpose(0, 1, 3, 2).reshape(2, HEADS, NREL)
    first = call(
        first_forward,
        [
            (window_order, HBM, None),
            (bias_index, HBM, None),
            (table, HBM, 0),
            (fields.transpose(0, 2, 3, 1, 4).reshape(cells), HBM, None),
            (order, HBM, None),
            (norm_gain, HBM, None),
            *qkv_parts(0),
            (out_weight, HBM, 0),
            (cotangent.transpose(0, 2, 3, 1, 4).reshape(cells), HBM, None),
        ],
        [((QUAD, 3 * D), bf16, HBM)] * 4
        + [
            ((WIN, 256), jnp.int32, HBM),
            ((WIN, D), bf16, HBM),
            ((WIN, 3 * D), bf16, HBM),
            ((HEADS, WIN, WIN), bf16, HBM),
        ],
        [pltpu.VMEM((HEADS, WIN, WIN), f32)] + gather_scratch + [hold, mixed_scratch],
        1_000_000_000,
        "first_forward",
    )
    wide, inputs, qkv_one, probs_one = first[4:]
    shifted = exchange(first[:4], True)
    bias_two, picks = call(
        functools.partial(second_bias, D // (n_pair * n_core)),
        [
            (region.transpose(1, 0, 2), HBM, None),
            (edge.reshape(1), SMEM, None),
            (at_line, HBM, None),
            (at_col, HBM, None),
            (table, HBM, 1),
            (wide, HBM, None),
            (core.reshape(1), SMEM, None),
        ],
        [
            ((HEADS, WIN, WIN), f32, pltpu.VMEM),
            ((2, D // 2, D), bf16, pltpu.VMEM),
        ],
        gather_scratch + [pltpu.VMEM((WIN, WIN), f32)],
        5_000_000_000,
        "second_bias",
        12,
    )
    second = call(
        second_block,
        [(quad, pltpu.VMEM, None) for quad in shifted]
        + [
            (norm_gain, HBM, None),
            (qkv_weight, pltpu.VMEM, None),
            (out_weight, pltpu.VMEM, None),
            (bias_two, pltpu.VMEM, None),
            (picks, pltpu.VMEM, None),
        ],
        [((QUAD, 2 * D), bf16, HBM)] * 4 + [((WIN, 3 * D), bf16, HBM)] * 2,
        [hold, mixed_scratch, pltpu.VMEM((WIN, 3 * D), bf16), pltpu.VMEM((HEADS, WIN, WIN), bf16)]
        + back_scratch
        + [pltpu.SemaphoreType.DMA((8,))],
        15_000_000_000,
        "second_block",
        16,
    )
    returned = exchange(second[:4], False)
    grad_fields, output = call(
        first_backward,
        [(quad, HBM, None) for quad in returned]
        + [
            (inputs, HBM, None),
            (qkv_one, HBM, None),
            (probs_one, HBM, None),
            (out_weight, HBM, 0),
            (norm_gain, HBM, None),
            (back_order, HBM, None),
        ]
        + qkv_parts(0),
        [(cells, bf16, HBM)] * 2,
        [hold] + back_scratch,
        9_000_000_000,
        "first_backward",
        61,
    )

    token_total = lax.axis_size("member") * lax.axis_size("lat") * n_pair * n_core * WIN
    scale = float(token_total) ** (-0.5)
    grad_out = reduce_terms(second[4], second[5], returned, grad_fields, scale)

    def whole(values):
        grid = values.reshape(1, WIN_LAT, WIN_LON, LEVELS, D)
        return grid.transpose(0, 3, 1, 2, 4)

    return whole(output), whole(grad_fields), grad_out


def solution(mesh):
    n_member, n_lat, n_lon = mesh.devices.shape
    split = mesh.devices.reshape(n_member, n_lat, n_lon // 2, 2)
    mesh = jax.sharding.Mesh(split, ("member", "lat", "pair", "core"))
    lon = ("pair", "core")
    grid = P("member", None, "lat", lon, None)
    placed = (grid, grid, P(), P(), P(), P(None, "lat", None, None), P(), P(None, "lat", lon))
    return jax.shard_map(
        body,
        mesh=mesh,
        in_specs=placed,
        out_specs=(grid, grid, P(None, "lat", lon)),
        check_vma=False,
    )
```

```python
import functools
import math

import jax
import jax.numpy as jnp
import numpy as np
from jax import lax
from jax.experimental import pallas as pl
from jax.experimental.pallas import tpu as pltpu
from jax.sharding import PartitionSpec as P

LEVELS = 2
WIN_LAT = 6
WIN_LON = 12
HALF_LAT = WIN_LAT // 2
HALF_LON = WIN_LON // 2
WIN = LEVELS * WIN_LAT * WIN_LON
QUAD = WIN // 4
D = 768
HEADS = 24
HEAD_DIM = D // HEADS
GROUP = 128 // HEAD_DIM
GROUPS = HEADS // GROUP
NREL = 759
CHUNKS = 6
DEPTH = 24
TAIL = WIN - 128
SCALE = HEAD_DIM ** (-0.5)
EPS = 1e-05

bf16 = jnp.bfloat16
f32 = jnp.float32


def quad_order():
    token = np.arange(WIN)
    quad, inside = token // QUAD, token % QUAD
    level = inside // (HALF_LAT * HALF_LON)
    row = inside // HALF_LON % HALF_LAT + HALF_LAT * (quad // 2)
    col = inside % HALF_LON + HALF_LON * (quad % 2)
    stored = (row * WIN_LON + col) * LEVELS + level
    window = (level * WIN_LAT + row) * WIN_LON + col
    return row * LEVELS + level, col, stored, window


def constants():
    line, col, stored, window = quad_order()
    order = np.eye(WIN, dtype=np.float32)[stored]
    window_order = np.eye(WIN, dtype=np.float32)[window]
    at_line = np.eye(LEVELS * WIN_LAT, dtype=np.float32)[line]
    at_col = np.eye(WIN_LON, dtype=np.float32)[col]
    return order, window_order, at_line, at_col


def contract(left, right, dims):
    return lax.dot_general(left, right, ((dims[:1], dims[1:]), ((), ())), preferred_element_type=f32)


def mm(left, right):
    return contract(left, right, (1, 0))


def mm_t(left, right):
    return contract(left, right, (1, 1))


def eye(size):
    rows = lax.broadcasted_iota(jnp.int32, (size, size), 0)
    cols = lax.broadcasted_iota(jnp.int32, (size, size), 1)
    return (rows == cols).astype(f32).astype(bf16)


def head_masks():
    lane = lax.broadcasted_iota(jnp.int32, (1, 128), 1)
    masks = []
    for head in range(GROUP):
        inside = jnp.logical_and(lane >= head * HEAD_DIM, lane < (head + 1) * HEAD_DIM)
        masks.append(inside.astype(f32).astype(bf16))
    return masks


def layer_norm(values_f):
    centred = values_f - jnp.mean(values_f, axis=-1, keepdims=True)
    variance = jnp.mean(centred * centred, axis=-1, keepdims=True)
    inv_std = lax.rsqrt(variance + EPS)
    return centred * inv_std, inv_std


def place_index(index_ref, order, wide_ref):
    index_f = index_ref[...].astype(f32)
    high = jnp.floor(index_f * 0.125)
    low = index_f - high * 8.0
    parts = []
    for part in (high, low):
        half = mm(order, part.astype(bf16)).astype(bf16)
        parts.append(mm_t(half, order))
    moved = parts[0] * 8.0 + parts[1]
    wide_ref[:, :WIN] = (moved + 0.5).astype(jnp.int32)
    wide_ref[:, WIN:] = jnp.zeros((WIN, 256 - WIN), jnp.int32)
    lane = lax.broadcasted_iota(jnp.int32, (DEPTH, 128), 1)
    packed = jnp.zeros((DEPTH, 128), jnp.int32)
    for strip in range(WIN // DEPTH):
        piece = wide_ref[strip * DEPTH : (strip + 1) * DEPTH, 128:256]
        if strip:
            piece = pltpu.roll(piece, strip * TAIL, axis=1)
        inside = jnp.logical_and(lane >= strip * TAIL, lane < (strip + 1) * TAIL)
        packed = jnp.where(inside, piece, packed)
    wide_ref[:DEPTH, 128:256] = packed


def lane_gather(row, index):
    numbers = lax.GatherDimensionNumbers(
        offset_dims=(),
        collapsed_slice_dims=(1,),
        start_index_map=(1,),
        operand_batching_dims=(0,),
        start_indices_batching_dims=(0,),
    )
    mode = lax.GatherScatterMode.PROMISE_IN_BOUNDS
    return lax.gather(row, index[..., None], numbers, slice_sizes=(1, 1), mode=mode)


def gather_bias(wide_ref, table_ref, bias_ref, rows_ref, tail_ref, mask_ref, done=None):
    for head in range(HEADS):
        rows_ref[head, :, :NREL] = jnp.broadcast_to(table_ref[head : head + 1, :], (8, NREL))

    def look_up(index, store):
        low_part = jnp.bitwise_and(index, 127)
        high_part = jnp.right_shift(index, 7)
        for head in range(HEADS):
            found = jnp.zeros((8, 128), f32)
            for chunk in range(CHUNKS):
                row = rows_ref[head, :, chunk * 128 : (chunk + 1) * 128]
                found = jnp.where(high_part == chunk, lane_gather(row, low_part), found)
            store(head, found)

    def main_strip(strip, carry):
        lines = pl.ds(pl.multiple_of(strip * 8, 8), 8)
        mask = None if mask_ref is None else mask_ref[lines, :128]

        def store(head, found):
            bias_ref[head, lines, :128] = found if mask is None else found + mask

        look_up(wide_ref[lines, :128], store)
        return carry

    def tail_strip(strip, carry):
        lines = pl.ds(pl.multiple_of(strip * 8, 8), 8)

        def store(head, found):
            tail_ref[head, lines, :] = found

        look_up(wide_ref[lines, 128:256], store)
        return carry

    def unpack(head, carry):
        rest = tail_ref[head]
        for strip in range(WIN // DEPTH):
            lines = slice(strip * DEPTH, (strip + 1) * DEPTH)
            piece = rest if strip == 0 else pltpu.roll(rest, 128 - strip * TAIL, axis=1)
            piece = piece[:, :TAIL]
            if mask_ref is not None:
                piece = piece + mask_ref[lines, 128:WIN]
            bias_ref[head, lines, 128:WIN] = piece
        return carry

    lax.fori_loop(0, DEPTH // 8, tail_strip, 0, unroll=3)
    lax.fori_loop(0, HEADS, unpack, 0, unroll=4)
    for third in range(3):
        lax.fori_loop(third * 6, third * 6 + 6, main_strip, 0, unroll=6)
        if done is not None:
            done(third)


def project_qkv(hidden, w_parts, qkv_ref):
    for part in range(3):
        qkv_ref[:, part * D : (part + 1) * D] = mm(hidden, w_parts(part)[...]).astype(bf16)


def stack_heads(values, masks):
    return jnp.concatenate([values * mask for mask in masks], axis=0)


def merge_heads(stacked):
    lane = lax.broadcasted_iota(jnp.int32, (1, 128), 1)
    merged = stacked[:WIN]
    for head in range(1, GROUP):
        later = lane >= head * HEAD_DIM
        merged = jnp.where(later, stacked[head * WIN : (head + 1) * WIN], merged)
    return merged


def group_cols(group, part):
    return slice(part * D + group * 128, part * D + (group + 1) * 128)


def attend(qkv_ref, bias_ref, probs_ref, mixed_ref, beside=None):
    masks = head_masks()
    ones = jnp.ones((WIN, 128), bf16)
    for group in range(GROUPS):
        heads = slice(group * GROUP, (group + 1) * GROUP)
        query = qkv_ref[:, group_cols(group, 0)]
        key = qkv_ref[:, group_cols(group, 1)]
        value = qkv_ref[:, group_cols(group, 2)]
        scores = mm_t(stack_heads(query, masks), key) * SCALE
        scores = scores + bias_ref[heads].reshape(GROUP * WIN, WIN)
        exponent = jnp.exp(scores - jnp.max(scores, axis=-1, keepdims=True)).astype(bf16)
        product = mm(exponent, jnp.concatenate([value, ones], axis=1))
        share = 1.0 / product[:, 128:]
        weights = exponent.astype(f32) * jnp.concatenate([share, share[:, : WIN - 128]], axis=1)
        probs_ref[heads] = weights.astype(bf16).reshape(GROUP, WIN, WIN)
        mixed = merge_heads(product[:, :128] * share)
        mixed_ref[:, group_cols(group, 0)] = mixed.astype(bf16)
        if beside is not None:
            beside(group)


def prepare_back(part, grad, qkv_ref, w_out_ref, grad_mixed_ref, turned_ref):
    unit = eye(256)
    cols = slice(part * 256, (part + 1) * 256)
    grad_mixed_ref[:, cols] = mm_t(grad, w_out_ref[cols, :]).astype(bf16)
    turned_ref[0, cols, :] = mm_t(unit, grad_mixed_ref[:, cols]).astype(bf16)
    turned_ref[1, cols, :] = mm_t(unit, qkv_ref[:, cols]).astype(bf16)


def back_attend(qkv_ref, probs_ref, mixed_ref, grad_mixed_ref, turned_ref, rows_ref, beside=None):
    masks = head_masks()
    small = eye(WIN)
    minus = -jnp.ones((WIN, 128), bf16)
    for group in range(GROUPS):
        heads = slice(group * GROUP, (group + 1) * GROUP)
        cols = group_cols(group, 0)
        grad_mixed = grad_mixed_ref[:, cols]
        key = qkv_ref[:, group_cols(group, 1)]
        value = qkv_ref[:, group_cols(group, 2)]
        weights = probs_ref[heads].reshape(GROUP * WIN, WIN)
        probs = weights.astype(f32)
        left = stack_heads(grad_mixed, masks)
        if mixed_ref is None:
            grad_weights = mm_t(left, value)
            moved = grad_weights - jnp.sum(grad_weights * probs, axis=-1, keepdims=True)
        else:
            inner = grad_mixed.astype(f32) * mixed_ref[:, cols].astype(f32)
            left = jnp.concatenate([left, stack_heads(inner.astype(bf16), masks)], axis=1)
            moved = mm_t(left, jnp.concatenate([value, minus], axis=1))
        grad_scores = (probs * moved * SCALE).astype(bf16)
        rows_ref[:, cols] = merge_heads(mm(grad_scores, key)).astype(bf16)
        for inner in range(GROUP):
            head = group * GROUP + inner
            lines = slice(head * HEAD_DIM, (head + 1) * HEAD_DIM)
            tokens = slice(inner * WIN, (inner + 1) * WIN)
            turned_ref[2, lines, :] = mm(turned_ref[1, lines, :], grad_scores[tokens]).astype(bf16)
            turned_ref[3, lines, :] = mm(turned_ref[0, lines, :], weights[tokens]).astype(bf16)
        if beside is not None:
            beside(group)
    for part in range(3):
        cols = slice(part * 256, (part + 1) * 256)
        for which in (1, 2):
            out = slice(which * D + part * 256, which * D + (part + 1) * 256)
            rows_ref[:, out] = mm_t(small, turned_ref[1 + which, cols, :]).astype(bf16)


def back_norm(grad_f, normed, inv_std, gain, rows_ref, w_parts):
    grad_hidden = jnp.zeros((WIN, D), f32)
    for part in range(3):
        grad_hidden += mm_t(rows_ref[:, part * D : (part + 1) * D], w_parts(part)[...])
    grad_normed = grad_hidden * gain
    mean_one = jnp.mean(grad_normed, axis=-1, keepdims=True)
    mean_two = jnp.mean(grad_normed * normed, axis=-1, keepdims=True)
    return grad_f + inv_std * (grad_normed - mean_one - normed * mean_two)


def put_quads(values_f, hold_ref, quad_refs, section):
    hold_ref[...] = values_f
    cols = slice(section * D, (section + 1) * D)
    for quad in range(4):
        quad_refs[quad][:, cols] = hold_ref[quad * QUAD : (quad + 1) * QUAD, :].astype(bf16)


def take_quads(quad_refs, hold_ref, section):
    cols = slice(section * D, (section + 1) * D)
    for quad in range(4):
        hold_ref[quad * QUAD : (quad + 1) * QUAD, :] = quad_refs[quad][:, cols].astype(f32)
    return hold_ref[...]


def first_forward(
    blocks, bias_ref, rows_ref, tail_ref, hold_ref, mixed_ref,
):
    quads = blocks.outs[:4]
    wide_ref, input_ref, qkv_ref, probs_ref = blocks.outs[4:]
    place_index(blocks.get(1), blocks.get(0)[...], wide_ref)
    blocks.put(4)
    order = blocks.get(4)[...]
    values_f = mm(order, blocks.get(3)[...].reshape(WIN, D))
    input_ref[...] = values_f.astype(bf16)
    blocks.put(5)
    normed, _ = layer_norm(values_f)
    hidden = (normed * blocks.get(5)[0:1, :]).astype(bf16)

    def project(third):
        cols = slice(third * D, (third + 1) * D)
        qkv_ref[:, cols] = mm(hidden, blocks.get(6 + third)[...]).astype(bf16)

    gather_bias(wide_ref, blocks.get(2), bias_ref, rows_ref, tail_ref, None, project)
    blocks.put(6)
    attend(qkv_ref, bias_ref, probs_ref, mixed_ref)
    blocks.put(7)
    put_quads(mm(order, blocks.get(10)[...].reshape(WIN, D)), hold_ref, quads, 1)
    mixed = mixed_ref[...]
    put_quads(mixed.astype(f32), hold_ref, quads, 2)
    result = input_ref[...].astype(f32) + mm(mixed, blocks.get(9)[...])
    put_quads(result, hold_ref, quads, 0)
    for quad in range(4):
        blocks.put(quad)


def pick_columns(core, width):
    rows = lax.broadcasted_iota(jnp.int32, (D // 2, D), 0)
    cols = lax.broadcasted_iota(jnp.int32, (D // 2, D), 1)
    part = jnp.floor((rows.astype(f32) + 0.5) * (1.0 / width)).astype(jnp.int32)
    return (cols == rows + width * (part + core)).astype(f32).astype(bf16)


def second_bias(width, blocks, rows_ref, tail_ref, mask_ref):
    region_ref, edge_ref, bias_ref = blocks.get(0), blocks.get(1), blocks.outs[0]
    labels = jnp.concatenate([region_ref[row] for row in range(WIN_LAT)], axis=0)
    labels = labels.astype(f32) * 2.0 - 1.0
    at_line, at_col = blocks.get(2)[...], blocks.get(3)[...]
    column = jnp.sum(mm(at_line, labels.astype(bf16)) * at_col.astype(f32), axis=1, keepdims=True)
    signs = jnp.broadcast_to(column, (WIN, 128)).astype(bf16)
    same = mm_t(signs, signs) > 0.0
    half = WIN // 2
    rows = lax.broadcasted_iota(jnp.int32, (WIN, WIN), 0) >= half
    cols = lax.broadcasted_iota(jnp.int32, (WIN, WIN), 1) >= half
    across = jnp.logical_and(jnp.logical_xor(rows, cols), edge_ref[0] != 0)
    allowed = jnp.logical_and(same, jnp.logical_not(across))
    mask_ref[...] = jnp.where(allowed, 0.0, -jnp.inf)

    core = blocks.get(6)[0]
    blocks.outs[1][0] = pick_columns(core, width)
    blocks.outs[1][1] = pick_columns(1 - core, width)
    gather_bias(blocks.get(5), blocks.get(4), bias_ref, rows_ref, tail_ref, mask_ref)


def second_block(
    blocks, hold_ref, mixed_ref, qkv_ref, probs_ref, grad_mixed_ref, turned_ref, grad_rows_ref,
    sems,
):
    leaving = blocks.outs[:4]
    own_ref, other_ref = blocks.outs[4:]
    arrived = [blocks.get(quad) for quad in range(4)]
    values_f = take_quads(arrived, hold_ref, 0)
    normed, inv_std = layer_norm(values_f)
    gain = blocks.get(4)[1:2, :]
    hidden = (normed * gain).astype(bf16)

    def w_parts(part):
        return blocks.get(5).at[1, :, pl.ds(part * D, D)]

    project_qkv(hidden, w_parts, qkv_ref)
    grad_f = take_quads(arrived, hold_ref, 1)
    grad = grad_f.astype(bf16)
    first_mixed = take_quads(arrived, hold_ref, 2).astype(bf16)
    half = D // 2
    bias_ref, w_out_ref, picks_ref = blocks.get(7), blocks.get(6).at[1], blocks.get(8)

    def beside_forward(group):
        if group < 3:
            prepare_back(group, grad, qkv_ref, w_out_ref, grad_mixed_ref, turned_ref)
        elif group < 5:
            ref = (own_ref, other_ref)[group - 3]
            ref[:, :D] = first_mixed
            ref[:, 2 * D + half :] = mm_t(grad, picks_ref[group - 3]).astype(bf16)

    attend(qkv_ref, bias_ref, probs_ref, mixed_ref, beside_forward)
    early = ((0, 2 * D), (2 * D + half, half))
    for place, ref in ((4, own_ref), (5, other_ref)):
        ref[:, D : 2 * D] = mixed_ref[...]
        for part, (start, size) in enumerate(early):
            blocks.put(place, (slice(None), pl.ds(start, size)), sems.at[2 * place - 4 + part])

    def beside_back(group):
        if group < 3:
            cols = slice(group * 256, (group + 1) * 256)
            hold_ref[:, cols] = values_f[:, cols] + mm(mixed_ref[...], w_out_ref[:, cols])
        elif group == 3:
            for quad in range(4):
                rows = slice(quad * QUAD, (quad + 1) * QUAD)
                leaving[quad][:, D:] = hold_ref[rows, :].astype(bf16)
                blocks.put(quad, (slice(None), pl.ds(D, D)), sems.at[quad])

    back_attend(
        qkv_ref, probs_ref, mixed_ref, grad_mixed_ref, turned_ref, grad_rows_ref, beside_back
    )
    grad_input = back_norm(grad_f, normed, inv_std, gain, grad_rows_ref, w_parts)
    first_grad = grad_input.astype(bf16)
    other_ref[:, 2 * D : 2 * D + half] = mm_t(first_grad, picks_ref[1]).astype(bf16)
    late = (slice(None), pl.ds(2 * D, half))
    blocks.put(5, late)
    put_quads(grad_input, hold_ref, leaving, 0)
    for quad in range(4):
        blocks.put(quad, (slice(None), pl.ds(0, D)))
    own_ref[:, 2 * D : 2 * D + half] = mm_t(first_grad, picks_ref[0]).astype(bf16)
    blocks.put(4, late)


def weight_terms(blocks, sems):
    terms_ref = blocks.outs[0]
    n_parts, rows, _ = terms_ref.shape
    n_parts //= 2
    half = n_parts * rows
    unit = eye(128)
    packs = (blocks.get(0), blocks.get(1))
    for block in range(2):
        cols = slice(2 * D + block * half, 2 * D + (block + 1) * half)
        total = jnp.zeros((half, D), f32)
        for pack in packs:
            turned = [
                mm_t(unit, pack[:, start : start + 128]).astype(bf16)
                for start in range(cols.start, cols.stop, 128)
            ]
            turned = jnp.concatenate(turned, axis=0)
            total += mm(turned, pack[:, block * D : (block + 1) * D])
        for part in range(n_parts):
            piece = total[part * rows : (part + 1) * rows, :].astype(bf16)
            terms_ref[block * n_parts + part] = piece
        blocks.put(0, pl.ds(block * n_parts, n_parts), sems.at[block])


def fold(width):
    return 128 // math.gcd(width, 128)


def sum_plane(blocks):
    parts_ref, out_ref = blocks.get(0), blocks.outs[0]
    total = parts_ref[0].astype(f32)
    for part in range(1, parts_ref.shape[0]):
        total += parts_ref[part].astype(f32)
    copies = 2
    places = out_ref.shape[0] // copies
    width = D // places
    for place in range(places):
        piece = total[:, place * width : (place + 1) * width]
        folds = fold(width)
        lines = total.shape[0] // folds
        flat = [piece[line * lines : (line + 1) * lines] for line in range(folds)]
        flat = jnp.concatenate(flat, axis=1)
        tiles = [flat[:, start : start + 128] for start in range(0, folds * width, 128)]
        piece = jnp.concatenate(tiles, axis=0).astype(bf16)
        for copy in range(copies):
            out_ref[copy * places + place] = piece


def sum_lat(scale, blocks):
    parts_ref, out_ref = blocks.get(0), blocks.outs[0]
    width = out_ref.shape[2]
    count = parts_ref.shape[0] // 2
    for block in range(2):
        total = parts_ref[block * count].astype(f32)
        for part in range(1, count):
            total += parts_ref[block * count + part].astype(f32)
        folds = fold(width)
        lines = out_ref.shape[1] // folds
        flat = [total[start : start + lines] for start in range(0, total.shape[0], lines)]
        flat = jnp.concatenate(flat, axis=1) * scale
        pieces = [flat[:, line * width : (line + 1) * width] for line in range(folds)]
        out_ref[block] = jnp.concatenate(pieces, axis=0)
    blocks.put(0)


def first_backward(blocks, hold_ref, grad_mixed_ref, turned_ref, grad_rows_ref):
    grad_fields_ref, output_ref = blocks.outs
    normed, inv_std = layer_norm(blocks.get(4)[...].astype(f32))
    arrived = [blocks.get(quad) for quad in range(4)]
    grad_f = take_quads(arrived, hold_ref, 0)
    qkv_ref, probs_ref, w_out_ref = blocks.get(5), blocks.get(6), blocks.get(7)
    for part in range(3):
        prepare_back(part, grad_f.astype(bf16), qkv_ref, w_out_ref, grad_mixed_ref, turned_ref)
    back_attend(qkv_ref, probs_ref, None, grad_mixed_ref, turned_ref, grad_rows_ref)
    gain = blocks.get(8)[0:1, :]
    grad_input = back_norm(
        grad_f, normed, inv_std, gain, grad_rows_ref, lambda part: blocks.get(10 + part)
    )
    back_order = blocks.get(9)[...]
    shape = grad_fields_ref.shape
    grad_input = mm(back_order, grad_input.astype(bf16))
    grad_fields_ref[...] = grad_input.astype(bf16).reshape(shape)
    blocks.put(0)
    result = mm(back_order, take_quads(arrived, hold_ref, 1).astype(bf16))
    output_ref[...] = result.astype(bf16).reshape(shape)
    blocks.put(1)


class Blocks:
    def __init__(self, in_refs, in_holds, out_refs, out_holds, in_sems, out_sems):
        self.ins, self.outs, self.waiting, self.leaving = [], [], {}, []
        self.out_refs, self.out_sems = out_refs, out_sems
        for place, (ref, hold) in enumerate(zip(in_refs, in_holds)):
            if hold is not None:
                copy = pltpu.make_async_copy(ref, hold, in_sems.at[place])
                copy.start()
                self.waiting[place] = copy
            self.ins.append(ref if hold is None else hold)
        for ref, hold in zip(out_refs, out_holds):
            self.outs.append(ref if hold is None else hold)

    def get(self, place):
        if place in self.waiting:
            self.waiting.pop(place).wait()
        return self.ins[place]

    def put(self, place, part=None, sem=None):
        source, target = self.outs[place], self.out_refs[place]
        if part is not None:
            source, target = source.at[part], target.at[part]
        sem = self.out_sems.at[place] if sem is None else sem
        copy = pltpu.make_async_copy(source, target, sem)
        copy.start()
        self.leaving.append(copy)


HBM, SMEM = pltpu.HBM, pltpu.SMEM


def call(kernel, ins, outs, scratch, flops, name, mib=63):
    holds = []
    for array, space, index in ins:
        if space is HBM:
            shape = array.shape
            if index is not None:
                shape = array.shape[1:] if isinstance(index, int) else index[0]
            holds.append(pltpu.VMEM(shape, array.dtype))
    for shape, kind, space in outs:
        if space is HBM:
            holds.append(pltpu.VMEM(shape, kind))
    n_in, n_out = len(ins), len(outs)

    def run(*refs):
        in_refs = []
        for ref, (_, _, index) in zip(refs, ins):
            if index is not None:
                ref = ref.at[index] if isinstance(index, int) else index[1](ref)
            in_refs.append(ref)
        out_refs = refs[n_in : n_in + n_out]
        spare = list(refs[n_in + n_out : n_in + n_out + len(holds)])
        in_sems, out_sems, *rest = refs[n_in + n_out + len(holds) :]
        in_holds = [spare.pop(0) if space is HBM else None for _, space, _ in ins]
        out_holds = [spare.pop(0) if space is HBM else None for _, _, space in outs]
        blocks = Blocks(in_refs, in_holds, out_refs, out_holds, in_sems, out_sems)
        kernel(blocks, *rest)
        for copy in blocks.leaving:
            copy.wait()

    return pl.pallas_call(
        run,
        out_shape=[jax.ShapeDtypeStruct(shape, kind) for shape, kind, _ in outs],
        in_specs=[pl.BlockSpec(memory_space=space) for _, space, _ in ins],
        out_specs=[pl.BlockSpec(memory_space=space) for _, _, space in outs],
        scratch_shapes=holds
        + [pltpu.SemaphoreType.DMA((n_in,)), pltpu.SemaphoreType.DMA((n_out,))]
        + scratch,
        compiler_params=pltpu.CompilerParams(vmem_limit_bytes=mib * 1024 * 1024),
        cost_estimate=pl.CostEstimate(flops=flops, bytes_accessed=4_000_000, transcendentals=0),
        name=name,
    )(*[array for array, _, _ in ins])


def exchange(quads, forward):
    n_lat, n_pair, n_core = (lax.axis_size(axis) for axis in ("lat", "pair", "core"))
    n_lon = n_pair * n_core
    by = -1 if forward else 1

    def moved(shard, over_lat, over_lon):
        pairs = []
        for row in range(n_lat):
            for col in range(n_lon):
                to = (row + by * over_lat) % n_lat * n_lon + (col + by * over_lon) % n_lon
                pairs.append((row * n_lon + col, to))
        return lax.ppermute(shard, ("lat", "pair", "core"), pairs)

    if forward:
        corner = moved(quads[0], 1, 1)
        row = moved(quads[1], 1, 0)
        return quads[3], moved(quads[2], 0, 1), row, corner
    return (
        moved(quads[3], 1, 1),
        moved(quads[2], 1, 0),
        moved(quads[1], 0, 1),
        quads[0],
    )


def reduce_terms(own, other, returned, after, scale):
    n_lat, n_member = lax.axis_size("lat"), lax.axis_size("member")
    n_pair, n_core = lax.axis_size("pair"), lax.axis_size("core")
    rows = D // (n_pair * n_core)
    width = D // n_lat
    partner = lax.ppermute(other, "core", [(i, (i + 1) % n_core) for i in range(n_core)])
    (terms,) = call(
        weight_terms,
        [(own, pltpu.VMEM, None), (partner, pltpu.VMEM, None)],
        [((n_member * n_pair, rows, D), bf16, HBM)],
        [pltpu.SemaphoreType.DMA((2,))],
        3_000_000_000,
        "weight_terms",
        16,
    )
    terms, *_ = lax.optimization_barrier((terms, *returned))
    parts = lax.all_to_all(terms, ("member", "pair"), 0, 0, tiled=True)
    (plane_sum,) = call(
        sum_plane,
        [(parts, pltpu.VMEM, None), (after, pl.ANY, None)],
        [((n_member * n_lat, rows * width // 128, 128), bf16, pltpu.VMEM)],
        [],
        5_000_000,
        "sum_plane",
        16,
    )
    parts = lax.all_to_all(plane_sum, ("member", "lat"), 0, 0, tiled=True)
    (total,) = call(
        functools.partial(sum_lat, scale),
        [(parts, pltpu.VMEM, None)],
        [((2, rows, width), f32, HBM)],
        [],
        1_000_000,
        "sum_lat",
        8,
    )
    return total.transpose(0, 2, 1)


def body(fields, cotangent, qkv_weight, out_weight, norm_gain, bias_table, bias_index, region):
    order, window_order, at_line, at_col = constants()
    window_order = jnp.asarray(window_order, bf16)
    back_order = jnp.asarray(order.T, bf16)
    order = jnp.asarray(order, bf16)
    at_line, at_col = jnp.asarray(at_line, bf16), jnp.asarray(at_col, bf16)
    edge = (lax.axis_index("lat") == lax.axis_size("lat") - 1).astype(jnp.int32)
    n_pair, n_core = lax.axis_size("pair"), lax.axis_size("core")
    core = lax.axis_index("core").astype(jnp.int32)

    def qkv_parts(block):
        def part_of(part):
            return (D, D), lambda ref: ref.at[block, :, pl.ds(part * D, D)]

        return [(qkv_weight, HBM, part_of(part)) for part in range(3)]

    gather_scratch = [pltpu.VMEM((HEADS, 8, CHUNKS * 128), f32), pltpu.VMEM((HEADS, DEPTH, 128), f32)]
    hold = pltpu.VMEM((WIN, D), f32)
    mixed_scratch = pltpu.VMEM((WIN, D), bf16)
    back_scratch = [
        pltpu.VMEM((WIN, D), bf16),
        pltpu.VMEM((4, D, WIN), bf16),
        pltpu.VMEM((WIN, 3 * D), bf16),
    ]
    cells = (WIN_LAT * WIN_LON, LEVELS, D)
    table = bias_table.transpose(0, 1, 3, 2).reshape(2, HEADS, NREL)
    first = call(
        first_forward,
        [
            (window_order, HBM, None),
            (bias_index, HBM, None),
            (table, HBM, 0),
            (fields.transpose(0, 2, 3, 1, 4).reshape(cells), HBM, None),
            (order, HBM, None),
            (norm_gain, HBM, None),
            *qkv_parts(0),
            (out_weight, HBM, 0),
            (cotangent.transpose(0, 2, 3, 1, 4).reshape(cells), HBM, None),
        ],
        [((QUAD, 3 * D), bf16, HBM)] * 4
        + [
            ((WIN, 256), jnp.int32, HBM),
            ((WIN, D), bf16, HBM),
            ((WIN, 3 * D), bf16, HBM),
            ((HEADS, WIN, WIN), bf16, HBM),
        ],
        [pltpu.VMEM((HEADS, WIN, WIN), f32)] + gather_scratch + [hold, mixed_scratch],
        1_000_000_000,
        "first_forward",
    )
    wide, inputs, qkv_one, probs_one = first[4:]
    shifted = exchange(first[:4], True)
    bias_two, picks = call(
        functools.partial(second_bias, D // (n_pair * n_core)),
        [
            (region.transpose(1, 0, 2), HBM, None),
            (edge.reshape(1), SMEM, None),
            (at_line, HBM, None),
            (at_col, HBM, None),
            (table, HBM, 1),
            (wide, HBM, None),
            (core.reshape(1), SMEM, None),
        ],
        [
            ((HEADS, WIN, WIN), f32, pltpu.VMEM),
            ((2, D // 2, D), bf16, pltpu.VMEM),
        ],
        gather_scratch + [pltpu.VMEM((WIN, WIN), f32)],
        5_000_000_000,
        "second_bias",
        12,
    )
    second = call(
        second_block,
        [(quad, pltpu.VMEM, None) for quad in shifted]
        + [
            (norm_gain, HBM, None),
            (qkv_weight, pltpu.VMEM, None),
            (out_weight, pltpu.VMEM, None),
            (bias_two, pltpu.VMEM, None),
            (picks, pltpu.VMEM, None),
        ],
        [((QUAD, 2 * D), bf16, HBM)] * 4 + [((WIN, 3 * D), bf16, HBM)] * 2,
        [hold, mixed_scratch, pltpu.VMEM((WIN, 3 * D), bf16), pltpu.VMEM((HEADS, WIN, WIN), bf16)]
        + back_scratch
        + [pltpu.SemaphoreType.DMA((8,))],
        15_000_000_000,
        "second_block",
        16,
    )
    returned = exchange(second[:4], False)
    grad_fields, output = call(
        first_backward,
        [(quad, HBM, None) for quad in returned]
        + [
            (inputs, HBM, None),
            (qkv_one, HBM, None),
            (probs_one, HBM, None),
            (out_weight, HBM, 0),
            (norm_gain, HBM, None),
            (back_order, HBM, None),
        ]
        + qkv_parts(0),
        [(cells, bf16, HBM)] * 2,
        [hold] + back_scratch,
        9_000_000_000,
        "first_backward",
        61,
    )

    token_total = lax.axis_size("member") * lax.axis_size("lat") * n_pair * n_core * WIN
    scale = float(token_total) ** (-0.5)
    grad_out = reduce_terms(second[4], second[5], returned, grad_fields, scale)

    def whole(values):
        grid = values.reshape(1, WIN_LAT, WIN_LON, LEVELS, D)
        return grid.transpose(0, 3, 1, 2, 4)

    return whole(output), whole(grad_fields), grad_out


def solution(mesh):
    n_member, n_lat, n_lon = mesh.devices.shape
    split = mesh.devices.reshape(n_member, n_lat, n_lon // 2, 2)
    mesh = jax.sharding.Mesh(split, ("member", "lat", "pair", "core"))
    lon = ("pair", "core")
    grid = P("member", None, "lat", lon, None)
    placed = (grid, grid, P(), P(), P(), P(None, "lat", None, None), P(), P(None, "lat", lon))
    return jax.shard_map(
        body,
        mesh=mesh,
        in_specs=placed,
        out_specs=(grid, grid, P(None, "lat", lon)),
        check_vma=False,
    )
```
